256 devices in a mesh: ctx: 16 (over z, x_lo), dp: 16 (over x_hi, y, core).
Axes of the slice: x: 4 (x_hi: 2, x_lo: 2; x = x_hi * 2 + x_lo), y: 4, z: 8, core: 2. Of those that a mesh axis runs over, the one named last changes fastest.
Arguments:
- q_hist: bfloat16 [16, 3072, 512], P('dp', 'ctx'), may hold values from -6 to 6
- k_hist: bfloat16 [16, 3072, 512], P('dp', 'ctx'), may hold values from -6 to 6
- v_hist: bfloat16 [16, 3072, 512], P('dp', 'ctx'), may hold values from -6 to 6
- u_hist: bfloat16 [16, 3072, 512], P('dp', 'ctx'), may hold values from -6 to 6
- cand_q: bfloat16 [16, 1024, 512], P('dp', 'ctx'), may hold values from -6 to 6
- cand_u: bfloat16 [16, 1024, 512], P('dp', 'ctx'), may hold values from -6 to 6
- lengths: int32 [16, 4], P('dp'), may hold values from 1 to 1536, 3072 in all within a row
- cand_user: int32 [16, 1024], P('dp', 'ctx'), may hold values from 0 to 3
- w_out: bfloat16 [512, 1024], replicated, may hold values from -0.25 to 0.25
- grad_hist: bfloat16 [16, 3072, 1024], P('dp', 'ctx'), may hold values from -6 to 6
- grad_cand: bfloat16 [16, 1024, 1024], P('dp', 'ctx'), may hold values from -6 to 6
Outputs:
- y_hist: bfloat16 [16, 3072, 1024], P('dp', 'ctx')
- y_cand: bfloat16 [16, 1024, 1024], P('dp', 'ctx')
- grad_q: bfloat16 [16, 3072, 512], P('dp', 'ctx')
- grad_k: bfloat16 [16, 3072, 512], P('dp', 'ctx')
- grad_v: bfloat16 [16, 3072, 512], P('dp', 'ctx')
- grad_u: bfloat16 [16, 3072, 512], P('dp', 'ctx')
- grad_cand_q: bfloat16 [16, 1024, 512], P('dp', 'ctx')
- grad_cand_u: bfloat16 [16, 1024, 512], P('dp', 'ctx')
- grad_w_out: bfloat16 [512, 1024], replicated
The draws below stay inside these ranges and needn't reach their ends.
Inputs may be any that keep to these rules, and one draw needn't show every extreme that they name: Row b lists the history lengths of the 4 users packed one after another in batch b; they sum to 3072. `cand_user`: the user of the candidate's own batch whose history the candidate attends to.
All inputs are finite; a program needn't handle non-finite values.
Results may differ from the reference program's by a relative error of at most 0.014.
Values may be sent and summed in bfloat16 or wider, within the bound.
A program may use at most 64 MiB of HBM per device.

```python
import math
import jax
import jax.numpy as jnp
import numpy as np
from jax import lax

D = 1024
HEADS = 4
HEAD_DIM = 128
USERS = 4
TOK_DEV = 192
CAND_DEV = 64
HD = 512
CONTEXT = 3072
NC = 1024
MOST = 1536
BATCHES = 16
ROWS_ALL = 65536


def plant(result, rng, least, top_value):
    spot = [jax.random.randint(jax.random.fold_in(rng, axis), (), 0, length) for axis, length in enumerate(result.shape)]
    longest = result.shape.index(max(result.shape))
    neighbour = spot[:longest] + [(spot[longest] + 1) % result.shape[longest]] + spot[longest + 1:]
    return result.at[tuple(spot)].set(least).at[tuple(neighbour)].set(top_value)


def block_levels(own_key, shape, split, smallest, top_value):
    def one(position, parts):
        heights = jax.random.uniform(jax.random.fold_in(jax.random.fold_in(own_key, 6), position), (parts,), jnp.float32, smallest / len(split), top_value / len(split))
        return jnp.repeat(jnp.exp(heights), shape[position] // parts).reshape((-1,) + (1,) * (len(shape) - position - 1))

    factor_of = one(*split[0])
    for cut in split[1:]:
        factor_of = factor_of * one(*cut)
    return factor_of


def split_up(amount, total, most, lean):
    weights = [(1 << 20) // math.isqrt(grade ** lean) + 1 for grade in range(2, amount + 1)]
    rest, counts = total - most - (amount - 1), [1] * (amount - 1)
    while rest > 0:
        candidates = [i for i in range(amount - 1) if counts[i] < most]
        whole, budget = sum([weights[i] for i in candidates]), rest
        for i in candidates:
            more = min(most - counts[i], max(1, budget * weights[i] // whole), rest)
            counts[i] = counts[i] + more
            rest = rest - more
    return np.array([most] + counts)


def uneven(key, number_of, total, reach, lean):
    if number_of == 2:
        one = jax.random.randint(key, (), max(1, total - reach), min(reach, total - 1) + 1)
        return jnp.stack([one, total - one])
    tallies = jnp.asarray(split_up(number_of, total, reach, lean), jnp.int32)
    pairs = (number_of - 1) // 2
    source_of, sink = tallies[1:1 + 2 * pairs:2], tallies[2:2 + 2 * pairs:2]
    margin = jnp.minimum(source_of - 1, reach - sink)
    moved = jax.random.randint(jax.random.fold_in(key, 1), (pairs,), 0, 1 << 20) % (margin + 1)
    tallies = tallies.at[1:1 + 2 * pairs:2].set(source_of - moved).at[2:2 + 2 * pairs:2].set(sink + moved)
    return tallies[jax.random.permutation(jax.random.fold_in(key, 2), number_of)]


def bell_draw(stream_key, dims, spread, most, pieces=(), held_as=jnp.bfloat16):
    values = spread * jax.random.normal(stream_key, dims, jnp.float32)
    if pieces:
        values = values * block_levels(stream_key, dims, pieces, -0.22, 0.18)
    return jnp.clip(values, -most, most).astype(held_as)


def setup_inputs(seed: int = 0) -> dict:
    streams_of = jax.random.split(jax.random.key(seed), 12)
    return {
        "q_hist": bell_draw(streams_of[0], (BATCHES, CONTEXT, HD), 1.0, 6.0, ((0, 16), (1, 16))),
        "k_hist": bell_draw(streams_of[1], (BATCHES, CONTEXT, HD), 1.0, 6.0, ((0, 16), (1, 16))),
        "v_hist": bell_draw(streams_of[2], (BATCHES, CONTEXT, HD), 1.0, 6.0, ((0, 16), (1, 16))),
        "u_hist": bell_draw(streams_of[3], (BATCHES, CONTEXT, HD), 1.0, 6.0, ((0, 16), (1, 16))),
        "cand_q": bell_draw(streams_of[4], (BATCHES, NC, HD), 1.0, 6.0, ((0, 16), (1, 16))),
        "cand_u": bell_draw(streams_of[5], (BATCHES, NC, HD), 1.0, 6.0, ((0, 16), (1, 16))),
        "lengths": jax.vmap(lambda own: uneven(own, USERS, CONTEXT, MOST, 2))(jax.random.split(streams_of[6], BATCHES)).reshape((BATCHES, USERS)).astype(jnp.int32),
        "cand_user": plant(jax.random.randint(streams_of[7], (BATCHES, NC), 0, USERS), jax.random.fold_in(streams_of[7], 1), 0, USERS - 1).astype(jnp.int32),
        "w_out": bell_draw(streams_of[8], (HD, D), HD ** -0.5, 0.25),
        "grad_hist": bell_draw(streams_of[9], (BATCHES, CONTEXT, D), 1.0, 6.0, ((0, 16), (1, 16))),
        "grad_cand": bell_draw(streams_of[10], (BATCHES, NC, D), 1.0, 6.0, ((0, 16), (1, 16))),
    }


EPS = 1e-05

def rounded(values):
    return lax.optimization_barrier(values.astype(jnp.bfloat16)).astype(jnp.float32)

def segment_of(ends, positions):
    return lax.optimization_barrier(jnp.sum((ends[None, :] <= positions[:, None]).astype(jnp.int32), axis=1))

def layer_norm(attended):
    mean = lax.optimization_barrier(jnp.mean(attended, axis=-1, keepdims=True))
    centered = attended - mean
    var = lax.optimization_barrier(jnp.mean(centered * centered, axis=-1, keepdims=True))
    rstd = lax.rsqrt(var + EPS)
    return (centered * rstd, rstd)

def reference(q_hist, k_hist, v_hist, u_hist, cand_q, cand_u, lengths, cand_user, w_out, grad_hist, grad_cand):
    scale = 1.0 / math.sqrt(HEAD_DIM)
    block_rows = TOK_DEV + CAND_DEV
    w32 = w_out.astype(jnp.float32)

    def per_batch(carry, items):
        qh, kh, vh, uh, cq, cu, lens, users, gh, gc = items
        ends = jnp.cumsum(lens.astype(jnp.int32))
        key_pos = jnp.arange(CONTEXT, dtype=jnp.int32)
        key_seg = segment_of(ends, key_pos)
        row_pos = jnp.concatenate([key_pos, jnp.full((NC,), CONTEXT, jnp.int32)])
        row_seg = jnp.concatenate([key_seg, users.astype(jnp.int32)])
        queries = jnp.concatenate([qh, cq]).astype(jnp.float32).reshape(CONTEXT + NC, HEADS, HEAD_DIM)
        keys3 = kh.astype(jnp.float32).reshape(CONTEXT, HEADS, HEAD_DIM)
        values3 = vh.astype(jnp.float32).reshape(CONTEXT, HEADS, HEAD_DIM)
        gates = jnp.concatenate([uh, cu]).astype(jnp.float32)
        upstream = jnp.concatenate([gh, gc]).astype(jnp.float32)
        blocks = CONTEXT // TOK_DEV
        q_blocks = queries.reshape(blocks, block_rows, HEADS, HEAD_DIM)
        p_blocks = row_pos.reshape(blocks, block_rows)
        s_blocks = row_seg.reshape(blocks, block_rows)

        def masking(pblk, sblk):
            return ((sblk[:, None] == key_seg[None, :]) & (key_pos[None, :] <= pblk[:, None])).astype(jnp.float32)

        def forward_block(args):
            qblk, pblk, sblk = args
            mask = masking(pblk, sblk)
            scores = jnp.einsum('rhe,khe->hrk', qblk, keys3) * scale
            weights = rounded(jax.nn.silu(scores) * mask[None])
            return jnp.einsum('hrk,khe->rhe', weights, values3).reshape(block_rows, HD)
        attended = lax.map(forward_block, (q_blocks, p_blocks, s_blocks)).reshape(CONTEXT + NC, HD)
        normed, rstd = layer_norm(attended)
        gated = rounded(normed * gates)
        outputs = jnp.dot(gated, w32).astype(jnp.bfloat16)
        grad_gated = jnp.dot(upstream, w32.T)
        grad_gates = (grad_gated * normed).astype(jnp.bfloat16)
        grad_normed = grad_gated * gates
        grad_att = rstd * (grad_normed - lax.optimization_barrier(jnp.mean(grad_normed, axis=-1, keepdims=True)) - normed * lax.optimization_barrier(jnp.mean(grad_normed * normed, axis=-1, keepdims=True)))
        grad3 = rounded(grad_att).reshape(blocks, block_rows, HEADS, HEAD_DIM)
        weight_term = jnp.dot(gated.T, upstream)

        def backward_block(acc, args):
            qblk, pblk, sblk, dblk = args
            mask = masking(pblk, sblk)
            scores = jnp.einsum('rhe,khe->hrk', qblk, keys3) * scale
            sig = jax.nn.sigmoid(scores)
            weights = rounded(scores * sig * mask[None])
            grad_w = jnp.einsum('rhe,khe->hrk', dblk, values3)
            grad_s = rounded(grad_w * sig * (1.0 + scores * (1.0 - sig)) * mask[None])
            dq = jnp.einsum('hrk,khe->rhe', grad_s, keys3) * scale
            dk = acc[0] + jnp.einsum('hrk,rhe->khe', grad_s, qblk) * scale
            dv = acc[1] + jnp.einsum('hrk,rhe->khe', weights, dblk)
            return ((dk, dv), dq.reshape(block_rows, HD))
        zeros3 = jnp.zeros((CONTEXT, HEADS, HEAD_DIM), jnp.float32)
        (dk, dv), dq = lax.scan(backward_block, (zeros3, zeros3), (q_blocks, p_blocks, s_blocks, grad3))
        dq = dq.reshape(CONTEXT + NC, HD).astype(jnp.bfloat16)
        results = (outputs[:CONTEXT], outputs[CONTEXT:], dq[:CONTEXT], dk.reshape(CONTEXT, HD).astype(jnp.bfloat16), dv.reshape(CONTEXT, HD).astype(jnp.bfloat16), grad_gates[:CONTEXT], dq[CONTEXT:], grad_gates[CONTEXT:])
        return (carry + weight_term, results)
    total, stacked = lax.scan(per_batch, jnp.zeros((HD, D), jnp.float32), (q_hist, k_hist, v_hist, u_hist, cand_q, cand_u, lengths, cand_user, grad_hist, grad_cand))
    grad_w_out = (total * (1.0 / math.sqrt(ROWS_ALL))).astype(jnp.bfloat16)
    return (stacked[0], stacked[1], stacked[2], stacked[3], stacked[4], stacked[5], stacked[6], stacked[7], grad_w_out)
```

```python
import functools
import math

import jax
import jax.numpy as jnp
from jax import lax
from jax.experimental import pallas as pl
from jax.experimental.pallas import tpu as pltpu
from jax.sharding import PartitionSpec as P

HEADS = 4
DIM = 128
EPS = 1e-05
ZN = 8
TOK = 192
CAND = 64
HALF = TOK // 2
CHALF = CAND // 2
ROWS = HALF + CHALF
META = 16
PACK = ROWS + META
KEYS = 3072
WIDTH = HEADS * DIM
MODEL = 1024
CANDS = ZN * CHALF
TILE = 512
SCALE = 1.0 / math.sqrt(DIM)
ORDER = (0, 1, 7, 2, 6, 3, 5, 4)
MESH = pl.DeviceIdType.MESH
bf16 = jnp.bfloat16
f32 = jnp.float32


def coords():
    ctx, dp = lax.axis_index("ctx"), lax.axis_index("dp")
    core = dp % 2
    return ctx // 2, ctx % 2, core, dp - core


def device(base, z, x, core):
    return {"ctx": z * 2 + x, "dp": base + core}


def greet(z, x, core, base, partner):
    barrier = pltpu.get_barrier_semaphore()
    for step in range(ZN):
        for other in range(2):
            if step or other:
                pl.semaphore_signal(
                    barrier,
                    inc=1,
                    device_id=device(base, (z + step) % ZN, x, (core + other) % 2),
                    device_id_type=MESH,
                )
    if partner:
        pl.semaphore_signal(
            barrier, inc=1, device_id=device(base, z, 1 - x, core), device_id_type=MESH
        )
    pl.semaphore_wait(barrier, 2 * ZN - 1 + int(partner))


def landed(ref, sem):
    pltpu.make_async_copy(ref, ref, sem).wait()


def remote(src, dst, send, recv, where):
    return pltpu.make_async_remote_copy(
        src_ref=src,
        dst_ref=dst,
        send_sem=send,
        recv_sem=recv,
        device_id=where,
        device_id_type=MESH,
    )


def half_start(core, z):
    return pl.multiple_of(((core + z) % 2) * HALF, HALF)


def spread_kernel(
    q_ref, k_ref, v_ref, c_ref, user_ref, len_ref, q_out, kv_out,
    pack, s_q, r_q, s_kv, r_kv, s_x, r_x, s_s, r_s,
):
    z, x, core, base = coords()
    greet(z, x, core, base, True)
    own = 2 * z + x
    dests = []
    for j in range(HEADS):
        h = (z // 2 + j) % HEADS
        dests.append((h, 2 * h + core))
    at_home = dests[0][1] == z

    def kv_source(j, kind):
        cols = pl.ds(pl.multiple_of(dests[j][0] * DIM, DIM), DIM)
        return (k_ref if kind == 0 else v_ref).at[:, cols]

    def send_kv(j, kind):
        return remote(
            kv_source(j, kind), kv_out.at[kind, own], s_kv.at[j, kind], r_kv.at[z],
            device(base, dests[j][1], x, kind),
        )

    def send_q(j, kind):
        return remote(
            pack.at[dests[j][0], kind], q_out.at[z], s_q.at[j, kind], r_q.at[z],
            device(base, dests[j][1], x, kind),
        )

    for j in range(HEADS):
        for kind in range(2):
            if j:
                send_kv(j, kind).start()
            else:
                here = at_home & (core == kind)

                @pl.when(here)
                def _():
                    pltpu.make_async_copy(
                        kv_source(j, kind), kv_out.at[kind, own], r_kv.at[z]
                    ).start()

                @pl.when(jnp.logical_not(here))
                def _():
                    send_kv(j, kind).start()

    lane = lax.broadcasted_iota(jnp.int32, (META, DIM), 1)
    row = lax.broadcasted_iota(jnp.int32, (META, DIM), 0)
    lens = jnp.zeros((META, DIM), jnp.int32)
    for i in range(4):
        lens = jnp.where(lane == i, len_ref[0, i], lens)
    lens_f = lens.astype(f32)
    high = jnp.floor(lens_f * (1.0 / 64.0))
    low = lens_f - high * 64.0
    users = jnp.broadcast_to(user_ref[...].astype(f32), (META, CAND)).astype(bf16)
    sel_j = lax.broadcasted_iota(jnp.int32, (CAND, DIM), 0)
    sel_l = lax.broadcasted_iota(jnp.int32, (CAND, DIM), 1)
    spot = CHALF * (z % 4)
    for kind in range(2):
        start = half_start(kind, z)
        pick = (
            (sel_l - spot + CHALF * kind == sel_j) & (sel_l >= spot) & (sel_l < spot + CHALF)
        ).astype(f32)
        placed = jnp.dot(users, pick.astype(bf16), preferred_element_type=f32)
        meta = jnp.where(row == 0, placed, jnp.where(row == 1, high, low)).astype(bf16)
        for h in range(HEADS):
            cols = slice(h * DIM, (h + 1) * DIM)
            pack[h, kind, 0:HALF, :] = q_ref[pl.ds(start, HALF), cols]
            pack[h, kind, HALF:ROWS, :] = c_ref[kind * CHALF : (kind + 1) * CHALF, cols]
            pack[h, kind, ROWS:PACK, :] = meta
    for j in range(HEADS):
        for kind in range(2):
            if j:
                send_q(j, kind).start()
            else:
                here = at_home & (core == kind)

                @pl.when(here)
                def _():
                    pltpu.make_async_copy(
                        pack.at[dests[j][0], kind], q_out.at[z], r_q.at[z]
                    ).start()

                @pl.when(jnp.logical_not(here))
                def _():
                    send_q(j, kind).start()

    def across(s, zi):
        slot = kv_out.at[core, s]
        return remote(slot, slot, s_x.at[zi], r_x.at[zi], device(base, z, 1 - x, core))

    def beside(s):
        slot = kv_out.at[core, s]
        return remote(slot, slot, s_s.at[s], r_s.at[s], device(base, z, x, 1 - core))

    def pass_on(step):
        zi = (z + ORDER[step]) % ZN
        s = 2 * zi + (1 - x)
        landed(kv_out.at[core, s], r_x.at[zi])
        beside(s).start()

    for step in range(ZN):
        zi = (z + ORDER[step]) % ZN
        s = 2 * zi + x
        landed(kv_out.at[core, s], r_kv.at[zi])
        across(s, zi).start()
        beside(s).start()
        if step >= 2:
            pass_on(step - 2)
    pass_on(ZN - 2)
    pass_on(ZN - 1)
    for zi in range(ZN):
        landed(q_out.at[zi], r_q.at[zi])
    for s in range(2 * ZN):
        landed(kv_out.at[1 - core, s], r_s.at[s])
    for s in range(2 * ZN):
        beside(s).wait_send()
    for zi in range(ZN):
        across(2 * zi + x, zi).wait_send()
    for j in range(HEADS):
        for kind in range(2):
            if j:
                send_kv(j, kind).wait_send()
                send_q(j, kind).wait_send()
            else:

                @pl.when(jnp.logical_not(at_home & (core == kind)))
                def _():
                    send_kv(j, kind).wait_send()
                    send_q(j, kind).wait_send()


def read_meta(q_ref):
    first = sum(q_ref[zi, ROWS:PACK, :].astype(f32) for zi in range(4))[0:1]
    second = sum(q_ref[zi, ROWS:PACK, :].astype(f32) for zi in range(4, 8))[0:1]
    users = jnp.concatenate([first, second], axis=1)
    block = q_ref[0, ROWS:PACK, :].astype(f32)
    lens = block[1:2] * 64.0 + block[2:3]
    lane = lax.broadcasted_iota(jnp.int32, (1, DIM), 1)
    ends = []
    for i in range(3):
        ends.append(jnp.sum(jnp.where(lane <= i, lens, 0.0)).astype(jnp.int32))
    starts = [jnp.sum((users < float(i)).astype(f32)).astype(jnp.int32) for i in range(1, 4)]
    sub = lax.broadcasted_iota(jnp.int32, (8, CANDS), 0).astype(f32)
    hot = (users == sub).astype(f32)
    before = jnp.sum((users < sub).astype(f32), axis=1, keepdims=True)
    rows = lax.broadcasted_iota(jnp.int32, (CANDS, CANDS), 0)
    cols = lax.broadcasted_iota(jnp.int32, (CANDS, CANDS), 1)
    upper = (rows < cols).astype(f32).astype(bf16)
    prior = jnp.dot(hot.astype(bf16), upper, preferred_element_type=f32)
    rank = jnp.sum(hot * (prior + before), axis=0, keepdims=True).astype(jnp.int32)
    perm = (rows == rank).astype(f32).astype(bf16)
    return ends, starts, perm


def first_of(ends, pos):
    low = jnp.where(pos >= ends[0], ends[0], 0)
    low = jnp.where(pos >= ends[1], ends[1], low)
    return jnp.where(pos >= ends[2], ends[2], low)


def cand_range(ends, starts, row):
    low = jnp.where(row >= starts[0], ends[0], 0)
    low = jnp.where(row >= starts[1], ends[1], low)
    low = jnp.where(row >= starts[2], ends[2], low)
    high = jnp.where(row >= starts[0], ends[1], ends[0])
    high = jnp.where(row >= starts[1], ends[2], high)
    high = jnp.where(row >= starts[2], KEYS, high)
    return low, high


def hist_start(zi):
    z, x, core, base = coords()
    return (2 * zi + x) * TOK + ((core + zi) % 2) * HALF


def hist_bounds(ends, zi):
    p0 = hist_start(zi)
    pos = p0 + lax.broadcasted_iota(jnp.int32, (HALF, 1), 0)
    return first_of(ends, pos), pos + 1, first_of(ends, p0), p0 + HALF


def cand_bounds(ends, starts, r0, count):
    row = r0 + lax.broadcasted_iota(jnp.int32, (count, 1), 0)
    low, high = cand_range(ends, starts, row)
    return low, high, cand_range(ends, starts, r0)[0], cand_range(ends, starts, r0 + count - 1)[1]


CTILE = 128
NT = (((1,), (1,)), ((), ()))
TN = (((0,), (0,)), ((), ()))


def forward_kernel(q_ref, kv_ref, a_ref, qs_ref, as_ref):
    ends, starts, perm = read_meta(q_ref)

    def tile(q, bounds):
        low, high, first, last = bounds

        def step(i, acc):
            start = pl.multiple_of(i * TILE, TILE)
            keys = kv_ref[0, pl.ds(start, TILE), :]
            values = kv_ref[1, pl.ds(start, TILE), :]
            t = lax.dot_general(q, keys, NT, preferred_element_type=f32) * (0.5 * SCALE)
            pos = start + lax.broadcasted_iota(jnp.int32, t.shape, 1)
            gate = jnp.where((pos >= low) & (pos < high), 1.0 + jnp.tanh(t), 0.0)
            return acc + jnp.dot((t * gate).astype(bf16), values, preferred_element_type=f32)

        return lax.fori_loop(
            first // TILE, (last + TILE - 1) // TILE, step, jnp.zeros((q.shape[0], DIM), f32)
        )

    for zi in range(ZN):
        a_ref[zi, 0:HALF, :] = tile(q_ref[zi, 0:HALF, :], hist_bounds(ends, zi)).astype(bf16)
    cand = jnp.concatenate([q_ref[zi, HALF:ROWS, :] for zi in range(ZN)], axis=0)
    qs_ref[...] = jnp.dot(perm, cand, preferred_element_type=f32).astype(bf16)
    for r0 in range(0, CANDS, CTILE):
        as_ref[r0 : r0 + CTILE, :] = tile(
            qs_ref[r0 : r0 + CTILE, :], cand_bounds(ends, starts, r0, CTILE)
        ).astype(bf16)
    back = lax.dot_general(perm, as_ref[...], TN, preferred_element_type=f32).astype(bf16)
    for zi in range(ZN):
        a_ref[zi, HALF:ROWS, :] = back[zi * CHALF : (zi + 1) * CHALF]


def backward_kernel(q_ref, kv_ref, da_ref, dq_ref, dkv_ref, acc, qs_ref, ds_ref, dqs_ref):
    ends, starts, perm = read_meta(q_ref)
    acc[...] = jnp.zeros(acc.shape, f32)

    def tile(q, da, bounds):
        low, high, first, last = bounds

        def step(i, dq):
            start = pl.multiple_of(i * TILE, TILE)
            keys = kv_ref[0, pl.ds(start, TILE), :]
            values = kv_ref[1, pl.ds(start, TILE), :]
            t = lax.dot_general(q, keys, NT, preferred_element_type=f32) * (0.5 * SCALE)
            dp = lax.dot_general(da, values, NT, preferred_element_type=f32)
            pos = start + lax.broadcasted_iota(jnp.int32, t.shape, 1)
            gate = jnp.where((pos >= low) & (pos < high), 1.0 + jnp.tanh(t), 0.0)
            p = t * gate
            ds = (dp * (gate * ((1.0 + t + t) - p))).astype(bf16)
            acc[0, pl.ds(start, TILE), :] += lax.dot_general(
                ds, q, TN, preferred_element_type=f32
            )
            acc[1, pl.ds(start, TILE), :] += lax.dot_general(
                p.astype(bf16), da, TN, preferred_element_type=f32
            )
            return dq + jnp.dot(ds, keys, preferred_element_type=f32)

        dq = lax.fori_loop(
            first // TILE, (last + TILE - 1) // TILE, step, jnp.zeros((q.shape[0], DIM), f32)
        )
        return (dq * (0.5 * SCALE)).astype(bf16)

    for zi in range(ZN):
        dq_ref[zi, 0:HALF, :] = tile(
            q_ref[zi, 0:HALF, :], da_ref[zi, 0:HALF, :], hist_bounds(ends, zi)
        )
    cand = jnp.concatenate([q_ref[zi, HALF:ROWS, :] for zi in range(ZN)], axis=0)
    qs_ref[...] = jnp.dot(perm, cand, preferred_element_type=f32).astype(bf16)
    cand = jnp.concatenate([da_ref[zi, HALF:ROWS, :] for zi in range(ZN)], axis=0)
    ds_ref[...] = jnp.dot(perm, cand, preferred_element_type=f32).astype(bf16)
    for r0 in range(0, CANDS, CTILE):
        dqs_ref[r0 : r0 + CTILE, :] = tile(
            qs_ref[r0 : r0 + CTILE, :],
            ds_ref[r0 : r0 + CTILE, :],
            cand_bounds(ends, starts, r0, CTILE),
        )
    back = lax.dot_general(perm, dqs_ref[...], TN, preferred_element_type=f32).astype(bf16)
    for zi in range(ZN):
        dq_ref[zi, HALF:ROWS, :] = back[zi * CHALF : (zi + 1) * CHALF]
    dkv_ref[0] = (acc[0] * (0.5 * SCALE)).astype(bf16)
    dkv_ref[1] = acc[1].astype(bf16)


def middle_kernel(
    a_ref, u_ref, cu_ref, g_ref, cg_ref, w_ref, y_out, cy_out, du_out, cdu_out, gw_out, da_out,
    a_in, da_pack, gated, up, dgs, s_a, r_a, s_d, r_d,
):
    z, x, core, base = coords()
    greet(z, x, core, base, False)
    batch = z % 2
    head = z // 2

    def send_a(step):
        zi = (z + step) % ZN
        return zi, a_ref.at[zi], a_in.at[head, core], s_a.at[step], r_a.at[head, core]

    for step in (4, 3, 5, 2, 6, 1, 7):
        zi, src, dst, send, recv = send_a(step)
        remote(src, dst, send, recv, device(base, zi, x, batch)).start()
    zi, src, dst, send, recv = send_a(0)

    @pl.when(core == batch)
    def _():
        pltpu.make_async_copy(src, dst, recv).start()

    @pl.when(core != batch)
    def _():
        remote(src, dst, send, recv, device(base, z, x, batch)).start()

    starts = [half_start(kind, z) for kind in range(2)]
    for kind in range(2):
        up[kind, 0:HALF, :] = g_ref[pl.ds(starts[kind], HALF), :]
        up[kind, HALF:ROWS, :] = cg_ref[kind * CHALF : (kind + 1) * CHALF, :]
        dgs[kind] = lax.dot_general(up[kind], w_ref[...], NT, preferred_element_type=f32)

    def send_d(j, kind):
        h = (z // 2 + j) % HEADS
        z2 = 2 * h + core
        return (
            z2 == z,
            da_pack.at[h, kind],
            da_out.at[z],
            s_d.at[j, kind],
            r_d.at[z],
            device(base, z2, x, kind),
        )

    for kind in range(2):
        for h in range(HEADS):
            landed(a_in.at[h, kind], r_a.at[h, kind])
        att = jnp.concatenate([a_in[h, kind] for h in range(HEADS)], axis=1).astype(f32)
        mean = jnp.mean(att, axis=1, keepdims=True)
        centered = att - mean
        var = jnp.mean(centered * centered, axis=1, keepdims=True)
        rstd = lax.rsqrt(var + EPS)
        normed = centered * rstd
        gates = jnp.concatenate(
            [u_ref[pl.ds(starts[kind], HALF), :], cu_ref[kind * CHALF : (kind + 1) * CHALF, :]],
            axis=0,
        ).astype(f32)
        gated[kind] = (normed * gates).astype(bf16)
        dg = dgs[kind]
        du = (dg * normed).astype(bf16)
        du_out[pl.ds(starts[kind], HALF), :] = du[0:HALF]
        cdu_out[kind * CHALF : (kind + 1) * CHALF, :] = du[HALF:ROWS]
        dn = dg * gates
        da = rstd * (
            dn
            - jnp.mean(dn, axis=1, keepdims=True)
            - normed * jnp.mean(dn * normed, axis=1, keepdims=True)
        )
        for h in range(HEADS):
            da_pack[h, kind] = da[:, h * DIM : (h + 1) * DIM].astype(bf16)
        for j in range(HEADS):
            home, src, dst, send, recv, where = send_d(j, kind)
            if j:
                remote(src, dst, send, recv, where).start()
            else:
                here = home & (core == kind)

                @pl.when(here)
                def _():
                    pltpu.make_async_copy(src, dst, recv).start()

                @pl.when(jnp.logical_not(here))
                def _():
                    remote(src, dst, send, recv, where).start()

    for kind in range(2):
        y = jnp.dot(gated[kind], w_ref[...], preferred_element_type=f32).astype(bf16)
        y_out[pl.ds(starts[kind], HALF), :] = y[0:HALF]
        cy_out[kind * CHALF : (kind + 1) * CHALF, :] = y[HALF:ROWS]
    gw_out[...] = (
        lax.dot_general(gated[0], up[0], TN, preferred_element_type=f32)
        + lax.dot_general(gated[1], up[1], TN, preferred_element_type=f32)
    ) * (1.0 / 256.0)

    for zi in range(ZN):
        landed(da_out.at[zi], r_d.at[zi])
    for step in range(1, ZN):
        zi, src, dst, send, recv = send_a(step)
        remote(src, dst, send, recv, device(base, zi, x, batch)).wait_send()

    @pl.when(core != batch)
    def _():
        zi, src, dst, send, recv = send_a(0)
        remote(src, dst, send, recv, device(base, zi, x, batch)).wait_send()

    for j in range(HEADS):
        for kind in range(2):
            home, src, dst, send, recv, where = send_d(j, kind)
            if j:
                remote(src, dst, send, recv, where).wait_send()
            else:

                @pl.when(jnp.logical_not(home & (core == kind)))
                def _():
                    remote(src, dst, send, recv, where).wait_send()


def collect_kernel(
    dq_ref, dkv_ref, q_out, c_out, k_out, v_out,
    q_in, beside_in, across_in, sums, kv_in, s_q, r_q, s_s, r_s, s_x, r_x, s_kv, r_kv,
):
    z, x, core, base = coords()
    greet(z, x, core, base, True)
    batch = z % 2
    head = z // 2
    order = (4, 3, 5, 2, 6, 1, 7, 0)

    def shard(step, side):
        return 2 * ((z + step) % ZN) + side

    def beside(step, side):
        s = shard(step, side)
        return remote(
            dkv_ref.at[1 - core, s], beside_in.at[s], s_s.at[s], r_s.at[s],
            device(base, z, x, 1 - core),
        )

    def across(step):
        zi = (z + step) % ZN
        return remote(
            sums.at[2 * zi + 1 - x], across_in.at[zi], s_x.at[zi], r_x.at[zi],
            device(base, z, 1 - x, core),
        )

    def q_parts(step):
        zi = (z + step) % ZN
        return dq_ref.at[zi], q_in.at[head, core], s_q.at[step], r_q.at[head, core]

    def kv_parts(step):
        zi = (z + step) % ZN
        return sums.at[2 * zi + x], kv_in.at[head, core], s_kv.at[step], r_kv.at[head, core]

    def home(step, parts):
        src, dst, send, recv = parts(step)
        where = device(base, (z + step) % ZN, x, batch)
        if step:
            remote(src, dst, send, recv, where).start()
            return

        @pl.when(core == batch)
        def _():
            pltpu.make_async_copy(src, dst, recv).start()

        @pl.when(core != batch)
        def _():
            remote(src, dst, send, recv, where).start()

    for step in order:
        beside(step, 1 - x).start()
    for step in order:
        beside(step, x).start()
    for step in order:
        home(step, q_parts)

    def add_beside(step, side):
        s = shard(step, side)
        landed(beside_in.at[s], r_s.at[s])
        return dkv_ref[core, s].astype(f32) + beside_in[s].astype(f32)

    def finish(step):
        zi = (z + step) % ZN
        total = add_beside(step, x)
        landed(across_in.at[zi], r_x.at[zi])
        sums[2 * zi + x] = (total + across_in[zi].astype(f32)).astype(bf16)
        home(step, kv_parts)

    for i, step in enumerate(order):
        sums[shard(step, 1 - x)] = add_beside(step, 1 - x).astype(bf16)
        across(step).start()
        if i >= 2:
            finish(order[i - 2])
    finish(order[-2])
    finish(order[-1])

    for kind in range(2):
        start = half_start(kind, z)
        for h in range(HEADS):
            cols = slice(h * DIM, (h + 1) * DIM)
            landed(q_in.at[h, kind], r_q.at[h, kind])
            q_out[pl.ds(start, HALF), cols] = q_in[h, kind, 0:HALF, :]
            c_out[kind * CHALF : (kind + 1) * CHALF, cols] = q_in[h, kind, HALF:ROWS, :]
    for h in range(HEADS):
        cols = slice(h * DIM, (h + 1) * DIM)
        for kind, out in ((0, k_out), (1, v_out)):
            landed(kv_in.at[h, kind], r_kv.at[h, kind])
            out[:, cols] = kv_in[h, kind]

    for step in order:
        beside(step, x).wait_send()
        beside(step, 1 - x).wait_send()
        across(step).wait_send()
        for parts in (q_parts, kv_parts):
            src, dst, send, recv = parts(step)
            where = device(base, (z + step) % ZN, x, batch)
            if step:
                remote(src, dst, send, recv, where).wait_send()
            else:

                @pl.when(core != batch)
                def _():
                    remote(src, dst, send, recv, where).wait_send()


VM = pl.BlockSpec(memory_space=pltpu.VMEM)
SM = pl.BlockSpec(memory_space=pltpu.SMEM)
DMA = pltpu.SemaphoreType.DMA


def shape(*dims, dtype=bf16):
    return jax.ShapeDtypeStruct(dims, dtype)


def params(collective=None, mib=40):
    if collective is None:
        return pltpu.CompilerParams(vmem_limit_bytes=mib << 20)
    return pltpu.CompilerParams(
        vmem_limit_bytes=mib << 20, collective_id=collective, has_side_effects=True
    )


def local(
    q_hist, k_hist, v_hist, u_hist, cand_q, cand_u, lengths, cand_user, w_out, grad_hist, grad_cand
):
    packs, kv = pl.pallas_call(
        spread_kernel,
        out_shape=(shape(ZN, PACK, DIM), shape(2, 2 * ZN, TOK, DIM)),
        in_specs=[VM] * 5 + [SM],
        out_specs=(VM, VM),
        scratch_shapes=[
            pltpu.VMEM((HEADS, 2, PACK, DIM), bf16),
            DMA((HEADS, 2)),
            DMA((ZN,)),
            DMA((HEADS, 2)),
            DMA((ZN,)),
            DMA((ZN,)),
            DMA((ZN,)),
            DMA((2 * ZN,)),
            DMA((2 * ZN,)),
        ],
        compiler_params=params(0),
        name="spread",
    )(q_hist[0], k_hist[0], v_hist[0], cand_q[0], cand_user, lengths)
    kv = kv.reshape(2, KEYS, DIM)
    att = pl.pallas_call(
        forward_kernel,
        out_shape=shape(ZN, ROWS, DIM),
        in_specs=[VM] * 2,
        out_specs=VM,
        scratch_shapes=[pltpu.VMEM((CANDS, DIM), bf16)] * 2,
        compiler_params=params(),
        name="forward",
    )(packs, kv)
    y, cy, du, cdu, gw, datt = pl.pallas_call(
        middle_kernel,
        out_shape=(
            shape(TOK, MODEL),
            shape(CAND, MODEL),
            shape(TOK, WIDTH),
            shape(CAND, WIDTH),
            shape(WIDTH, MODEL, dtype=f32),
            shape(ZN, ROWS, DIM),
        ),
        in_specs=[VM] * 6,
        out_specs=(VM,) * 6,
        scratch_shapes=[
            pltpu.VMEM((HEADS, 2, ROWS, DIM), bf16),
            pltpu.VMEM((HEADS, 2, ROWS, DIM), bf16),
            pltpu.VMEM((2, ROWS, WIDTH), bf16),
            pltpu.VMEM((2, ROWS, MODEL), bf16),
            pltpu.VMEM((2, ROWS, WIDTH), f32),
            DMA((ZN,)),
            DMA((HEADS, 2)),
            DMA((HEADS, 2)),
            DMA((ZN,)),
        ],
        compiler_params=params(1),
        name="middle",
    )(att, u_hist[0], cand_u[0], grad_hist[0], grad_cand[0], w_out)
    grad_weight = lax.psum(gw, ("ctx", "dp")).astype(bf16)
    dq, dkv = pl.pallas_call(
        backward_kernel,
        out_shape=(shape(ZN, ROWS, DIM), shape(2, KEYS, DIM)),
        in_specs=[VM] * 3,
        out_specs=(VM, VM),
        scratch_shapes=[pltpu.VMEM((2, KEYS, DIM), f32)] + [pltpu.VMEM((CANDS, DIM), bf16)] * 3,
        compiler_params=params(),
        name="backward",
    )(packs, kv, datt)
    gq, gcq, gk, gv = pl.pallas_call(
        collect_kernel,
        out_shape=(shape(TOK, WIDTH), shape(CAND, WIDTH), shape(TOK, WIDTH), shape(TOK, WIDTH)),
        in_specs=[VM] * 2,
        out_specs=(VM,) * 4,
        scratch_shapes=[
            pltpu.VMEM((HEADS, 2, ROWS, DIM), bf16),
            pltpu.VMEM((2 * ZN, TOK, DIM), bf16),
            pltpu.VMEM((ZN, TOK, DIM), bf16),
            pltpu.VMEM((2 * ZN, TOK, DIM), bf16),
            pltpu.VMEM((HEADS, 2, TOK, DIM), bf16),
            DMA((ZN,)),
            DMA((HEADS, 2)),
            DMA((2 * ZN,)),
            DMA((2 * ZN,)),
            DMA((ZN,)),
            DMA((ZN,)),
            DMA((ZN,)),
            DMA((HEADS, 2)),
        ],
        compiler_params=params(2),
        name="collect",
    )(dq, dkv.reshape(2, 2 * ZN, TOK, DIM))
    return (
        y[None], cy[None], gq[None], gk[None], gv[None], du[None], gcq[None], cdu[None],
        grad_weight,
    )


def solution(mesh):
    rows = P("dp", "ctx", None)
    return jax.shard_map(
        local,
        mesh=mesh,
        in_specs=(rows, rows, rows, rows, rows, rows, P("dp", None), P("dp", "ctx"), P(), rows, rows),
        out_specs=(rows, rows, rows, rows, rows, rows, rows, rows, P()),
        check_vma=False,
    )
```

```python
import functools
import math

import jax
import jax.numpy as jnp
from jax import lax
from jax.experimental import pallas as pl
from jax.experimental.pallas import tpu as pltpu
from jax.sharding import PartitionSpec as P

HEADS = 4
DIM = 128
EPS = 1e-05
ZN = 8
SIDE = 4
BAND = 32
SLAB = 256
PART = 64
TOK = 192
CAND = 64
HALF = TOK // 2
CHALF = CAND // 2
ROWS = HALF + CHALF
META = 16
PACK = ROWS + META
KEYS = 3072
WIDTH = HEADS * DIM
MODEL = 1024
CANDS = ZN * CHALF
SCALE = 1.0 / math.sqrt(DIM)
ORDER = (0, 1, 7, 2, 6, 3, 5, 4)
TILE = 768
GROUP = 4
NTILE = 11
BLOCKS = KEYS // TILE
ROOM = BLOCKS * (NTILE + GROUP)
STAGES = {0: 1, 2: 2, 4: 3, 6: 4}
MESH = pl.DeviceIdType.MESH
bf16 = jnp.bfloat16
f32 = jnp.float32


def coords():
    ctx, dp = lax.axis_index("ctx"), lax.axis_index("dp")
    core = dp % 2
    return ctx // 2, ctx % 2, core, dp - core


def device(base, z, x, core):
    return {"ctx": z * 2 + x, "dp": base + core}


def column(z, x, core, base):
    return [
        device(base, (z + step) % ZN, x, (core + other) % 2)
        for step in range(ZN)
        for other in range(2)
        if step or other
    ]


def spots(x, base):
    return base // 8 * 2 + x, base % 8 // 2


def along(z, core, axis, spot, place):
    wide, high = (place, spot[1]) if axis == 0 else (spot[0], place)
    return {"ctx": z * 2 + wide % 2, "dp": wide // 2 * 8 + high * 2 + core}


def plane(z, x, core, base):
    spot = spots(x, base)
    return [
        along(z, core, axis, spot, (spot[axis] + step) % SIDE)
        for axis in range(2)
        for step in range(1, SIDE)
    ]


def greet(others):
    barrier = pltpu.get_barrier_semaphore()
    for other in others:
        pl.semaphore_signal(barrier, inc=1, device_id=other, device_id_type=MESH)
    pl.semaphore_wait(barrier, len(others))


def landed(ref, sem):
    pltpu.make_async_copy(ref, ref, sem).wait()


def remote(src, dst, send, recv, where):
    return pltpu.make_async_remote_copy(
        src_ref=src,
        dst_ref=dst,
        send_sem=send,
        recv_sem=recv,
        device_id=where,
        device_id_type=MESH,
    )


def half_start(core, z):
    return pl.multiple_of(((core + z) % 2) * HALF, HALF)


def spread_kernel(
    q_hbm, k_hbm, v_hbm, c_hbm, user_hbm, len_hbm, q_out, kv_out,
    q_ref, k_ref, v_ref, c_ref, user_ref, len_ref, l_sem, pack, s_q, r_q, s_kv, r_kv, s_x, r_x, s_s, r_s,
):
    z, x, core, base = coords()
    fetches = [
        pltpu.make_async_copy(src, dst, l_sem.at[i])
        for i, (src, dst) in enumerate(
            (
                (k_hbm, k_ref),
                (v_hbm, v_ref),
                (q_hbm, q_ref),
                (c_hbm, c_ref),
                (user_hbm, user_ref),
                (len_hbm, len_ref),
            )
        )
    ]
    for fetch in fetches:
        fetch.start()
    greet(column(z, x, core, base) + [device(base, z, 1 - x, core)])
    own = 2 * z + x
    turn = jnp.where(z % 2 > core, 1, 3)
    turns = (0, turn, 4 - turn, 2)
    dests = []
    for j in range(HEADS):
        h = (z // 2 + turns[j]) % HEADS
        dests.append((h, 2 * h + core))
    at_home = dests[0][1] == z

    def kv_source(j, kind):
        cols = pl.ds(pl.multiple_of(dests[j][0] * DIM, DIM), DIM)
        return (k_ref if kind == 0 else v_ref).at[:, cols]

    def send_kv(j, kind):
        return remote(
            kv_source(j, kind), kv_out.at[kind, own], s_kv.at[j, kind], r_kv.at[z],
            device(base, dests[j][1], x, kind),
        )

    def send_q(j, kind):
        return remote(
            pack.at[dests[j][0], kind], q_out.at[z], s_q.at[j, kind], r_q.at[z],
            device(base, dests[j][1], x, kind),
        )

    for fetch in fetches[:2]:
        fetch.wait()
    def start_all(j, send, local_pair):
        for kind in range(2):
            if j:
                send(j, kind).start()
            else:
                here = at_home & (core == kind)

                @pl.when(here)
                def _():
                    pltpu.make_async_copy(*local_pair(kind)).start()

                @pl.when(jnp.logical_not(here))
                def _():
                    send(j, kind).start()

    def sent(j, send):
        for kind in range(2):
            if j:
                send(j, kind).wait_send()
            else:

                @pl.when(jnp.logical_not(at_home & (core == kind)))
                def _():
                    send(j, kind).wait_send()

    def start_kv(j):
        start_all(j, send_kv, lambda kind: (kv_source(0, kind), kv_out.at[kind, own], r_kv.at[z]))

    def start_q(j):
        start_all(j, send_q, lambda kind: (pack.at[dests[0][0], kind], q_out.at[z], r_q.at[z]))

    start_kv(0)
    start_kv(1)
    for fetch in fetches[2:]:
        fetch.wait()
    lane = lax.broadcasted_iota(jnp.int32, (META, DIM), 1)
    row = lax.broadcasted_iota(jnp.int32, (META, DIM), 0)
    lens = jnp.zeros((META, DIM), jnp.int32)
    for i in range(4):
        lens = jnp.where(lane == i, len_ref[0, i], lens)
    lens_f = lens.astype(f32)
    high = jnp.floor(lens_f * (1.0 / 64.0))
    low = lens_f - high * 64.0
    users = jnp.broadcast_to(user_ref[...].astype(f32), (META, CAND)).astype(bf16)
    sel_j = lax.broadcasted_iota(jnp.int32, (CAND, DIM), 0)
    sel_l = lax.broadcasted_iota(jnp.int32, (CAND, DIM), 1)
    spot = CHALF * (z % 4)
    for kind in range(2):
        start = half_start(kind, z)
        pick = (
            (sel_l - spot + CHALF * kind == sel_j) & (sel_l >= spot) & (sel_l < spot + CHALF)
        ).astype(f32)
        placed = jnp.dot(users, pick.astype(bf16), preferred_element_type=f32)
        meta = jnp.where(row == 0, placed, jnp.where(row == 1, high, low)).astype(bf16)
        for h in range(HEADS):
            cols = slice(h * DIM, (h + 1) * DIM)
            pack[h, kind, 0:HALF, :] = q_ref[pl.ds(start, HALF), cols]
            pack[h, kind, HALF:ROWS, :] = c_ref[kind * CHALF : (kind + 1) * CHALF, cols]
            pack[h, kind, ROWS:PACK, :] = meta
    def across(s, zi):
        slot = kv_out.at[core, s]
        return remote(slot, slot, s_x.at[zi], r_x.at[zi], device(base, z, 1 - x, core))

    def beside(s):
        slot = kv_out.at[core, s]
        return remote(slot, slot, s_s.at[s], r_s.at[s], device(base, z, x, 1 - core))

    def pass_on(step):
        zi = (z + ORDER[step]) % ZN
        s = 2 * zi + (1 - x)
        landed(kv_out.at[core, s], r_x.at[zi])
        beside(s).start()

    for step in range(ZN):
        zi = (z + ORDER[step]) % ZN
        s = 2 * zi + x
        landed(kv_out.at[core, s], r_kv.at[zi])
        across(s, zi).start()
        beside(s).start()
        if step == 0:
            sent(0, send_kv)
            start_kv(2)
        if step == 2:
            sent(1, send_kv)
            start_kv(3)
        if step == 4:
            sent(2, send_kv)
            start_q(0)
            start_q(1)
        if step == 6:
            sent(3, send_kv)
            start_q(2)
            start_q(3)
        if step >= 2:
            pass_on(step - 2)
    pass_on(ZN - 2)
    pass_on(ZN - 1)
    for zi in range(ZN):
        landed(q_out.at[zi], r_q.at[zi])
    for s in range(2 * ZN):
        landed(kv_out.at[1 - core, s], r_s.at[s])
    for s in range(2 * ZN):
        beside(s).wait_send()
    for zi in range(ZN):
        across(2 * zi + x, zi).wait_send()
    for j in range(HEADS):
        sent(j, send_q)


def read_meta(q_ref):
    first = sum(q_ref[zi, ROWS:PACK, :].astype(f32) for zi in range(4))[0:1]
    second = sum(q_ref[zi, ROWS:PACK, :].astype(f32) for zi in range(4, 8))[0:1]
    users = jnp.concatenate([first, second], axis=1)
    block = q_ref[0, ROWS:PACK, :].astype(f32)
    lens = block[1:2] * 64.0 + block[2:3]
    lane = lax.broadcasted_iota(jnp.int32, (1, DIM), 1)
    ends = []
    for i in range(3):
        ends.append(jnp.sum(jnp.where(lane <= i, lens, 0.0)).astype(jnp.int32))
    starts = [jnp.sum((users < float(i)).astype(f32)).astype(jnp.int32) for i in range(1, 4)]
    sub = lax.broadcasted_iota(jnp.int32, (8, CANDS), 0).astype(f32)
    hot = (users == sub).astype(f32)
    before = jnp.sum((users < sub).astype(f32), axis=1, keepdims=True)
    rows = lax.broadcasted_iota(jnp.int32, (CANDS, CANDS), 0)
    cols = lax.broadcasted_iota(jnp.int32, (CANDS, CANDS), 1)
    upper = (rows < cols).astype(f32).astype(bf16)
    prior = jnp.dot(hot.astype(bf16), upper, preferred_element_type=f32)
    rank = jnp.sum(hot * (prior + before), axis=0, keepdims=True).astype(jnp.int32)
    perm = (rows == rank).astype(f32).astype(bf16)
    return ends, starts, perm


def first_of(ends, pos):
    low = jnp.where(pos >= ends[0], ends[0], 0)
    low = jnp.where(pos >= ends[1], ends[1], low)
    return jnp.where(pos >= ends[2], ends[2], low)


def cand_range(ends, starts, row):
    low = jnp.where(row >= starts[0], ends[0], 0)
    low = jnp.where(row >= starts[1], ends[1], low)
    low = jnp.where(row >= starts[2], ends[2], low)
    high = jnp.where(row >= starts[0], ends[1], ends[0])
    high = jnp.where(row >= starts[1], ends[2], high)
    high = jnp.where(row >= starts[2], KEYS, high)
    return low, high


def hist_start(zi):
    z, x, core, base = coords()
    return (2 * zi + x) * TOK + ((core + zi) % 2) * HALF


NT = (((1,), (1,)), ((), ()))
TN = (((0,), (0,)), ((), ()))


def work_list(z, x, core, ends, starts, tiles, counts):
    ranges = []
    for zi in range(ZN):
        p0 = hist_start(zi)
        ranges.append((first_of(ends, p0), p0 + HALF))
    for c in range(NTILE - ZN):
        first, last = c * HALF, min((c + 1) * HALF, CANDS) - 1
        ranges.append((cand_range(ends, starts, first)[0], cand_range(ends, starts, last)[1]))
    for block in range(BLOCKS):
        at = block * (NTILE + GROUP)
        used = jnp.int32(0)
        for i, (low, high) in enumerate(ranges):
            hit = (low < (block + 1) * TILE) & (high > block * TILE)
            tiles[at + used] = jnp.int32(i)
            used = used + hit.astype(jnp.int32)
        for i in range(GROUP - 1):
            tiles[at + used + i] = jnp.int32(NTILE)
        counts[block] = (used + GROUP - 1) // GROUP


def set_bounds(ends, starts, low_ref, high_ref):
    lane = lax.broadcasted_iota(jnp.int32, (HALF, DIM), 1)
    row = lax.broadcasted_iota(jnp.int32, (HALF, DIM), 0)
    for zi in range(ZN):
        pos = hist_start(zi) + row
        low_ref[zi] = first_of(ends, pos) - lane
        high_ref[zi] = pos + 1 - lane
    for c in range(NTILE - ZN):
        low, high = cand_range(ends, starts, c * HALF + row)
        low_ref[ZN + c] = low - lane
        high_ref[ZN + c] = jnp.where(c * HALF + row < CANDS, high, 0) - lane
    low_ref[NTILE] = jnp.zeros((HALF, DIM), jnp.int32)
    high_ref[NTILE] = jnp.full((HALF, DIM), -KEYS, jnp.int32)


def set_bounds_t(ends, starts, low_ref, high_ref):
    lane = lax.broadcasted_iota(jnp.int32, (8, HALF), 1)
    for zi in range(ZN):
        pos = hist_start(zi) + lane
        low_ref[zi] = first_of(ends, pos)
        high_ref[zi] = pos + 1
    for c in range(NTILE - ZN):
        low, high = cand_range(ends, starts, c * HALF + lane)
        low_ref[ZN + c] = low
        high_ref[ZN + c] = jnp.where(c * HALF + lane < CANDS, high, 0)
    low_ref[NTILE] = jnp.zeros((8, HALF), jnp.int32)
    high_ref[NTILE] = jnp.full((8, HALF), -KEYS, jnp.int32)


def inside(low, high, start):
    masks = []
    for i in range(TILE // DIM):
        at = start + i * DIM
        masks.append((low <= at) & (high > at))
    return jnp.concatenate(masks, axis=1)


def load_rows(src, perm, dst):
    for zi in range(ZN):
        dst[zi] = src[zi, 0:HALF, :]
    cand = jnp.concatenate([src[zi, HALF:ROWS, :] for zi in range(ZN)], axis=0)
    cand = jnp.dot(perm, cand, preferred_element_type=f32).astype(bf16)
    dst[ZN] = cand[0:HALF]
    dst[ZN + 1] = cand[HALF : 2 * HALF]
    dst[ZN + 2, 0 : CANDS - 2 * HALF, :] = cand[2 * HALF :]
    dst[ZN + 2, CANDS - 2 * HALF :, :] = jnp.zeros((3 * HALF - CANDS, DIM), bf16)
    dst[NTILE] = jnp.zeros((HALF, DIM), bf16)


def store_rows(acc, perm, dst, factor):
    for zi in range(ZN):
        dst[zi, 0:HALF, :] = (acc[zi] * factor).astype(bf16)
    cand = jnp.concatenate([acc[ZN], acc[ZN + 1], acc[ZN + 2, 0 : CANDS - 2 * HALF, :]], axis=0)
    back = lax.dot_general(
        perm, (cand * factor).astype(bf16), TN, preferred_element_type=f32
    ).astype(bf16)
    for zi in range(ZN):
        dst[zi, HALF:ROWS, :] = back[zi * CHALF : (zi + 1) * CHALF]


def group_of(tiles, block, step):
    at = block * (NTILE + GROUP) + step * GROUP
    return [tiles[at + i] for i in range(GROUP)]


def stacked(ref, picks):
    return jnp.concatenate([ref[i] for i in picks], axis=0)


def forward_kernel(q_ref, kv_ref, a_ref, q_all, acc, low_ref, high_ref, tiles, counts):
    z, x, core, base = coords()
    ends, starts, perm = read_meta(q_ref)
    work_list(z, x, core, ends, starts, tiles, counts)
    set_bounds(ends, starts, low_ref, high_ref)
    load_rows(q_ref, perm, q_all)
    acc[...] = jnp.zeros(acc.shape, f32)
    for block in range(BLOCKS):
        start = block * TILE

        def step(i, carry):
            picks = group_of(tiles, block, i)
            keys = kv_ref[0, start : start + TILE, :]
            values = kv_ref[1, start : start + TILE, :]
            q = stacked(q_all, picks)
            t = lax.dot_general(q, keys, NT, preferred_element_type=f32) * (0.5 * SCALE)
            ok = inside(stacked(low_ref, picks), stacked(high_ref, picks), start)
            gate = jnp.where(ok, 1.0 + jnp.tanh(t), 0.0)
            out = jnp.dot((t * gate).astype(bf16), values, preferred_element_type=f32)
            for n, pick in enumerate(picks):
                acc[pick] += out[n * HALF : (n + 1) * HALF]
            return carry

        lax.fori_loop(0, counts[block], step, jnp.int32(0))
    store_rows(acc, perm, a_ref, 1.0)


def ordered(src, hist, cand, sems):
    z = coords()[0]
    copies = []
    for kind in range(2):
        start = half_start(kind, z)
        low = kind * PART
        pieces = (
            (src.at[0, pl.ds(low, PART)], hist.at[pl.ds(start, PART)]),
            (src.at[1, pl.ds(low, HALF - PART)], hist.at[pl.ds(start + PART, HALF - PART)]),
            (src.at[1, pl.ds(low + HALF - PART, CHALF)], cand.at[pl.ds(kind * CHALF, CHALF)]),
        )
        for i, (one, two) in enumerate(pieces):
            copies.append(pltpu.make_async_copy(one, two, sems.at[kind, i]))
    return copies


def backward_kernel(
    q_ref, kv_ref, da_ref, y_ref, du_ref, dq_ref, dkv_ref, y_out, cy_out, du_out, cdu_out,
    q_all, da_all, acc, low_ref, high_ref, tiles, counts, dk_acc, dv_acc, y_sem, du_sem,
):
    copies = ordered(y_ref, y_out, cy_out, y_sem) + ordered(du_ref, du_out, cdu_out, du_sem)
    for copy in copies:
        copy.start()
    z, x, core, base = coords()
    ends, starts, perm = read_meta(q_ref)
    work_list(z, x, core, ends, starts, tiles, counts)
    set_bounds_t(ends, starts, low_ref, high_ref)
    load_rows(q_ref, perm, q_all)
    load_rows(da_ref, perm, da_all)
    acc[...] = jnp.zeros(acc.shape, f32)
    for block in range(BLOCKS):
        start = block * TILE
        dk_acc[...] = jnp.zeros(dk_acc.shape, f32)
        dv_acc[...] = jnp.zeros(dv_acc.shape, f32)

        def step(i, carry):
            picks = group_of(tiles, block, i)
            keys = kv_ref[0, start : start + TILE, :]
            values = kv_ref[1, start : start + TILE, :]
            q = stacked(q_all, picks)
            da = stacked(da_all, picks)
            t = lax.dot_general(keys, q, NT, preferred_element_type=f32) * (0.5 * SCALE)
            dp = lax.dot_general(values, da, NT, preferred_element_type=f32)
            low = jnp.concatenate([low_ref[i] for i in picks], axis=1)[0:1] - start
            high = jnp.concatenate([high_ref[i] for i in picks], axis=1)[0:1] - start
            pos = lax.broadcasted_iota(jnp.int32, t.shape, 0)
            gate = jnp.where((pos >= low) & (pos < high), 1.0 + jnp.tanh(t), 0.0)
            p = t * gate
            ds = (dp * (gate * ((1.0 + t + t) - p))).astype(bf16)
            dk_acc[...] += jnp.dot(ds, q, preferred_element_type=f32)
            dv_acc[...] += jnp.dot(p.astype(bf16), da, preferred_element_type=f32)
            out = lax.dot_general(ds, keys, TN, preferred_element_type=f32)
            for n, pick in enumerate(picks):
                acc[pick] += out[n * HALF : (n + 1) * HALF]
            return carry

        lax.fori_loop(0, counts[block], step, jnp.int32(0))
        dkv_ref[0, start : start + TILE, :] = (dk_acc[...] * (0.5 * SCALE)).astype(bf16)
        dkv_ref[1, start : start + TILE, :] = dv_acc[...].astype(bf16)
    store_rows(acc, perm, dq_ref, 0.5 * SCALE)
    for copy in copies:
        copy.wait()


def middle_kernel(
    a_ref, u_ref, cu_ref, g_ref, cg_ref, w_ref, y_out, du_out, gw_out, da_out,
    a_in, da_pack, gated, up, gates, dgs, g_part, g_send, g_in, g_sum, g_side,
    s_a, r_a, s_d, r_d, s_g, r_g, s_p, r_p,
):
    z, x, core, base = coords()
    greet(column(z, x, core, base) + plane(z, x, core, base))
    batch = z % 2
    head = z // 2

    def send_a(part, step):
        zi = (z + step) % ZN
        return remote(
            a_ref.at[zi, pl.ds(part * PART, PART)], a_in.at[part, head, core],
            s_a.at[part, step], r_a.at[part, head, core], device(base, zi, x, batch),
        )

    def start_a(part):
        for step in (4, 3, 5, 2, 6, 1, 7):
            send_a(part, step).start()

        @pl.when(core == batch)
        def _():
            pltpu.make_async_copy(
                a_ref.at[z, pl.ds(part * PART, PART)],
                a_in.at[part, head, core],
                r_a.at[part, head, core],
            ).start()

        @pl.when(core != batch)
        def _():
            send_a(part, 0).start()

    start_a(0)
    for kind in range(2):
        start = half_start(kind, z)
        low, mid, high = kind * PART, kind * PART + HALF - PART, (kind + 1) * PART
        later = pl.multiple_of(start + PART, 32)
        cands = slice(kind * CHALF, (kind + 1) * CHALF)
        for dst, hist, cand in ((up, g_ref, cg_ref), (gates, u_ref, cu_ref)):
            dst[0, low:high, :] = hist[pl.ds(start, PART), :]
            dst[1, low:mid, :] = hist[pl.ds(later, HALF - PART), :]
            dst[1, mid:high, :] = cand[cands, :]
    for part in range(2):
        dgs[part] = lax.dot_general(up[part], w_ref[...], NT, preferred_element_type=f32)
        if part == 0:
            start_a(1)

    def dest(j):
        h = (z // 2 + j) % HEADS
        return h, 2 * h + core

    def send_d(part, j, kind):
        h, z2 = dest(j)
        return remote(
            da_pack.at[part, h, kind], da_out.at[z, pl.ds(part * PART, PART)],
            s_d.at[part, j, kind], r_d.at[part, z], device(base, z2, x, kind),
        )

    at_home = dest(0)[1] == z
    for part in range(2):
        for h in range(HEADS):
            for kind in range(2):
                landed(a_in.at[part, h, kind], r_a.at[part, h, kind])
        att = jnp.concatenate(
            [a_in[part, h].reshape(2 * PART, DIM) for h in range(HEADS)], axis=1
        ).astype(f32)
        mean = jnp.mean(att, axis=1, keepdims=True)
        centered = att - mean
        var = jnp.mean(centered * centered, axis=1, keepdims=True)
        rstd = lax.rsqrt(var + EPS)
        normed = centered * rstd
        gate = gates[part].astype(f32)
        dg = dgs[part]
        dn = dg * gate
        da = rstd * (
            dn
            - jnp.mean(dn, axis=1, keepdims=True)
            - normed * jnp.mean(dn * normed, axis=1, keepdims=True)
        )
        for h in range(HEADS):
            da_pack[part, h] = (
                da[:, h * DIM : (h + 1) * DIM].astype(bf16).reshape(2, PART, DIM)
            )
        for j in (2, 1, 3):
            for kind in range(2):
                send_d(part, j, kind).start()
        for kind in range(2):
            here = at_home & (core == kind)

            @pl.when(here)
            def _():
                pltpu.make_async_copy(
                    da_pack.at[part, dest(0)[0], kind],
                    da_out.at[z, pl.ds(part * PART, PART)],
                    r_d.at[part, z],
                ).start()

            @pl.when(jnp.logical_not(here))
            def _():
                send_d(part, 0, kind).start()

        gated[part] = (normed * gate).astype(bf16)
        if part == 0:
            for half in range(2):
                g_part[half] = lax.dot_general(
                    gated[0, :, half * SLAB : (half + 1) * SLAB], up[0], TN,
                    preferred_element_type=f32,
                )
        dgs[part] = dg * normed

    def weight_half(owner):
        cols = pl.ds(pl.multiple_of(owner * SLAB, SLAB), SLAB)
        total = lax.dot_general(gated[1, :, cols], up[1], TN, preferred_element_type=f32)
        return (g_part[owner] + total) * (1.0 / 256.0)

    g_send[...] = weight_half(1 - core).astype(bf16)
    beside = remote(g_send, g_in, s_g.at[0], r_g.at[0], device(base, z, x, 1 - core))
    beside.start()
    own = weight_half(core)
    landed(g_in, r_g.at[0])
    g_sum[...] = (own + g_in[...].astype(f32)).astype(bf16)
    spot = spots(x, base)

    def piece(axis, place):
        row = pl.multiple_of(((1 - axis) * SIDE + place) * BAND, BAND)
        return g_sum.at[pl.ds(row, BAND)]

    def send_p(axis, step):
        place = (spot[axis] + step) % SIDE
        return remote(
            piece(axis, place), g_side.at[axis, spot[axis]], s_p.at[axis, step],
            r_p.at[axis, spot[axis]], along(z, core, axis, spot, place),
        )

    for axis in range(2):
        for step in (2, 1, 3):
            send_p(axis, step).start()
        pltpu.make_async_copy(
            piece(axis, spot[axis]), g_side.at[axis, spot[axis]], r_p.at[axis, spot[axis]]
        ).start()
    for part in range(2):
        du_out[part] = dgs[part].astype(bf16)
    for part in range(2):
        y_out[part] = jnp.dot(gated[part], w_ref[...], preferred_element_type=f32).astype(bf16)
    for axis in range(2):
        for place in range(SIDE):
            landed(g_side.at[axis, place], r_p.at[axis, place])
        gw_out[axis] = jnp.sum(g_side[axis].astype(f32), axis=0).astype(bf16)

    for part in range(2):
        for zi in range(ZN):
            landed(da_out.at[zi, pl.ds(part * PART, PART)], r_d.at[part, zi])
        for step in range(1, ZN):
            send_a(part, step).wait_send()

        @pl.when(core != batch)
        def _():
            send_a(part, 0).wait_send()

        for j in range(HEADS):
            for kind in range(2):
                if j:
                    send_d(part, j, kind).wait_send()
                else:

                    @pl.when(jnp.logical_not(at_home & (core == kind)))
                    def _():
                        send_d(part, 0, kind).wait_send()

    beside.wait_send()
    for axis in range(2):
        for step in range(1, SIDE):
            send_p(axis, step).wait_send()


def collect_kernel(
    dq_ref, dkv_ref, gw_ref, q_in, kv_in, g_all,
    beside_in, across_in, sums, g_two, g_slab, g_z, g_mine,
    s_q, r_q, s_s, r_s, s_x, r_x, s_kv, r_kv,
    s_two, r_two, s_z, r_z, s_zz, r_zz, s_five, r_five, s_six, r_six, s_b, r_b,
):
    z, x, core, base = coords()
    greet(column(z, x, core, base) + plane(z, x, core, base))
    batch = z % 2
    head = z // 2
    order = (4, 3, 5, 2, 6, 1, 7, 0)
    spot = spots(x, base)

    def block(axis, rows, slab):
        return g_all.at[core, 1 - axis, rows, :, slab]

    def slab_of(place):
        return pl.ds(pl.multiple_of(place * SLAB, SLAB), SLAB)

    def two(axis, step):
        other = 1 - axis
        place = (spot[other] + step) % SIDE
        return remote(
            gw_ref.at[axis, :, slab_of(place)], g_two.at[axis, spot[other]],
            s_two.at[axis, step], r_two.at[axis, spot[other]],
            along(z, core, other, spot, place),
        )

    def z_part(zi):
        return (
            zi // 4,
            pl.ds(pl.multiple_of(zi % 2 * 16, 16), 16),
            pl.ds(pl.multiple_of(zi // 2 % 2 * DIM, DIM), DIM),
        )

    def z_place(zi):
        half, rows, lanes = z_part(zi)
        start = jnp.where(half == 0, spot[1], spot[0]) * SLAB + zi // 2 % 2 * DIM
        band = jnp.where(half == 0, spot[0], spot[1])
        return g_all.at[core, 1 - half, band, rows, pl.ds(pl.multiple_of(start, DIM), DIM)]

    def scatter_z(step):
        zi = (z + step) % ZN
        half, rows, lanes = z_part(zi)
        return remote(
            g_slab.at[half, rows, lanes], g_z.at[z], s_z.at[step], r_z.at[z],
            device(base, zi, x, core),
        )

    def gather_z(step):
        zi = (z + step) % ZN
        return remote(
            g_mine, z_place(z), s_zz.at[step], r_zz.at[z], device(base, zi, x, core)
        )

    def five(axis, step):
        other = 1 - axis
        here = block(axis, spot[axis], slab_of(spot[other]))
        return remote(
            here, here, s_five.at[axis, step], r_five.at[axis, spot[other]],
            along(z, core, other, spot, (spot[other] + step) % SIDE),
        )

    def six(axis, step):
        here = g_all.at[core, 1 - axis, spot[axis]]
        return remote(
            here, here, s_six.at[axis, step], r_six.at[axis, spot[axis]],
            along(z, core, axis, spot, (spot[axis] + step) % SIDE),
        )

    def gather_b(axis, place):
        here = g_all.at[core, 1 - axis, place]
        return remote(
            here, here, s_b.at[axis, place], r_b.at[axis, place],
            device(base, z, x, 1 - core),
        )

    def stage(number):
        if number == 0:
            for axis in range(2):
                for step in (2, 1, 3):
                    two(axis, step).start()
                mine = spot[1 - axis]
                pltpu.make_async_copy(
                    gw_ref.at[axis, :, slab_of(mine)], g_two.at[axis, mine],
                    r_two.at[axis, mine],
                ).start()
        if number == 1:
            for axis in range(2):
                for place in range(SIDE):
                    landed(g_two.at[axis, place], r_two.at[axis, place])
                g_slab[axis] = jnp.sum(g_two[axis].astype(f32), axis=0).astype(bf16)
            for step in (4, 3, 5, 2, 6, 1, 7):
                scatter_z(step).start()
            half, rows, lanes = z_part(z)
            pltpu.make_async_copy(g_slab.at[half, rows, lanes], g_z.at[z], r_z.at[z]).start()
        if number == 2:
            for zi in range(ZN):
                landed(g_z.at[zi], r_z.at[zi])
            g_mine[...] = jnp.sum(g_z[...].astype(f32), axis=0).astype(bf16)
            for step in (4, 3, 5, 2, 6, 1, 7):
                gather_z(step).start()
            pltpu.make_async_copy(g_mine, z_place(z), r_zz.at[z]).start()
        if number == 3:
            for zi in range(ZN):
                landed(z_place(zi), r_zz.at[zi])
            for axis in range(2):
                for step in (2, 1, 3):
                    five(axis, step).start()
        if number == 4:
            for axis in range(2):
                other = 1 - axis
                for step in range(1, SIDE):
                    place = (spot[other] + step) % SIDE
                    landed(block(axis, spot[axis], slab_of(place)), r_five.at[axis, place])
                for step in (2, 1, 3):
                    six(axis, step).start()
                gather_b(axis, spot[axis]).start()
        if number == 5:
            for axis in range(2):
                for step in (1, 3, 2):
                    place = (spot[axis] + step) % SIDE
                    landed(g_all.at[core, 1 - axis, place], r_six.at[axis, place])
                    gather_b(axis, place).start()

    def shard(step, side):
        return 2 * ((z + step) % ZN) + side

    def beside(step, side):
        s = shard(step, side)
        return remote(
            dkv_ref.at[1 - core, s], beside_in.at[s], s_s.at[s], r_s.at[s],
            device(base, z, x, 1 - core),
        )

    def across(step):
        zi = (z + step) % ZN
        return remote(
            sums.at[2 * zi + 1 - x], across_in.at[zi], s_x.at[zi], r_x.at[zi],
            device(base, z, 1 - x, core),
        )

    def q_parts(step):
        zi = (z + step) % ZN
        return dq_ref.at[zi], q_in.at[head, core], s_q.at[step], r_q.at[head, core]

    def kv_parts(step):
        zi = (z + step) % ZN
        return sums.at[2 * zi + x], kv_in.at[head, core], s_kv.at[step], r_kv.at[head, core]

    def home(step, parts):
        src, dst, send, recv = parts(step)
        where = device(base, (z + step) % ZN, x, batch)
        if step:
            remote(src, dst, send, recv, where).start()
            return

        @pl.when(core == batch)
        def _():
            pltpu.make_async_copy(src, dst, recv).start()

        @pl.when(core != batch)
        def _():
            remote(src, dst, send, recv, where).start()

    stage(0)
    for step in order:
        beside(step, 1 - x).start()
    for step in order:
        beside(step, x).start()
    for step in order:
        home(step, q_parts)

    def add_beside(step, side):
        s = shard(step, side)
        landed(beside_in.at[s], r_s.at[s])
        return dkv_ref[core, s].astype(f32) + beside_in[s].astype(f32)

    def finish(step):
        zi = (z + step) % ZN
        total = add_beside(step, x)
        landed(across_in.at[zi], r_x.at[zi])
        sums[2 * zi + x] = (total + across_in[zi].astype(f32)).astype(bf16)
        home(step, kv_parts)

    def cross(i):
        step = order[i]
        sums[shard(step, 1 - x)] = add_beside(step, 1 - x).astype(bf16)
        across(step).start()

    cross(0)
    cross(1)
    for i, step in enumerate(order):
        if i in STAGES:
            stage(STAGES[i])
        across(step).wait_send()
        if i + 2 < ZN:
            cross(i + 2)
        finish(step)

    stage(5)
    for kind in range(2):
        for h in range(HEADS):
            landed(q_in.at[h, kind], r_q.at[h, kind])
            landed(kv_in.at[h, kind], r_kv.at[h, kind])
    for axis in range(2):
        for place in range(SIDE):
            landed(g_all.at[1 - core, 1 - axis, place], r_b.at[axis, place])

    for step in range(1, ZN):
        scatter_z(step).wait_send()
        gather_z(step).wait_send()
    for axis in range(2):
        for step in range(1, SIDE):
            two(axis, step).wait_send()
            five(axis, step).wait_send()
            six(axis, step).wait_send()
        for place in range(SIDE):
            gather_b(axis, place).wait_send()
    for step in order:
        beside(step, x).wait_send()
        beside(step, 1 - x).wait_send()
        for parts in (q_parts, kv_parts):
            src, dst, send, recv = parts(step)
            where = device(base, (z + step) % ZN, x, batch)
            if step:
                remote(src, dst, send, recv, where).wait_send()
            else:

                @pl.when(core != batch)
                def _():
                    remote(src, dst, send, recv, where).wait_send()


def finish_kernel(q_in, kv_in, g_all, q_out, c_out, k_out, v_out, g_out, sems):
    z = coords()[0]
    copies = [(g_all, g_out)]
    for h in range(HEADS):
        cols = slice(h * DIM, (h + 1) * DIM)
        copies.append((kv_in.at[h, 0], k_out.at[:, cols]))
        copies.append((kv_in.at[h, 1], v_out.at[:, cols]))
        for kind in range(2):
            start = half_start(kind, z)
            copies.append((q_in.at[h, kind, 0:HALF], q_out.at[pl.ds(start, HALF), cols]))
            copies.append(
                (
                    q_in.at[h, kind, HALF:ROWS],
                    c_out.at[kind * CHALF : (kind + 1) * CHALF, cols],
                )
            )
    started = [
        pltpu.make_async_copy(src, dst, sems.at[i]) for i, (src, dst) in enumerate(copies)
    ]
    for copy in started:
        copy.start()
    for copy in started:
        copy.wait()


VM = pl.BlockSpec(memory_space=pltpu.VMEM)
HB = pl.BlockSpec(memory_space=pltpu.HBM)
DMA = pltpu.SemaphoreType.DMA


def shape(*dims, dtype=bf16):
    return jax.ShapeDtypeStruct(dims, dtype)


def params(collective=None, mib=40):
    if collective is None:
        return pltpu.CompilerParams(vmem_limit_bytes=mib << 20)
    return pltpu.CompilerParams(
        vmem_limit_bytes=mib << 20, collective_id=collective, has_side_effects=True
    )


def local(
    q_hist, k_hist, v_hist, u_hist, cand_q, cand_u, lengths, cand_user, w_out, grad_hist, grad_cand
):
    packs, kv = pl.pallas_call(
        spread_kernel,
        out_shape=(shape(ZN, PACK, DIM), shape(2, 2 * ZN, TOK, DIM)),
        in_specs=[HB] * 6,
        out_specs=(VM, VM),
        scratch_shapes=[
            pltpu.VMEM((TOK, WIDTH), bf16),
            pltpu.VMEM((TOK, WIDTH), bf16),
            pltpu.VMEM((TOK, WIDTH), bf16),
            pltpu.VMEM((CAND, WIDTH), bf16),
            pltpu.VMEM((1, CAND), jnp.int32),
            pltpu.SMEM((1, 4), jnp.int32),
            DMA((6,)),
            pltpu.VMEM((HEADS, 2, PACK, DIM), bf16),
            DMA((HEADS, 2)),
            DMA((ZN,)),
            DMA((HEADS, 2)),
            DMA((ZN,)),
            DMA((ZN,)),
            DMA((ZN,)),
            DMA((2 * ZN,)),
            DMA((2 * ZN,)),
        ],
        compiler_params=params(0),
        name="spread",
    )(*[
        pltpu.with_memory_space_constraint(a, pltpu.HBM)
        for a in (q_hist[0], k_hist[0], v_hist[0], cand_q[0], cand_user, lengths)
    ])
    kv = kv.reshape(2, KEYS, DIM)
    att = pl.pallas_call(
        forward_kernel,
        out_shape=shape(ZN, ROWS, DIM),
        in_specs=[VM] * 2,
        out_specs=VM,
        scratch_shapes=[
            pltpu.VMEM((NTILE + 1, HALF, DIM), bf16),
            pltpu.VMEM((NTILE + 1, HALF, DIM), f32),
            pltpu.VMEM((NTILE + 1, HALF, DIM), jnp.int32),
            pltpu.VMEM((NTILE + 1, HALF, DIM), jnp.int32),
            pltpu.SMEM((ROOM,), jnp.int32),
            pltpu.SMEM((BLOCKS,), jnp.int32),
        ],
        compiler_params=params(),
        name="forward",
    )(packs, kv)
    y, du, gw, datt = pl.pallas_call(
        middle_kernel,
        out_shape=(
            shape(2, 2 * PART, MODEL),
            shape(2, 2 * PART, WIDTH),
            shape(2, BAND, MODEL),
            shape(ZN, ROWS, DIM),
        ),
        in_specs=[VM] * 6,
        out_specs=(VM,) * 4,
        scratch_shapes=[
            pltpu.VMEM((2, HEADS, 2, PART, DIM), bf16),
            pltpu.VMEM((2, HEADS, 2, PART, DIM), bf16),
            pltpu.VMEM((2, 2 * PART, WIDTH), bf16),
            pltpu.VMEM((2, 2 * PART, MODEL), bf16),
            pltpu.VMEM((2, 2 * PART, WIDTH), bf16),
            pltpu.VMEM((2, 2 * PART, WIDTH), f32),
            pltpu.VMEM((2, SLAB, MODEL), f32),
            pltpu.VMEM((SLAB, MODEL), bf16),
            pltpu.VMEM((SLAB, MODEL), bf16),
            pltpu.VMEM((SLAB, MODEL), bf16),
            pltpu.VMEM((2, SIDE, BAND, MODEL), bf16),
            DMA((2, ZN)),
            DMA((2, HEADS, 2)),
            DMA((2, HEADS, 2)),
            DMA((2, ZN)),
            DMA((1,)),
            DMA((1,)),
            DMA((2, SIDE)),
            DMA((2, SIDE)),
        ],
        compiler_params=params(1),
        name="middle",
    )(att, u_hist[0], cand_u[0], grad_hist[0], grad_cand[0], w_out)
    dq, dkv, y_hist, y_cand, du_hist, du_cand = pl.pallas_call(
        backward_kernel,
        out_shape=(
            shape(ZN, ROWS, DIM),
            shape(2, KEYS, DIM),
            shape(TOK, MODEL),
            shape(CAND, MODEL),
            shape(TOK, WIDTH),
            shape(CAND, WIDTH),
        ),
        in_specs=[VM] * 5,
        out_specs=(VM, VM, HB, HB, HB, HB),
        scratch_shapes=[
            pltpu.VMEM((NTILE + 1, HALF, DIM), bf16),
            pltpu.VMEM((NTILE + 1, HALF, DIM), bf16),
            pltpu.VMEM((NTILE + 1, HALF, DIM), f32),
            pltpu.VMEM((NTILE + 1, 8, HALF), jnp.int32),
            pltpu.VMEM((NTILE + 1, 8, HALF), jnp.int32),
            pltpu.SMEM((ROOM,), jnp.int32),
            pltpu.SMEM((BLOCKS,), jnp.int32),
            pltpu.VMEM((TILE, DIM), f32),
            pltpu.VMEM((TILE, DIM), f32),
            DMA((2, 3)),
            DMA((2, 3)),
        ],
        compiler_params=params(),
        name="backward",
    )(packs, kv, datt, y, du)
    q_in, kv_in, g_all = pl.pallas_call(
        collect_kernel,
        out_shape=(
            shape(HEADS, 2, ROWS, DIM),
            shape(HEADS, 2, TOK, DIM),
            shape(2, 2, SIDE, BAND, MODEL),
        ),
        in_specs=[VM] * 3,
        out_specs=(VM,) * 3,
        scratch_shapes=[
            pltpu.VMEM((2 * ZN, TOK, DIM), bf16),
            pltpu.VMEM((ZN, TOK, DIM), bf16),
            pltpu.VMEM((2 * ZN, TOK, DIM), bf16),
            pltpu.VMEM((2, SIDE, BAND, SLAB), bf16),
            pltpu.VMEM((2, BAND, SLAB), bf16),
            pltpu.VMEM((ZN, 16, DIM), bf16),
            pltpu.VMEM((16, DIM), bf16),
            DMA((ZN,)),
            DMA((HEADS, 2)),
            DMA((2 * ZN,)),
            DMA((2 * ZN,)),
            DMA((ZN,)),
            DMA((ZN,)),
            DMA((ZN,)),
            DMA((HEADS, 2)),
            DMA((2, SIDE)),
            DMA((2, SIDE)),
            DMA((ZN,)),
            DMA((ZN,)),
            DMA((ZN,)),
            DMA((ZN,)),
            DMA((2, SIDE)),
            DMA((2, SIDE)),
            DMA((2, SIDE)),
            DMA((2, SIDE)),
            DMA((2, SIDE)),
            DMA((2, SIDE)),
        ],
        compiler_params=params(2),
        name="collect",
    )(dq, dkv.reshape(2, 2 * ZN, TOK, DIM), gw)
    gq, gcq, gk, gv, g_out = pl.pallas_call(
        finish_kernel,
        out_shape=(
            shape(TOK, WIDTH),
            shape(CAND, WIDTH),
            shape(TOK, WIDTH),
            shape(TOK, WIDTH),
            shape(WIDTH, MODEL),
        ),
        in_specs=[VM] * 3,
        out_specs=(HB,) * 5,
        scratch_shapes=[DMA((1 + 6 * HEADS,))],
        compiler_params=params(),
        name="finish",
    )(q_in, kv_in, g_all.reshape(WIDTH, MODEL))
    return (
        y_hist[None], y_cand[None], gq[None], gk[None], gv[None], du_hist[None], gcq[None],
        du_cand[None], g_out,
    )


def solution(mesh):
    rows = P("dp", "ctx", None)
    return jax.shard_map(
        local,
        mesh=mesh,
        in_specs=(rows, rows, rows, rows, rows, rows, P("dp", None), P("dp", "ctx"), P(), rows, rows),
        out_specs=(rows, rows, rows, rows, rows, rows, rows, rows, P()),
        check_vma=False,
    )
```

```python
import functools
import math

import jax
import jax.numpy as jnp
from jax import lax
from jax.experimental import pallas as pl
from jax.experimental.pallas import tpu as pltpu
from jax.sharding import PartitionSpec as P

HEADS = 4
DIM = 128
EPS = 1e-05
ZN = 8
SIDE = 4
BAND = 32
SLAB = 256
PART = 64
TOK = 192
CAND = 64
HALF = TOK // 2
CHALF = CAND // 2
ROWS = HALF + CHALF
META = 16
PACK = ROWS + META
KEYS = 3072
WIDTH = HEADS * DIM
MODEL = 1024
CANDS = ZN * CHALF
SCALE = 1.0 / math.sqrt(DIM)
ORDER = (0, 1, 7, 2, 6, 3, 5, 4)
TILE = 768
GROUP = 4
NTILE = 11
BLOCKS = KEYS // TILE
ROOM = BLOCKS * (NTILE + GROUP)
STAGES = {0: 1, 1: 2, 3: 3, 5: 4}
MESH = pl.DeviceIdType.MESH
bf16 = jnp.bfloat16
f32 = jnp.float32


def coords():
    ctx, dp = lax.axis_index("ctx"), lax.axis_index("dp")
    core = dp % 2
    return ctx // 2, ctx % 2, core, dp - core


def device(base, z, x, core):
    return {"ctx": z * 2 + x, "dp": base + core}


def column(z, x, core, base):
    return [
        device(base, (z + step) % ZN, x, (core + other) % 2)
        for step in range(ZN)
        for other in range(2)
        if step or other
    ]


def spots(x, base):
    return base // 8 * 2 + x, base % 8 // 2


def along(z, core, axis, spot, place):
    wide, high = (place, spot[1]) if axis == 0 else (spot[0], place)
    return {"ctx": z * 2 + wide % 2, "dp": wide // 2 * 8 + high * 2 + core}


def plane(z, x, core, base):
    spot = spots(x, base)
    return [
        along(z, core, axis, spot, (spot[axis] + step) % SIDE)
        for axis in range(2)
        for step in range(1, SIDE)
    ]


def greet(others):
    barrier = pltpu.get_barrier_semaphore()
    for other in others:
        pl.semaphore_signal(barrier, inc=1, device_id=other, device_id_type=MESH)
    pl.semaphore_wait(barrier, len(others))


def landed(ref, sem):
    pltpu.make_async_copy(ref, ref, sem).wait()


def remote(src, dst, send, recv, where):
    return pltpu.make_async_remote_copy(
        src_ref=src,
        dst_ref=dst,
        send_sem=send,
        recv_sem=recv,
        device_id=where,
        device_id_type=MESH,
    )


def half_start(core, z):
    return pl.multiple_of(((core + z) % 2) * HALF, HALF)


def spread_kernel(
    q_hbm, k_hbm, v_hbm, c_hbm, user_hbm, len_hbm, q_out, kv_out,
    q_ref, kv_ref, c_ref, user_ref, len_ref, l_sem, pack, s_q, r_q, s_kv, r_kv, s_x, r_x, s_s, r_s,
):
    z, x, core, base = coords()
    fetches = [
        pltpu.make_async_copy(src, dst, l_sem.at[i])
        for i, (src, dst) in enumerate(
            [
                (src.at[:, h * DIM : (h + 1) * DIM], kv_ref.at[kind, h])
                for h in range(HEADS)
                for kind, src in ((0, k_hbm), (1, v_hbm))
            ]
            + [
                (q_hbm, q_ref),
                (c_hbm, c_ref),
                (user_hbm, user_ref),
                (len_hbm, len_ref),
            ]
        )
    ]
    for fetch in fetches:
        fetch.start()
    greet(column(z, x, core, base) + [device(base, z, 1 - x, core)])
    own = 2 * z + x
    turn = jnp.where(z % 2 > core, 1, 3)
    turns = (0, turn, 4 - turn, 2)
    dests = []
    for j in range(HEADS):
        h = (z // 2 + turns[j]) % HEADS
        dests.append((h, 2 * h + core))
    at_home = dests[0][1] == z

    def kv_source(j, kind):
        return kv_ref.at[kind, dests[j][0]]

    def send_kv(j, kind):
        return remote(
            kv_source(j, kind), kv_out.at[kind, own], s_kv.at[j, kind], r_kv.at[z],
            device(base, dests[j][1], x, kind),
        )

    def send_q(j, kind):
        return remote(
            pack.at[dests[j][0], kind], q_out.at[z], s_q.at[j, kind], r_q.at[z],
            device(base, dests[j][1], x, kind),
        )

    for fetch in fetches[: 2 * HEADS]:
        fetch.wait()
    def start_all(j, send, local_pair):
        for kind in range(2):
            if j:
                send(j, kind).start()
            else:
                here = at_home & (core == kind)

                @pl.when(here)
                def _():
                    pltpu.make_async_copy(*local_pair(kind)).start()

                @pl.when(jnp.logical_not(here))
                def _():
                    send(j, kind).start()

    def sent(j, send):
        for kind in range(2):
            if j:
                send(j, kind).wait_send()
            else:

                @pl.when(jnp.logical_not(at_home & (core == kind)))
                def _():
                    send(j, kind).wait_send()

    def start_kv(j):
        start_all(j, send_kv, lambda kind: (kv_source(0, kind), kv_out.at[kind, own], r_kv.at[z]))

    def start_q(j):
        start_all(j, send_q, lambda kind: (pack.at[dests[0][0], kind], q_out.at[z], r_q.at[z]))

    for j in range(HEADS):
        start_kv(j)
    for fetch in fetches[2 * HEADS :]:
        fetch.wait()
    lane = lax.broadcasted_iota(jnp.int32, (META, DIM), 1)
    row = lax.broadcasted_iota(jnp.int32, (META, DIM), 0)
    lens = jnp.zeros((META, DIM), jnp.int32)
    for i in range(4):
        lens = jnp.where(lane == i, len_ref[0, i], lens)
    lens_f = lens.astype(f32)
    high = jnp.floor(lens_f * (1.0 / 64.0))
    low = lens_f - high * 64.0
    users = jnp.broadcast_to(user_ref[...].astype(f32), (META, CAND)).astype(bf16)
    sel_j = lax.broadcasted_iota(jnp.int32, (CAND, DIM), 0)
    sel_l = lax.broadcasted_iota(jnp.int32, (CAND, DIM), 1)
    spot = CHALF * (z % 4)
    for kind in range(2):
        start = half_start(kind, z)
        pick = (
            (sel_l - spot + CHALF * kind == sel_j) & (sel_l >= spot) & (sel_l < spot + CHALF)
        ).astype(f32)
        placed = jnp.dot(users, pick.astype(bf16), preferred_element_type=f32)
        meta = jnp.where(row == 0, placed, jnp.where(row == 1, high, low)).astype(bf16)
        for h in range(HEADS):
            cols = slice(h * DIM, (h + 1) * DIM)
            pack[h, kind, 0:HALF, :] = q_ref[pl.ds(start, HALF), cols]
            pack[h, kind, HALF:ROWS, :] = c_ref[kind * CHALF : (kind + 1) * CHALF, cols]
            pack[h, kind, ROWS:PACK, :] = meta
    def across(s, zi):
        slot = kv_out.at[core, s]
        return remote(slot, slot, s_x.at[zi], r_x.at[zi], device(base, z, 1 - x, core))

    def beside(s):
        slot = kv_out.at[core, s]
        return remote(slot, slot, s_s.at[s], r_s.at[s], device(base, z, x, 1 - core))

    def pass_on(step):
        zi = (z + ORDER[step]) % ZN
        s = 2 * zi + (1 - x)
        landed(kv_out.at[core, s], r_x.at[zi])
        beside(s).start()

    for step in range(ZN):
        zi = (z + ORDER[step]) % ZN
        s = 2 * zi + x
        landed(kv_out.at[core, s], r_kv.at[zi])
        across(s, zi).start()
        beside(s).start()
        if step == 0:
            sent(0, send_kv)
        if step == 2:
            sent(1, send_kv)
        if step == 4:
            sent(2, send_kv)
            start_q(0)
            start_q(1)
        if step == 6:
            sent(3, send_kv)
            start_q(2)
            start_q(3)
        if step >= 2:
            pass_on(step - 2)
    pass_on(ZN - 2)
    pass_on(ZN - 1)
    for zi in range(ZN):
        landed(q_out.at[zi], r_q.at[zi])
    for s in range(2 * ZN):
        landed(kv_out.at[1 - core, s], r_s.at[s])
    for s in range(2 * ZN):
        beside(s).wait_send()
    for zi in range(ZN):
        across(2 * zi + x, zi).wait_send()
    for j in range(HEADS):
        sent(j, send_q)


def read_meta(q_ref):
    first = sum(q_ref[zi, ROWS:PACK, :].astype(f32) for zi in range(4))[0:1]
    second = sum(q_ref[zi, ROWS:PACK, :].astype(f32) for zi in range(4, 8))[0:1]
    users = jnp.concatenate([first, second], axis=1)
    block = q_ref[0, ROWS:PACK, :].astype(f32)
    lens = block[1:2] * 64.0 + block[2:3]
    lane = lax.broadcasted_iota(jnp.int32, (1, DIM), 1)
    ends = []
    for i in range(3):
        ends.append(jnp.sum(jnp.where(lane <= i, lens, 0.0)).astype(jnp.int32))
    starts = [jnp.sum((users < float(i)).astype(f32)).astype(jnp.int32) for i in range(1, 4)]
    sub = lax.broadcasted_iota(jnp.int32, (8, CANDS), 0).astype(f32)
    hot = (users == sub).astype(f32)
    before = jnp.sum((users < sub).astype(f32), axis=1, keepdims=True)
    rows = lax.broadcasted_iota(jnp.int32, (CANDS, CANDS), 0)
    cols = lax.broadcasted_iota(jnp.int32, (CANDS, CANDS), 1)
    upper = (rows < cols).astype(f32).astype(bf16)
    prior = jnp.dot(hot.astype(bf16), upper, preferred_element_type=f32)
    rank = jnp.sum(hot * (prior + before), axis=0, keepdims=True).astype(jnp.int32)
    perm = (rows == rank).astype(f32).astype(bf16)
    return ends, starts, perm


def first_of(ends, pos):
    low = jnp.where(pos >= ends[0], ends[0], 0)
    low = jnp.where(pos >= ends[1], ends[1], low)
    return jnp.where(pos >= ends[2], ends[2], low)


def cand_range(ends, starts, row):
    low = jnp.where(row >= starts[0], ends[0], 0)
    low = jnp.where(row >= starts[1], ends[1], low)
    low = jnp.where(row >= starts[2], ends[2], low)
    high = jnp.where(row >= starts[0], ends[1], ends[0])
    high = jnp.where(row >= starts[1], ends[2], high)
    high = jnp.where(row >= starts[2], KEYS, high)
    return low, high


def hist_start(zi):
    z, x, core, base = coords()
    return (2 * zi + x) * TOK + ((core + zi) % 2) * HALF


NT = (((1,), (1,)), ((), ()))
TN = (((0,), (0,)), ((), ()))


def work_list(z, x, core, ends, starts, tiles, counts):
    ranges = []
    for zi in range(ZN):
        p0 = hist_start(zi)
        ranges.append((first_of(ends, p0), p0 + HALF))
    for c in range(NTILE - ZN):
        first, last = c * HALF, min((c + 1) * HALF, CANDS) - 1
        ranges.append((cand_range(ends, starts, first)[0], cand_range(ends, starts, last)[1]))
    for block in range(BLOCKS):
        at = block * (NTILE + GROUP)
        used = jnp.int32(0)
        for i, (low, high) in enumerate(ranges):
            hit = (low < (block + 1) * TILE) & (high > block * TILE)
            tiles[at + used] = jnp.int32(i)
            used = used + hit.astype(jnp.int32)
        for i in range(GROUP - 1):
            tiles[at + used + i] = jnp.int32(NTILE)
        counts[block] = used


def set_bounds(ends, starts, low_ref, high_ref):
    lane = lax.broadcasted_iota(jnp.int32, (HALF, DIM), 1)
    row = lax.broadcasted_iota(jnp.int32, (HALF, DIM), 0)
    for zi in range(ZN):
        pos = hist_start(zi) + row
        low_ref[zi] = first_of(ends, pos) - lane
        high_ref[zi] = pos + 1 - lane
    for c in range(NTILE - ZN):
        low, high = cand_range(ends, starts, c * HALF + row)
        low_ref[ZN + c] = low - lane
        high_ref[ZN + c] = jnp.where(c * HALF + row < CANDS, high, 0) - lane
    low_ref[NTILE] = jnp.zeros((HALF, DIM), jnp.int32)
    high_ref[NTILE] = jnp.full((HALF, DIM), -KEYS, jnp.int32)


def set_bounds_t(ends, starts, low_ref, high_ref):
    lane = lax.broadcasted_iota(jnp.int32, (8, HALF), 1)
    for zi in range(ZN):
        pos = hist_start(zi) + lane
        low_ref[zi] = first_of(ends, pos)
        high_ref[zi] = pos + 1
    for c in range(NTILE - ZN):
        low, high = cand_range(ends, starts, c * HALF + lane)
        low_ref[ZN + c] = low
        high_ref[ZN + c] = jnp.where(c * HALF + lane < CANDS, high, 0)
    low_ref[NTILE] = jnp.zeros((8, HALF), jnp.int32)
    high_ref[NTILE] = jnp.full((8, HALF), -KEYS, jnp.int32)


def inside(low, high, start):
    masks = []
    for i in range(TILE // DIM):
        at = start + i * DIM
        masks.append((low <= at) & (high > at))
    return jnp.concatenate(masks, axis=1)


def load_rows(src, perm, dst):
    for zi in range(ZN):
        dst[zi] = src[zi, 0:HALF, :]
    cand = jnp.concatenate([src[zi, HALF:ROWS, :] for zi in range(ZN)], axis=0)
    cand = jnp.dot(perm, cand, preferred_element_type=f32).astype(bf16)
    dst[ZN] = cand[0:HALF]
    dst[ZN + 1] = cand[HALF : 2 * HALF]
    dst[ZN + 2, 0 : CANDS - 2 * HALF, :] = cand[2 * HALF :]
    dst[ZN + 2, CANDS - 2 * HALF :, :] = jnp.zeros((3 * HALF - CANDS, DIM), bf16)
    dst[NTILE] = jnp.zeros((HALF, DIM), bf16)


def store_rows(acc, perm, dst, factor):
    for zi in range(ZN):
        dst[zi, 0:HALF, :] = (acc[zi] * factor).astype(bf16)
    cand = jnp.concatenate([acc[ZN], acc[ZN + 1], acc[ZN + 2, 0 : CANDS - 2 * HALF, :]], axis=0)
    back = lax.dot_general(
        perm, (cand * factor).astype(bf16), TN, preferred_element_type=f32
    ).astype(bf16)
    for zi in range(ZN):
        dst[zi, HALF:ROWS, :] = back[zi * CHALF : (zi + 1) * CHALF]


def for_groups(tiles, counts, block, body):
    at = block * (NTILE + GROUP)
    used = counts[block]
    whole = used // GROUP
    rest = used - whole * GROUP

    def step(i, carry):
        body([tiles[at + i * GROUP + n] for n in range(GROUP)])
        return carry

    lax.fori_loop(0, whole, step, jnp.int32(0))

    @pl.when((rest > 0) & (rest <= GROUP // 2))
    def _():
        body([tiles[at + whole * GROUP + n] for n in range(GROUP // 2)])

    @pl.when(rest > GROUP // 2)
    def _():
        body([tiles[at + whole * GROUP + n] for n in range(GROUP)])


def stacked(ref, picks):
    return jnp.concatenate([ref[i] for i in picks], axis=0)


def forward_kernel(q_ref, kv_ref, a_ref, q_all, acc, low_ref, high_ref, tiles, counts):
    z, x, core, base = coords()
    ends, starts, perm = read_meta(q_ref)
    work_list(z, x, core, ends, starts, tiles, counts)
    set_bounds(ends, starts, low_ref, high_ref)
    load_rows(q_ref, perm, q_all)
    acc[...] = jnp.zeros(acc.shape, f32)
    for block in range(BLOCKS):
        start = block * TILE

        def body(picks):
            keys = kv_ref[0, start : start + TILE, :]
            values = kv_ref[1, start : start + TILE, :]
            q = stacked(q_all, picks)
            t = lax.dot_general(q, keys, NT, preferred_element_type=f32) * (0.5 * SCALE)
            ok = inside(stacked(low_ref, picks), stacked(high_ref, picks), start)
            gate = jnp.where(ok, 1.0 + jnp.tanh(t), 0.0)
            out = jnp.dot((t * gate).astype(bf16), values, preferred_element_type=f32)
            for n, pick in enumerate(picks):
                acc[pick] += out[n * HALF : (n + 1) * HALF]

        for_groups(tiles, counts, block, body)
    store_rows(acc, perm, a_ref, 1.0)


def ordered(src, hist, cand, sems):
    z = coords()[0]
    copies = []
    for kind in range(2):
        start = half_start(kind, z)
        low = kind * PART
        pieces = (
            (src.at[0, pl.ds(low, PART)], hist.at[pl.ds(start, PART)]),
            (src.at[1, pl.ds(low, HALF - PART)], hist.at[pl.ds(start + PART, HALF - PART)]),
            (src.at[1, pl.ds(low + HALF - PART, CHALF)], cand.at[pl.ds(kind * CHALF, CHALF)]),
        )
        for i, (one, two) in enumerate(pieces):
            copies.append(pltpu.make_async_copy(one, two, sems.at[kind, i]))
    return copies


def backward_kernel(
    q_ref, kv_ref, da_ref, y_ref, du_ref, dq_ref, dkv_ref, y_out, cy_out, du_out, cdu_out,
    q_all, da_all, acc, low_ref, high_ref, tiles, counts, dk_acc, dv_acc, y_sem, du_sem,
):
    copies = ordered(y_ref, y_out, cy_out, y_sem) + ordered(du_ref, du_out, cdu_out, du_sem)
    for copy in copies:
        copy.start()
    z, x, core, base = coords()
    ends, starts, perm = read_meta(q_ref)
    work_list(z, x, core, ends, starts, tiles, counts)
    set_bounds_t(ends, starts, low_ref, high_ref)
    load_rows(q_ref, perm, q_all)
    load_rows(da_ref, perm, da_all)
    acc[...] = jnp.zeros(acc.shape, f32)
    for block in range(BLOCKS):
        start = block * TILE
        dk_acc[...] = jnp.zeros(dk_acc.shape, f32)
        dv_acc[...] = jnp.zeros(dv_acc.shape, f32)

        def body(picks):
            keys = kv_ref[0, start : start + TILE, :]
            values = kv_ref[1, start : start + TILE, :]
            q = stacked(q_all, picks)
            da = stacked(da_all, picks)
            t = lax.dot_general(keys, q, NT, preferred_element_type=f32) * (0.5 * SCALE)
            dp = lax.dot_general(values, da, NT, preferred_element_type=f32)
            low = jnp.concatenate([low_ref[i] for i in picks], axis=1)[0:1] - start
            high = jnp.concatenate([high_ref[i] for i in picks], axis=1)[0:1] - start
            pos = lax.broadcasted_iota(jnp.int32, t.shape, 0)
            gate = jnp.where((pos >= low) & (pos < high), 1.0 + jnp.tanh(t), 0.0)
            p = t * gate
            ds = (dp * (gate * ((1.0 + t + t) - p))).astype(bf16)
            dk_acc[...] += jnp.dot(ds, q, preferred_element_type=f32)
            dv_acc[...] += jnp.dot(p.astype(bf16), da, preferred_element_type=f32)
            out = lax.dot_general(ds, keys, TN, preferred_element_type=f32)
            for n, pick in enumerate(picks):
                acc[pick] += out[n * HALF : (n + 1) * HALF]

        for_groups(tiles, counts, block, body)
        dkv_ref[0, start : start + TILE, :] = (dk_acc[...] * (0.5 * SCALE)).astype(bf16)
        dkv_ref[1, start : start + TILE, :] = dv_acc[...].astype(bf16)
    store_rows(acc, perm, dq_ref, 0.5 * SCALE)
    for copy in copies:
        copy.wait()


def middle_kernel(
    a_ref, u_ref, cu_ref, g_ref, cg_ref, w_ref, y_out, du_out, gw_out, da_out,
    a_in, da_pack, gated, up, gates, dgs, g_part, g_send, g_in, g_sum, g_side,
    s_a, r_a, s_d, r_d, s_g, r_g, s_p, r_p,
):
    z, x, core, base = coords()
    greet(column(z, x, core, base) + plane(z, x, core, base))
    batch = z % 2
    head = z // 2

    def send_a(part, step):
        zi = (z + step) % ZN
        return remote(
            a_ref.at[zi, pl.ds(part * PART, PART)], a_in.at[part, head, core],
            s_a.at[part, step], r_a.at[part, head, core], device(base, zi, x, batch),
        )

    def start_a(part):
        for step in (4, 3, 5, 2, 6, 1, 7):
            send_a(part, step).start()

        @pl.when(core == batch)
        def _():
            pltpu.make_async_copy(
                a_ref.at[z, pl.ds(part * PART, PART)],
                a_in.at[part, head, core],
                r_a.at[part, head, core],
            ).start()

        @pl.when(core != batch)
        def _():
            send_a(part, 0).start()

    start_a(0)
    for kind in range(2):
        start = half_start(kind, z)
        low, mid, high = kind * PART, kind * PART + HALF - PART, (kind + 1) * PART
        later = pl.multiple_of(start + PART, 32)
        cands = slice(kind * CHALF, (kind + 1) * CHALF)
        for dst, hist, cand in ((up, g_ref, cg_ref), (gates, u_ref, cu_ref)):
            dst[0, low:high, :] = hist[pl.ds(start, PART), :]
            dst[1, low:mid, :] = hist[pl.ds(later, HALF - PART), :]
            dst[1, mid:high, :] = cand[cands, :]
    for part in range(2):
        dgs[part] = lax.dot_general(up[part], w_ref[...], NT, preferred_element_type=f32)
        if part == 0:
            start_a(1)

    def dest(j):
        h = (z // 2 + j) % HEADS
        return h, 2 * h + core

    def send_d(part, j, kind):
        h, z2 = dest(j)
        return remote(
            da_pack.at[part, h, kind], da_out.at[z, pl.ds(part * PART, PART)],
            s_d.at[part, j, kind], r_d.at[part, z], device(base, z2, x, kind),
        )

    at_home = dest(0)[1] == z
    for part in range(2):
        for h in range(HEADS):
            for kind in range(2):
                landed(a_in.at[part, h, kind], r_a.at[part, h, kind])
        att = jnp.concatenate(
            [a_in[part, h].reshape(2 * PART, DIM) for h in range(HEADS)], axis=1
        ).astype(f32)
        mean = jnp.mean(att, axis=1, keepdims=True)
        centered = att - mean
        var = jnp.mean(centered * centered, axis=1, keepdims=True)
        rstd = lax.rsqrt(var + EPS)
        normed = centered * rstd
        gate = gates[part].astype(f32)
        dg = dgs[part]
        dn = dg * gate
        da = rstd * (
            dn
            - jnp.mean(dn, axis=1, keepdims=True)
            - normed * jnp.mean(dn * normed, axis=1, keepdims=True)
        )
        for h in range(HEADS):
            da_pack[part, h] = (
                da[:, h * DIM : (h + 1) * DIM].astype(bf16).reshape(2, PART, DIM)
            )
        for j in (2, 1, 3):
            for kind in range(2):
                send_d(part, j, kind).start()
        for kind in range(2):
            here = at_home & (core == kind)

            @pl.when(here)
            def _():
                pltpu.make_async_copy(
                    da_pack.at[part, dest(0)[0], kind],
                    da_out.at[z, pl.ds(part * PART, PART)],
                    r_d.at[part, z],
                ).start()

            @pl.when(jnp.logical_not(here))
            def _():
                send_d(part, 0, kind).start()

        gated[part] = (normed * gate).astype(bf16)
        if part == 0:
            for half in range(2):
                g_part[half] = lax.dot_general(
                    gated[0, :, half * SLAB : (half + 1) * SLAB], up[0], TN,
                    preferred_element_type=f32,
                )
        dgs[part] = dg * normed

    def weight_half(owner):
        cols = pl.ds(pl.multiple_of(owner * SLAB, SLAB), SLAB)
        total = lax.dot_general(gated[1, :, cols], up[1], TN, preferred_element_type=f32)
        return (g_part[owner] + total) * (1.0 / 256.0)

    g_send[...] = weight_half(1 - core).astype(bf16)
    beside = remote(g_send, g_in, s_g.at[0], r_g.at[0], device(base, z, x, 1 - core))
    beside.start()
    own = weight_half(core)
    landed(g_in, r_g.at[0])
    g_sum[...] = (own + g_in[...].astype(f32)).astype(bf16)
    spot = spots(x, base)

    def piece(axis, place):
        row = pl.multiple_of(((1 - axis) * SIDE + place) * BAND, BAND)
        return g_sum.at[pl.ds(row, BAND)]

    def send_p(axis, step):
        place = (spot[axis] + step) % SIDE
        return remote(
            piece(axis, place), g_side.at[axis, spot[axis]], s_p.at[axis, step],
            r_p.at[axis, spot[axis]], along(z, core, axis, spot, place),
        )

    for axis in range(2):
        for step in (2, 1, 3):
            send_p(axis, step).start()
        pltpu.make_async_copy(
            piece(axis, spot[axis]), g_side.at[axis, spot[axis]], r_p.at[axis, spot[axis]]
        ).start()
    for part in range(2):
        du_out[part] = dgs[part].astype(bf16)
    for part in range(2):
        y_out[part] = jnp.dot(gated[part], w_ref[...], preferred_element_type=f32).astype(bf16)
    for axis in range(2):
        for place in range(SIDE):
            landed(g_side.at[axis, place], r_p.at[axis, place])
        gw_out[axis] = jnp.sum(g_side[axis].astype(f32), axis=0).astype(bf16)

    for part in range(2):
        for zi in range(ZN):
            landed(da_out.at[zi, pl.ds(part * PART, PART)], r_d.at[part, zi])
        for step in range(1, ZN):
            send_a(part, step).wait_send()

        @pl.when(core != batch)
        def _():
            send_a(part, 0).wait_send()

        for j in range(HEADS):
            for kind in range(2):
                if j:
                    send_d(part, j, kind).wait_send()
                else:

                    @pl.when(jnp.logical_not(at_home & (core == kind)))
                    def _():
                        send_d(part, 0, kind).wait_send()

    beside.wait_send()
    for axis in range(2):
        for step in range(1, SIDE):
            send_p(axis, step).wait_send()


def collect_kernel(
    dq_ref, dkv_ref, gw_ref, q_in, kv_in, g_all,
    beside_in, across_in, sums, g_two, g_slab, g_z, g_mine,
    s_q, r_q, s_s, r_s, s_x, r_x, s_kv, r_kv,
    s_two, r_two, s_z, r_z, s_zz, r_zz, s_five, r_five, s_six, r_six, s_b, r_b,
):
    z, x, core, base = coords()
    greet(column(z, x, core, base) + plane(z, x, core, base))
    batch = z % 2
    head = z // 2
    order = (4, 3, 5, 2, 6, 1, 7, 0)
    spot = spots(x, base)

    def block(axis, rows, slab):
        return g_all.at[core, 1 - axis, rows, :, slab]

    def slab_of(place):
        return pl.ds(pl.multiple_of(place * SLAB, SLAB), SLAB)

    def two(axis, step):
        other = 1 - axis
        place = (spot[other] + step) % SIDE
        return remote(
            gw_ref.at[axis, :, slab_of(place)], g_two.at[axis, spot[other]],
            s_two.at[axis, step], r_two.at[axis, spot[other]],
            along(z, core, other, spot, place),
        )

    def z_part(zi):
        return (
            zi // 4,
            pl.ds(pl.multiple_of(zi % 2 * 16, 16), 16),
            pl.ds(pl.multiple_of(zi // 2 % 2 * DIM, DIM), DIM),
        )

    def z_place(zi):
        half, rows, lanes = z_part(zi)
        start = jnp.where(half == 0, spot[1], spot[0]) * SLAB + zi // 2 % 2 * DIM
        band = jnp.where(half == 0, spot[0], spot[1])
        return g_all.at[core, 1 - half, band, rows, pl.ds(pl.multiple_of(start, DIM), DIM)]

    def scatter_z(step):
        zi = (z + step) % ZN
        half, rows, lanes = z_part(zi)
        return remote(
            g_slab.at[half, rows, lanes], g_z.at[z], s_z.at[step], r_z.at[z],
            device(base, zi, x, core),
        )

    def gather_z(step):
        zi = (z + step) % ZN
        return remote(
            g_mine, z_place(z), s_zz.at[step], r_zz.at[z], device(base, zi, x, core)
        )

    def five(axis, step):
        other = 1 - axis
        here = block(axis, spot[axis], slab_of(spot[other]))
        return remote(
            here, here, s_five.at[axis, step], r_five.at[axis, spot[other]],
            along(z, core, other, spot, (spot[other] + step) % SIDE),
        )

    def six(axis, step):
        here = g_all.at[core, 1 - axis, spot[axis]]
        return remote(
            here, here, s_six.at[axis, step], r_six.at[axis, spot[axis]],
            along(z, core, axis, spot, (spot[axis] + step) % SIDE),
        )

    def gather_b(axis, place):
        here = g_all.at[core, 1 - axis, place]
        return remote(
            here, here, s_b.at[axis, place], r_b.at[axis, place],
            device(base, z, x, 1 - core),
        )

    def stage(number):
        if number == 0:
            for axis in range(2):
                for step in (2, 1, 3):
                    two(axis, step).start()
                mine = spot[1 - axis]
                pltpu.make_async_copy(
                    gw_ref.at[axis, :, slab_of(mine)], g_two.at[axis, mine],
                    r_two.at[axis, mine],
                ).start()
        if number == 1:
            for axis in range(2):
                for place in range(SIDE):
                    landed(g_two.at[axis, place], r_two.at[axis, place])
                g_slab[axis] = jnp.sum(g_two[axis].astype(f32), axis=0).astype(bf16)
            for step in (4, 3, 5, 2, 6, 1, 7):
                scatter_z(step).start()
            half, rows, lanes = z_part(z)
            pltpu.make_async_copy(g_slab.at[half, rows, lanes], g_z.at[z], r_z.at[z]).start()
        if number == 2:
            for zi in range(ZN):
                landed(g_z.at[zi], r_z.at[zi])
            g_mine[...] = jnp.sum(g_z[...].astype(f32), axis=0).astype(bf16)
            for step in (4, 3, 5, 2, 6, 1, 7):
                gather_z(step).start()
            pltpu.make_async_copy(g_mine, z_place(z), r_zz.at[z]).start()
        if number == 3:
            for zi in range(ZN):
                landed(z_place(zi), r_zz.at[zi])
            for axis in range(2):
                for step in (2, 1, 3):
                    five(axis, step).start()
        if number == 4:
            for axis in range(2):
                other = 1 - axis
                for step in range(1, SIDE):
                    place = (spot[other] + step) % SIDE
                    landed(block(axis, spot[axis], slab_of(place)), r_five.at[axis, place])
                for step in (2, 1, 3):
                    six(axis, step).start()
                gather_b(axis, spot[axis]).start()
        if number == 5:
            for axis in range(2):
                for step in (1, 3, 2):
                    place = (spot[axis] + step) % SIDE
                    landed(g_all.at[core, 1 - axis, place], r_six.at[axis, place])
                    gather_b(axis, place).start()

    def shard(step, side):
        return 2 * ((z + step) % ZN) + side

    def beside(step, side):
        s = shard(step, side)
        return remote(
            dkv_ref.at[1 - core, s], beside_in.at[s], s_s.at[s], r_s.at[s],
            device(base, z, x, 1 - core),
        )

    def across(step):
        zi = (z + step) % ZN
        return remote(
            sums.at[2 * zi + 1 - x], across_in.at[zi], s_x.at[zi], r_x.at[zi],
            device(base, z, 1 - x, core),
        )

    def q_parts(step):
        zi = (z + step) % ZN
        return dq_ref.at[zi], q_in.at[head, core], s_q.at[step], r_q.at[head, core]

    def kv_parts(step):
        zi = (z + step) % ZN
        return sums.at[2 * zi + x], kv_in.at[head, core], s_kv.at[step], r_kv.at[head, core]

    def home(step, parts):
        src, dst, send, recv = parts(step)
        where = device(base, (z + step) % ZN, x, batch)
        if step:
            remote(src, dst, send, recv, where).start()
            return

        @pl.when(core == batch)
        def _():
            pltpu.make_async_copy(src, dst, recv).start()

        @pl.when(core != batch)
        def _():
            remote(src, dst, send, recv, where).start()

    stage(0)
    for step in order:
        beside(step, 1 - x).start()
    for step in order:
        beside(step, x).start()

    def add_beside(step, side):
        s = shard(step, side)
        landed(beside_in.at[s], r_s.at[s])
        return dkv_ref[core, s].astype(f32) + beside_in[s].astype(f32)

    def finish(step):
        zi = (z + step) % ZN
        total = add_beside(step, x)
        landed(across_in.at[zi], r_x.at[zi])
        sums[2 * zi + x] = (total + across_in[zi].astype(f32)).astype(bf16)
        home(step, kv_parts)

    def cross(i):
        step = order[i]
        sums[shard(step, 1 - x)] = add_beside(step, 1 - x).astype(bf16)
        across(step).start()

    cross(0)
    cross(1)
    for i, step in enumerate(order):
        if i in STAGES:
            stage(STAGES[i])
        if i == 3:
            for far in order:
                home(far, q_parts)
        across(step).wait_send()
        if i + 2 < ZN:
            cross(i + 2)
        finish(step)

    stage(5)
    for kind in range(2):
        for h in range(HEADS):
            landed(q_in.at[h, kind], r_q.at[h, kind])
            landed(kv_in.at[h, kind], r_kv.at[h, kind])
    for axis in range(2):
        for place in range(SIDE):
            landed(g_all.at[1 - core, 1 - axis, place], r_b.at[axis, place])

    for step in range(1, ZN):
        scatter_z(step).wait_send()
        gather_z(step).wait_send()
    for axis in range(2):
        for step in range(1, SIDE):
            two(axis, step).wait_send()
            five(axis, step).wait_send()
            six(axis, step).wait_send()
        for place in range(SIDE):
            gather_b(axis, place).wait_send()
    for step in order:
        beside(step, x).wait_send()
        beside(step, 1 - x).wait_send()
        for parts in (q_parts, kv_parts):
            src, dst, send, recv = parts(step)
            where = device(base, (z + step) % ZN, x, batch)
            if step:
                remote(src, dst, send, recv, where).wait_send()
            else:

                @pl.when(core != batch)
                def _():
                    remote(src, dst, send, recv, where).wait_send()


def finish_kernel(q_in, kv_in, g_all, q_out, c_out, k_out, v_out, g_out, sems):
    z = coords()[0]
    copies = [(g_all, g_out)]
    for h in range(HEADS):
        cols = slice(h * DIM, (h + 1) * DIM)
        copies.append((kv_in.at[h, 0], k_out.at[:, cols]))
        copies.append((kv_in.at[h, 1], v_out.at[:, cols]))
        for kind in range(2):
            start = half_start(kind, z)
            copies.append((q_in.at[h, kind, 0:HALF], q_out.at[pl.ds(start, HALF), cols]))
            copies.append(
                (
                    q_in.at[h, kind, HALF:ROWS],
                    c_out.at[kind * CHALF : (kind + 1) * CHALF, cols],
                )
            )
    started = [
        pltpu.make_async_copy(src, dst, sems.at[i]) for i, (src, dst) in enumerate(copies)
    ]
    for copy in started:
        copy.start()
    for copy in started:
        copy.wait()


VM = pl.BlockSpec(memory_space=pltpu.VMEM)
HB = pl.BlockSpec(memory_space=pltpu.HBM)
DMA = pltpu.SemaphoreType.DMA


def shape(*dims, dtype=bf16):
    return jax.ShapeDtypeStruct(dims, dtype)


def params(collective=None, mib=40):
    if collective is None:
        return pltpu.CompilerParams(vmem_limit_bytes=mib << 20)
    return pltpu.CompilerParams(
        vmem_limit_bytes=mib << 20, collective_id=collective, has_side_effects=True
    )


def local(
    q_hist, k_hist, v_hist, u_hist, cand_q, cand_u, lengths, cand_user, w_out, grad_hist, grad_cand
):
    packs, kv = pl.pallas_call(
        spread_kernel,
        out_shape=(shape(ZN, PACK, DIM), shape(2, 2 * ZN, TOK, DIM)),
        in_specs=[HB] * 6,
        out_specs=(VM, VM),
        scratch_shapes=[
            pltpu.VMEM((TOK, WIDTH), bf16),
            pltpu.VMEM((2, HEADS, TOK, DIM), bf16),
            pltpu.VMEM((CAND, WIDTH), bf16),
            pltpu.VMEM((1, CAND), jnp.int32),
            pltpu.SMEM((1, 4), jnp.int32),
            DMA((2 * HEADS + 4,)),
            pltpu.VMEM((HEADS, 2, PACK, DIM), bf16),
            DMA((HEADS, 2)),
            DMA((ZN,)),
            DMA((HEADS, 2)),
            DMA((ZN,)),
            DMA((ZN,)),
            DMA((ZN,)),
            DMA((2 * ZN,)),
            DMA((2 * ZN,)),
        ],
        compiler_params=params(0),
        name="spread",
    )(*[
        pltpu.with_memory_space_constraint(a, pltpu.HBM)
        for a in (q_hist[0], k_hist[0], v_hist[0], cand_q[0], cand_user, lengths)
    ])
    kv = kv.reshape(2, KEYS, DIM)
    att = pl.pallas_call(
        forward_kernel,
        out_shape=shape(ZN, ROWS, DIM),
        in_specs=[VM] * 2,
        out_specs=VM,
        scratch_shapes=[
            pltpu.VMEM((NTILE + 1, HALF, DIM), bf16),
            pltpu.VMEM((NTILE + 1, HALF, DIM), f32),
            pltpu.VMEM((NTILE + 1, HALF, DIM), jnp.int32),
            pltpu.VMEM((NTILE + 1, HALF, DIM), jnp.int32),
            pltpu.SMEM((ROOM,), jnp.int32),
            pltpu.SMEM((BLOCKS,), jnp.int32),
        ],
        compiler_params=params(),
        name="forward",
    )(packs, kv)
    y, du, gw, datt = pl.pallas_call(
        middle_kernel,
        out_shape=(
            shape(2, 2 * PART, MODEL),
            shape(2, 2 * PART, WIDTH),
            shape(2, BAND, MODEL),
            shape(ZN, ROWS, DIM),
        ),
        in_specs=[VM] * 6,
        out_specs=(VM,) * 4,
        scratch_shapes=[
            pltpu.VMEM((2, HEADS, 2, PART, DIM), bf16),
            pltpu.VMEM((2, HEADS, 2, PART, DIM), bf16),
            pltpu.VMEM((2, 2 * PART, WIDTH), bf16),
            pltpu.VMEM((2, 2 * PART, MODEL), bf16),
            pltpu.VMEM((2, 2 * PART, WIDTH), bf16),
            pltpu.VMEM((2, 2 * PART, WIDTH), f32),
            pltpu.VMEM((2, SLAB, MODEL), f32),
            pltpu.VMEM((SLAB, MODEL), bf16),
            pltpu.VMEM((SLAB, MODEL), bf16),
            pltpu.VMEM((SLAB, MODEL), bf16),
            pltpu.VMEM((2, SIDE, BAND, MODEL), bf16),
            DMA((2, ZN)),
            DMA((2, HEADS, 2)),
            DMA((2, HEADS, 2)),
            DMA((2, ZN)),
            DMA((1,)),
            DMA((1,)),
            DMA((2, SIDE)),
            DMA((2, SIDE)),
        ],
        compiler_params=params(1),
        name="middle",
    )(att, u_hist[0], cand_u[0], grad_hist[0], grad_cand[0], w_out)
    dq, dkv, y_hist, y_cand, du_hist, du_cand = pl.pallas_call(
        backward_kernel,
        out_shape=(
            shape(ZN, ROWS, DIM),
            shape(2, KEYS, DIM),
            shape(TOK, MODEL),
            shape(CAND, MODEL),
            shape(TOK, WIDTH),
            shape(CAND, WIDTH),
        ),
        in_specs=[VM] * 5,
        out_specs=(VM, VM, HB, HB, HB, HB),
        scratch_shapes=[
            pltpu.VMEM((NTILE + 1, HALF, DIM), bf16),
            pltpu.VMEM((NTILE + 1, HALF, DIM), bf16),
            pltpu.VMEM((NTILE + 1, HALF, DIM), f32),
            pltpu.VMEM((NTILE + 1, 8, HALF), jnp.int32),
            pltpu.VMEM((NTILE + 1, 8, HALF), jnp.int32),
            pltpu.SMEM((ROOM,), jnp.int32),
            pltpu.SMEM((BLOCKS,), jnp.int32),
            pltpu.VMEM((TILE, DIM), f32),
            pltpu.VMEM((TILE, DIM), f32),
            DMA((2, 3)),
            DMA((2, 3)),
        ],
        compiler_params=params(),
        name="backward",
    )(packs, kv, datt, y, du)
    q_in, kv_in, g_all = pl.pallas_call(
        collect_kernel,
        out_shape=(
            shape(HEADS, 2, ROWS, DIM),
            shape(HEADS, 2, TOK, DIM),
            shape(2, 2, SIDE, BAND, MODEL),
        ),
        in_specs=[VM] * 3,
        out_specs=(VM,) * 3,
        scratch_shapes=[
            pltpu.VMEM((2 * ZN, TOK, DIM), bf16),
            pltpu.VMEM((ZN, TOK, DIM), bf16),
            pltpu.VMEM((2 * ZN, TOK, DIM), bf16),
            pltpu.VMEM((2, SIDE, BAND, SLAB), bf16),
            pltpu.VMEM((2, BAND, SLAB), bf16),
            pltpu.VMEM((ZN, 16, DIM), bf16),
            pltpu.VMEM((16, DIM), bf16),
            DMA((ZN,)),
            DMA((HEADS, 2)),
            DMA((2 * ZN,)),
            DMA((2 * ZN,)),
            DMA((ZN,)),
            DMA((ZN,)),
            DMA((ZN,)),
            DMA((HEADS, 2)),
            DMA((2, SIDE)),
            DMA((2, SIDE)),
            DMA((ZN,)),
            DMA((ZN,)),
            DMA((ZN,)),
            DMA((ZN,)),
            DMA((2, SIDE)),
            DMA((2, SIDE)),
            DMA((2, SIDE)),
            DMA((2, SIDE)),
            DMA((2, SIDE)),
            DMA((2, SIDE)),
        ],
        compiler_params=params(2),
        name="collect",
    )(dq, dkv.reshape(2, 2 * ZN, TOK, DIM), gw)
    gq, gcq, gk, gv, g_out = pl.pallas_call(
        finish_kernel,
        out_shape=(
            shape(TOK, WIDTH),
            shape(CAND, WIDTH),
            shape(TOK, WIDTH),
            shape(TOK, WIDTH),
            shape(WIDTH, MODEL),
        ),
        in_specs=[VM] * 3,
        out_specs=(HB,) * 5,
        scratch_shapes=[DMA((1 + 6 * HEADS,))],
        compiler_params=params(),
        name="finish",
    )(q_in, kv_in, g_all.reshape(WIDTH, MODEL))
    return (
        y_hist[None], y_cand[None], gq[None], gk[None], gv[None], du_hist[None], gcq[None],
        du_cand[None], g_out,
    )


def solution(mesh):
    rows = P("dp", "ctx", None)
    return jax.shard_map(
        local,
        mesh=mesh,
        in_specs=(rows, rows, rows, rows, rows, rows, P("dp", None), P("dp", "ctx"), P(), rows, rows),
        out_specs=(rows, rows, rows, rows, rows, rows, rows, rows, P()),
        check_vma=False,
    )
```

```python
import functools
import math

import jax
import jax.numpy as jnp
from jax import lax
from jax.experimental import pallas as pl
from jax.experimental.pallas import tpu as pltpu
from jax.sharding import PartitionSpec as P

HEADS = 4
DIM = 128
EPS = 1e-05
ZN = 8
SIDE = 4
BAND = 32
SLAB = 256
PART = 64
TOK = 192
CAND = 64
HALF = TOK // 2
CHALF = CAND // 2
ROWS = HALF + CHALF
META = 16
PACK = ROWS + META
KEYS = 3072
WIDTH = HEADS * DIM
MODEL = 1024
CANDS = ZN * CHALF
SCALE = 1.0 / math.sqrt(DIM)
ORDER = (0, 1, 7, 2, 6, 3, 5, 4)
TILE = 768
GROUP = 4
NTILE = 11
BLOCKS = KEYS // TILE
ROOM = BLOCKS * (NTILE + GROUP)
SHARDS = TILE // TOK
PLAN = (
    ((0, 1, 2, 3), (4, 5, 8, 9, 10)),
    ((2, 3, 4, 5), (6, 7, 8, 9, 10)),
    ((4, 5, 6, 7), (8, 9, 10)),
    ((6, 7, 8, 9, 10),),
)
MESH = pl.DeviceIdType.MESH
bf16 = jnp.bfloat16
f32 = jnp.float32


def coords():
    ctx, dp = lax.axis_index("ctx"), lax.axis_index("dp")
    core = dp % 2
    return ctx // 2, ctx % 2, core, dp - core


def device(base, z, x, core):
    return {"ctx": z * 2 + x, "dp": base + core}


def column(z, x, core, base):
    return [
        device(base, (z + step) % ZN, x, (core + other) % 2)
        for step in range(ZN)
        for other in range(2)
        if step or other
    ]


def spots(x, base):
    return base // 8 * 2 + x, base % 8 // 2


def along(z, core, axis, spot, place):
    wide, high = (place, spot[1]) if axis == 0 else (spot[0], place)
    return {"ctx": z * 2 + wide % 2, "dp": wide // 2 * 8 + high * 2 + core}


def plane(z, x, core, base):
    spot = spots(x, base)
    return [
        along(z, core, axis, spot, (spot[axis] + step) % SIDE)
        for axis in range(2)
        for step in range(1, SIDE)
    ]


def greet(others):
    barrier = pltpu.get_barrier_semaphore()
    for other in others:
        pl.semaphore_signal(barrier, inc=1, device_id=other, device_id_type=MESH)
    pl.semaphore_wait(barrier, len(others))


def landed(ref, sem):
    pltpu.make_async_copy(ref, ref, sem).wait()


def remote(src, dst, send, recv, where):
    return pltpu.make_async_remote_copy(
        src_ref=src,
        dst_ref=dst,
        send_sem=send,
        recv_sem=recv,
        device_id=where,
        device_id_type=MESH,
    )


def half_start(core, z):
    return pl.multiple_of(((core + z) % 2) * HALF, HALF)


def spread_kernel(
    q_hbm, k_hbm, v_hbm, c_hbm, user_hbm, len_hbm, q_out, kv_out,
    q_ref, kv_ref, c_ref, user_ref, len_ref, l_sem, pack, s_q, r_q, s_kv, r_kv, s_x, r_x, s_s, r_s,
):
    z, x, core, base = coords()
    fetches = [
        pltpu.make_async_copy(src, dst, l_sem.at[i])
        for i, (src, dst) in enumerate(
            [
                (src.at[:, h * DIM : (h + 1) * DIM], kv_ref.at[kind, h])
                for h in range(HEADS)
                for kind, src in ((0, k_hbm), (1, v_hbm))
            ]
            + [
                (q_hbm, q_ref),
                (c_hbm, c_ref),
                (user_hbm, user_ref),
                (len_hbm, len_ref),
            ]
        )
    ]
    for fetch in fetches:
        fetch.start()
    greet(column(z, x, core, base) + [device(base, z, 1 - x, core)])
    own = 2 * z + x
    turn = jnp.where(z % 2 > core, 1, 3)
    turns = (0, turn, 4 - turn, 2)
    dests = []
    for j in range(HEADS):
        h = (z // 2 + turns[j]) % HEADS
        dests.append((h, 2 * h + core))
    at_home = dests[0][1] == z

    def kv_source(j, kind):
        return kv_ref.at[kind, dests[j][0]]

    def send_kv(j, kind):
        return remote(
            kv_source(j, kind), kv_out.at[kind, own], s_kv.at[j, kind], r_kv.at[z],
            device(base, dests[j][1], x, kind),
        )

    def send_q(j, kind):
        return remote(
            pack.at[dests[j][0], kind], q_out.at[z], s_q.at[j, kind], r_q.at[z],
            device(base, dests[j][1], x, kind),
        )

    for fetch in fetches[: 2 * HEADS]:
        fetch.wait()
    def start_all(j, send, local_pair):
        for kind in range(2):
            if j:
                send(j, kind).start()
            else:
                here = at_home & (core == kind)

                @pl.when(here)
                def _():
                    pltpu.make_async_copy(*local_pair(kind)).start()

                @pl.when(jnp.logical_not(here))
                def _():
                    send(j, kind).start()

    def sent(j, send):
        for kind in range(2):
            if j:
                send(j, kind).wait_send()
            else:

                @pl.when(jnp.logical_not(at_home & (core == kind)))
                def _():
                    send(j, kind).wait_send()

    def start_kv(j):
        start_all(j, send_kv, lambda kind: (kv_source(0, kind), kv_out.at[kind, own], r_kv.at[z]))

    def start_q(j):
        start_all(j, send_q, lambda kind: (pack.at[dests[0][0], kind], q_out.at[z], r_q.at[z]))

    for j in range(HEADS):
        start_kv(j)
    for fetch in fetches[2 * HEADS :]:
        fetch.wait()
    lane = lax.broadcasted_iota(jnp.int32, (META, DIM), 1)
    row = lax.broadcasted_iota(jnp.int32, (META, DIM), 0)
    lens = jnp.zeros((META, DIM), jnp.int32)
    for i in range(4):
        lens = jnp.where(lane == i, len_ref[0, i], lens)
    lens_f = lens.astype(f32)
    high = jnp.floor(lens_f * (1.0 / 64.0))
    low = lens_f - high * 64.0
    users = jnp.broadcast_to(user_ref[...].astype(f32), (META, CAND)).astype(bf16)
    sel_j = lax.broadcasted_iota(jnp.int32, (CAND, DIM), 0)
    sel_l = lax.broadcasted_iota(jnp.int32, (CAND, DIM), 1)
    spot = CHALF * (z % 4)
    for kind in range(2):
        start = half_start(kind, z)
        pick = (
            (sel_l - spot + CHALF * kind == sel_j) & (sel_l >= spot) & (sel_l < spot + CHALF)
        ).astype(f32)
        placed = jnp.dot(users, pick.astype(bf16), preferred_element_type=f32)
        meta = jnp.where(row == 0, placed, jnp.where(row == 1, high, low)).astype(bf16)
        for h in range(HEADS):
            cols = slice(h * DIM, (h + 1) * DIM)
            pack[h, kind, 0:HALF, :] = q_ref[pl.ds(start, HALF), cols]
            pack[h, kind, HALF:ROWS, :] = c_ref[kind * CHALF : (kind + 1) * CHALF, cols]
            pack[h, kind, ROWS:PACK, :] = meta
    def across(s, zi):
        slot = kv_out.at[core, s]
        return remote(slot, slot, s_x.at[zi], r_x.at[zi], device(base, z, 1 - x, core))

    def beside(s):
        slot = kv_out.at[core, s]
        return remote(slot, slot, s_s.at[s], r_s.at[s], device(base, z, x, 1 - core))

    def pass_on(step):
        zi = (z + ORDER[step]) % ZN
        s = 2 * zi + (1 - x)
        landed(kv_out.at[core, s], r_x.at[zi])
        beside(s).start()

    for step in range(ZN):
        zi = (z + ORDER[step]) % ZN
        s = 2 * zi + x
        landed(kv_out.at[core, s], r_kv.at[zi])
        across(s, zi).start()
        beside(s).start()
        if step == 0:
            sent(0, send_kv)
        if step == 2:
            sent(1, send_kv)
        if step == 4:
            sent(2, send_kv)
            start_q(0)
            start_q(1)
        if step == 6:
            sent(3, send_kv)
            start_q(2)
            start_q(3)
        if step >= 2:
            pass_on(step - 2)
    pass_on(ZN - 2)
    pass_on(ZN - 1)
    for zi in range(ZN):
        landed(q_out.at[zi], r_q.at[zi])
    for s in range(2 * ZN):
        landed(kv_out.at[1 - core, s], r_s.at[s])
    for s in range(2 * ZN):
        beside(s).wait_send()
    for zi in range(ZN):
        across(2 * zi + x, zi).wait_send()
    for j in range(HEADS):
        sent(j, send_q)


def read_meta(q_ref):
    first = sum(q_ref[zi, ROWS:PACK, :].astype(f32) for zi in range(4))[0:1]
    second = sum(q_ref[zi, ROWS:PACK, :].astype(f32) for zi in range(4, 8))[0:1]
    users = jnp.concatenate([first, second], axis=1)
    block = q_ref[0, ROWS:PACK, :].astype(f32)
    lens = block[1:2] * 64.0 + block[2:3]
    lane = lax.broadcasted_iota(jnp.int32, (1, DIM), 1)
    ends = []
    for i in range(3):
        ends.append(jnp.sum(jnp.where(lane <= i, lens, 0.0)).astype(jnp.int32))
    starts = [jnp.sum((users < float(i)).astype(f32)).astype(jnp.int32) for i in range(1, 4)]
    sub = lax.broadcasted_iota(jnp.int32, (8, CANDS), 0).astype(f32)
    hot = (users == sub).astype(f32)
    before = jnp.sum((users < sub).astype(f32), axis=1, keepdims=True)
    rows = lax.broadcasted_iota(jnp.int32, (CANDS, CANDS), 0)
    cols = lax.broadcasted_iota(jnp.int32, (CANDS, CANDS), 1)
    upper = (rows < cols).astype(f32).astype(bf16)
    prior = jnp.dot(hot.astype(bf16), upper, preferred_element_type=f32)
    rank = jnp.sum(hot * (prior + before), axis=0, keepdims=True).astype(jnp.int32)
    perm = (rows == rank).astype(f32).astype(bf16)
    return ends, starts, perm


def first_of(ends, pos):
    low = jnp.where(pos >= ends[0], ends[0], 0)
    low = jnp.where(pos >= ends[1], ends[1], low)
    return jnp.where(pos >= ends[2], ends[2], low)


def cand_range(ends, starts, row):
    low = jnp.where(row >= starts[0], ends[0], 0)
    low = jnp.where(row >= starts[1], ends[1], low)
    low = jnp.where(row >= starts[2], ends[2], low)
    high = jnp.where(row >= starts[0], ends[1], ends[0])
    high = jnp.where(row >= starts[1], ends[2], high)
    high = jnp.where(row >= starts[2], KEYS, high)
    return low, high


def hist_start(zi):
    z, x, core, base = coords()
    return (2 * zi + x) * TOK + ((core + zi) % 2) * HALF


NT = (((1,), (1,)), ((), ()))
TN = (((0,), (0,)), ((), ()))


def work_list(z, x, core, ends, starts, tiles, counts):
    ranges = []
    for zi in range(ZN):
        p0 = hist_start(zi)
        ranges.append((first_of(ends, p0), p0 + HALF))
    for c in range(NTILE - ZN):
        first, last = c * HALF, min((c + 1) * HALF, CANDS) - 1
        ranges.append((cand_range(ends, starts, first)[0], cand_range(ends, starts, last)[1]))
    for block in range(BLOCKS):
        at = block * (NTILE + GROUP)
        used = jnp.int32(0)
        for i, (low, high) in enumerate(ranges):
            hit = (low < (block + 1) * TILE) & (high > block * TILE)
            tiles[at + used] = jnp.int32(i)
            used = used + hit.astype(jnp.int32)
        for i in range(GROUP - 1):
            tiles[at + used + i] = jnp.int32(NTILE)
        counts[block] = used


def set_bounds(ends, starts, low_ref, high_ref):
    lane = lax.broadcasted_iota(jnp.int32, (HALF, DIM), 1)
    row = lax.broadcasted_iota(jnp.int32, (HALF, DIM), 0)
    for zi in range(ZN):
        pos = hist_start(zi) + row
        low_ref[zi] = first_of(ends, pos) - lane
        high_ref[zi] = pos + 1 - lane
    for c in range(NTILE - ZN):
        low, high = cand_range(ends, starts, c * HALF + row)
        low_ref[ZN + c] = low - lane
        high_ref[ZN + c] = jnp.where(c * HALF + row < CANDS, high, 0) - lane
    low_ref[NTILE] = jnp.zeros((HALF, DIM), jnp.int32)
    high_ref[NTILE] = jnp.full((HALF, DIM), -KEYS, jnp.int32)


def set_bounds_t(ends, starts, low_ref, high_ref):
    lane = lax.broadcasted_iota(jnp.int32, (8, HALF), 1)
    for zi in range(ZN):
        pos = hist_start(zi) + lane
        low_ref[zi] = first_of(ends, pos)
        high_ref[zi] = pos + 1
    for c in range(NTILE - ZN):
        low, high = cand_range(ends, starts, c * HALF + lane)
        low_ref[ZN + c] = low
        high_ref[ZN + c] = jnp.where(c * HALF + lane < CANDS, high, 0)
    low_ref[NTILE] = jnp.zeros((8, HALF), jnp.int32)
    high_ref[NTILE] = jnp.full((8, HALF), -KEYS, jnp.int32)


def inside(low, high, start):
    masks = []
    for i in range(TILE // DIM):
        at = start + i * DIM
        masks.append((low <= at) & (high > at))
    return jnp.concatenate(masks, axis=1)


def load_rows(src, perm, dst):
    for zi in range(ZN):
        dst[zi] = src[zi, 0:HALF, :]
    cand = jnp.concatenate([src[zi, HALF:ROWS, :] for zi in range(ZN)], axis=0)
    cand = jnp.dot(perm, cand, preferred_element_type=f32).astype(bf16)
    dst[ZN] = cand[0:HALF]
    dst[ZN + 1] = cand[HALF : 2 * HALF]
    dst[ZN + 2, 0 : CANDS - 2 * HALF, :] = cand[2 * HALF :]
    dst[ZN + 2, CANDS - 2 * HALF :, :] = jnp.zeros((3 * HALF - CANDS, DIM), bf16)
    dst[NTILE] = jnp.zeros((HALF, DIM), bf16)


def store_rows(acc, perm, dst, factor):
    for zi in range(ZN):
        dst[zi, 0:HALF, :] = (acc[zi] * factor).astype(bf16)
    cand = jnp.concatenate([acc[ZN], acc[ZN + 1], acc[ZN + 2, 0 : CANDS - 2 * HALF, :]], axis=0)
    back = lax.dot_general(
        perm, (cand * factor).astype(bf16), TN, preferred_element_type=f32
    ).astype(bf16)
    for zi in range(ZN):
        dst[zi, HALF:ROWS, :] = back[zi * CHALF : (zi + 1) * CHALF]


def for_groups(tiles, counts, block, body):
    at = block * (NTILE + GROUP)
    used = counts[block]
    whole = used // GROUP
    rest = used - whole * GROUP

    def step(i, carry):
        body([tiles[at + i * GROUP + n] for n in range(GROUP)])
        return carry

    lax.fori_loop(0, whole, step, jnp.int32(0))

    @pl.when((rest > 0) & (rest <= GROUP // 2))
    def _():
        body([tiles[at + whole * GROUP + n] for n in range(GROUP // 2)])

    @pl.when(rest > GROUP // 2)
    def _():
        body([tiles[at + whole * GROUP + n] for n in range(GROUP)])


def stacked(ref, picks):
    return jnp.concatenate([ref[i] for i in picks], axis=0)


def forward_kernel(q_ref, kv_ref, a_ref, q_all, acc, low_ref, high_ref, tiles, counts):
    z, x, core, base = coords()
    ends, starts, perm = read_meta(q_ref)
    work_list(z, x, core, ends, starts, tiles, counts)
    set_bounds(ends, starts, low_ref, high_ref)
    load_rows(q_ref, perm, q_all)
    acc[...] = jnp.zeros(acc.shape, f32)
    for block in range(BLOCKS):
        start = block * TILE

        def body(picks):
            keys = kv_ref[0, start : start + TILE, :]
            values = kv_ref[1, start : start + TILE, :]
            q = stacked(q_all, picks)
            t = lax.dot_general(q, keys, NT, preferred_element_type=f32) * (0.5 * SCALE)
            ok = inside(stacked(low_ref, picks), stacked(high_ref, picks), start)
            gate = jnp.where(ok, 1.0 + jnp.tanh(t), 0.0)
            out = jnp.dot((t * gate).astype(bf16), values, preferred_element_type=f32)
            for n, pick in enumerate(picks):
                acc[pick] += out[n * HALF : (n + 1) * HALF]

        for_groups(tiles, counts, block, body)
    store_rows(acc, perm, a_ref, 1.0)


def ordered(src, hist, cand, sems):
    z = coords()[0]
    copies = []
    for kind in range(2):
        start = half_start(kind, z)
        low = kind * PART
        pieces = (
            (src.at[0, pl.ds(low, PART)], hist.at[pl.ds(start, PART)]),
            (src.at[1, pl.ds(low, HALF - PART)], hist.at[pl.ds(start + PART, HALF - PART)]),
            (src.at[1, pl.ds(low + HALF - PART, CHALF)], cand.at[pl.ds(kind * CHALF, CHALF)]),
        )
        for i, (one, two) in enumerate(pieces):
            copies.append(pltpu.make_async_copy(one, two, sems.at[kind, i]))
    return copies


def middle_kernel(
    a_ref, u_ref, cu_ref, g_ref, cg_ref, w_ref, y_out, du_out, gw_out, da_out,
    a_in, da_pack, gated, up, gates, dgs, g_part, g_send, g_in, g_sum, g_side,
    s_a, r_a, s_d, r_d, s_g, r_g, s_p, r_p,
):
    z, x, core, base = coords()
    greet(column(z, x, core, base) + plane(z, x, core, base))
    batch = z % 2
    head = z // 2

    def send_a(part, step):
        zi = (z + step) % ZN
        return remote(
            a_ref.at[zi, pl.ds(part * PART, PART)], a_in.at[part, head, core],
            s_a.at[part, step], r_a.at[part, head, core], device(base, zi, x, batch),
        )

    def start_a(part):
        for step in (4, 3, 5, 2, 6, 1, 7):
            send_a(part, step).start()

        @pl.when(core == batch)
        def _():
            pltpu.make_async_copy(
                a_ref.at[z, pl.ds(part * PART, PART)],
                a_in.at[part, head, core],
                r_a.at[part, head, core],
            ).start()

        @pl.when(core != batch)
        def _():
            send_a(part, 0).start()

    start_a(0)
    for kind in range(2):
        start = half_start(kind, z)
        low, mid, high = kind * PART, kind * PART + HALF - PART, (kind + 1) * PART
        later = pl.multiple_of(start + PART, 32)
        cands = slice(kind * CHALF, (kind + 1) * CHALF)
        for dst, hist, cand in ((up, g_ref, cg_ref), (gates, u_ref, cu_ref)):
            dst[0, low:high, :] = hist[pl.ds(start, PART), :]
            dst[1, low:mid, :] = hist[pl.ds(later, HALF - PART), :]
            dst[1, mid:high, :] = cand[cands, :]
    for part in range(2):
        dgs[part] = lax.dot_general(up[part], w_ref[...], NT, preferred_element_type=f32)
        if part == 0:
            start_a(1)

    def dest(j):
        h = (z // 2 + j) % HEADS
        return h, 2 * h + core

    def send_d(part, j, kind):
        h, z2 = dest(j)
        return remote(
            da_pack.at[part, h, kind], da_out.at[z, pl.ds(part * PART, PART)],
            s_d.at[part, j, kind], r_d.at[part, z], device(base, z2, x, kind),
        )

    at_home = dest(0)[1] == z
    for part in range(2):
        for h in range(HEADS):
            for kind in range(2):
                landed(a_in.at[part, h, kind], r_a.at[part, h, kind])
        att = jnp.concatenate(
            [a_in[part, h].reshape(2 * PART, DIM) for h in range(HEADS)], axis=1
        ).astype(f32)
        mean = jnp.mean(att, axis=1, keepdims=True)
        centered = att - mean
        var = jnp.mean(centered * centered, axis=1, keepdims=True)
        rstd = lax.rsqrt(var + EPS)
        normed = centered * rstd
        gate = gates[part].astype(f32)
        dg = dgs[part]
        dn = dg * gate
        da = rstd * (
            dn
            - jnp.mean(dn, axis=1, keepdims=True)
            - normed * jnp.mean(dn * normed, axis=1, keepdims=True)
        )
        for h in range(HEADS):
            da_pack[part, h] = (
                da[:, h * DIM : (h + 1) * DIM].astype(bf16).reshape(2, PART, DIM)
            )
        for j in (2, 1, 3):
            for kind in range(2):
                send_d(part, j, kind).start()
        for kind in range(2):
            here = at_home & (core == kind)

            @pl.when(here)
            def _():
                pltpu.make_async_copy(
                    da_pack.at[part, dest(0)[0], kind],
                    da_out.at[z, pl.ds(part * PART, PART)],
                    r_d.at[part, z],
                ).start()

            @pl.when(jnp.logical_not(here))
            def _():
                send_d(part, 0, kind).start()

        gated[part] = (normed * gate).astype(bf16)
        if part == 0:
            for half in range(2):
                g_part[half] = lax.dot_general(
                    gated[0, :, half * SLAB : (half + 1) * SLAB], up[0], TN,
                    preferred_element_type=f32,
                )
        dgs[part] = dg * normed

    def weight_half(owner):
        cols = pl.ds(pl.multiple_of(owner * SLAB, SLAB), SLAB)
        total = lax.dot_general(gated[1, :, cols], up[1], TN, preferred_element_type=f32)
        return (g_part[owner] + total) * (1.0 / 256.0)

    g_send[...] = weight_half(1 - core).astype(bf16)
    beside = remote(g_send, g_in, s_g.at[0], r_g.at[0], device(base, z, x, 1 - core))
    beside.start()
    own = weight_half(core)
    landed(g_in, r_g.at[0])
    g_sum[...] = (own + g_in[...].astype(f32)).astype(bf16)
    spot = spots(x, base)

    def piece(axis, place):
        row = pl.multiple_of(((1 - axis) * SIDE + place) * BAND, BAND)
        return g_sum.at[pl.ds(row, BAND)]

    def send_p(axis, step):
        place = (spot[axis] + step) % SIDE
        return remote(
            piece(axis, place), g_side.at[axis, spot[axis]], s_p.at[axis, step],
            r_p.at[axis, spot[axis]], along(z, core, axis, spot, place),
        )

    for axis in range(2):
        for step in (2, 1, 3):
            send_p(axis, step).start()
        pltpu.make_async_copy(
            piece(axis, spot[axis]), g_side.at[axis, spot[axis]], r_p.at[axis, spot[axis]]
        ).start()
    for part in range(2):
        du_out[part] = dgs[part].astype(bf16)
    for part in range(2):
        y_out[part] = jnp.dot(gated[part], w_ref[...], preferred_element_type=f32).astype(bf16)
    for axis in range(2):
        for place in range(SIDE):
            landed(g_side.at[axis, place], r_p.at[axis, place])
        gw_out[axis] = jnp.sum(g_side[axis].astype(f32), axis=0).astype(bf16)

    for part in range(2):
        for zi in range(ZN):
            landed(da_out.at[zi, pl.ds(part * PART, PART)], r_d.at[part, zi])
        for step in range(1, ZN):
            send_a(part, step).wait_send()

        @pl.when(core != batch)
        def _():
            send_a(part, 0).wait_send()

        for j in range(HEADS):
            for kind in range(2):
                if j:
                    send_d(part, j, kind).wait_send()
                else:

                    @pl.when(jnp.logical_not(at_home & (core == kind)))
                    def _():
                        send_d(part, 0, kind).wait_send()

    beside.wait_send()
    for axis in range(2):
        for step in range(1, SIDE):
            send_p(axis, step).wait_send()


def gradient_kernel(
    q_ref, key_ref, da_ref, gw_ref, q_in, kv_in, g_all,
    q_all, da_all, acc, low_ref, high_ref, dk_acc, dv_acc, dq_ref, dkv_ref,
    beside_in, across_in, sums, g_two, g_slab, g_z, g_mine,
    s_q, r_q, s_s, r_s, s_x, r_x, s_kv, r_kv,
    s_two, r_two, s_z, r_z, s_zz, r_zz, s_five, r_five, s_six, r_six, s_b, r_b,
):
    z, x, core, base = coords()
    greet(column(z, x, core, base) + plane(z, x, core, base))
    batch = z % 2
    head = z // 2
    spot = spots(x, base)

    def block(axis, rows, slab):
        return g_all.at[core, 1 - axis, rows, :, slab]

    def slab_of(place):
        return pl.ds(pl.multiple_of(place * SLAB, SLAB), SLAB)

    def two(axis, step):
        other = 1 - axis
        place = (spot[other] + step) % SIDE
        return remote(
            gw_ref.at[axis, :, slab_of(place)], g_two.at[axis, spot[other]],
            s_two.at[axis, step], r_two.at[axis, spot[other]],
            along(z, core, other, spot, place),
        )

    def z_part(zi):
        return (
            zi // 4,
            pl.ds(pl.multiple_of(zi % 2 * 16, 16), 16),
            pl.ds(pl.multiple_of(zi // 2 % 2 * DIM, DIM), DIM),
        )

    def z_place(zi):
        half, rows, lanes = z_part(zi)
        start = jnp.where(half == 0, spot[1], spot[0]) * SLAB + zi // 2 % 2 * DIM
        band = jnp.where(half == 0, spot[0], spot[1])
        return g_all.at[core, 1 - half, band, rows, pl.ds(pl.multiple_of(start, DIM), DIM)]

    def scatter_z(step):
        zi = (z + step) % ZN
        half, rows, lanes = z_part(zi)
        return remote(
            g_slab.at[half, rows, lanes], g_z.at[z], s_z.at[step], r_z.at[z],
            device(base, zi, x, core),
        )

    def gather_z(step):
        zi = (z + step) % ZN
        return remote(
            g_mine, z_place(z), s_zz.at[step], r_zz.at[z], device(base, zi, x, core)
        )

    def five(axis, step):
        other = 1 - axis
        here = block(axis, spot[axis], slab_of(spot[other]))
        return remote(
            here, here, s_five.at[axis, step], r_five.at[axis, spot[other]],
            along(z, core, other, spot, (spot[other] + step) % SIDE),
        )

    def six(axis, step):
        here = g_all.at[core, 1 - axis, spot[axis]]
        return remote(
            here, here, s_six.at[axis, step], r_six.at[axis, spot[axis]],
            along(z, core, axis, spot, (spot[axis] + step) % SIDE),
        )

    def gather_b(axis, place):
        here = g_all.at[core, 1 - axis, place]
        return remote(
            here, here, s_b.at[axis, place], r_b.at[axis, place],
            device(base, z, x, 1 - core),
        )

    def stage(number):
        if number == 0:
            for axis in range(2):
                for step in (2, 1, 3):
                    two(axis, step).start()
                mine = spot[1 - axis]
                pltpu.make_async_copy(
                    gw_ref.at[axis, :, slab_of(mine)], g_two.at[axis, mine],
                    r_two.at[axis, mine],
                ).start()
        if number == 1:
            for axis in range(2):
                for place in range(SIDE):
                    landed(g_two.at[axis, place], r_two.at[axis, place])
                g_slab[axis] = jnp.sum(g_two[axis].astype(f32), axis=0).astype(bf16)
            for step in (4, 3, 5, 2, 6, 1, 7):
                scatter_z(step).start()
            half, rows, lanes = z_part(z)
            pltpu.make_async_copy(g_slab.at[half, rows, lanes], g_z.at[z], r_z.at[z]).start()
        if number == 2:
            for zi in range(ZN):
                landed(g_z.at[zi], r_z.at[zi])
            g_mine[...] = jnp.sum(g_z[...].astype(f32), axis=0).astype(bf16)
            for step in (4, 3, 5, 2, 6, 1, 7):
                gather_z(step).start()
            pltpu.make_async_copy(g_mine, z_place(z), r_zz.at[z]).start()
        if number == 3:
            for zi in range(ZN):
                landed(z_place(zi), r_zz.at[zi])
            for axis in range(2):
                for step in (2, 1, 3):
                    five(axis, step).start()
        if number == 4:
            for axis in range(2):
                other = 1 - axis
                for step in range(1, SIDE):
                    place = (spot[other] + step) % SIDE
                    landed(block(axis, spot[axis], slab_of(place)), r_five.at[axis, place])
                for step in (2, 1, 3):
                    six(axis, step).start()
                gather_b(axis, spot[axis]).start()
        if number == 5:
            for axis in range(2):
                for step in (1, 3, 2):
                    place = (spot[axis] + step) % SIDE
                    landed(g_all.at[core, 1 - axis, place], r_six.at[axis, place])
                    gather_b(axis, place).start()

    def beside(zi, side):
        s = 2 * zi + side
        return remote(
            dkv_ref.at[1 - core, s], beside_in.at[s], s_s.at[s], r_s.at[s],
            device(base, z, x, 1 - core),
        )

    def across(zi):
        return remote(
            sums.at[2 * zi + 1 - x], across_in.at[zi], s_x.at[zi], r_x.at[zi],
            device(base, z, 1 - x, core),
        )

    def q_parts(zi):
        return dq_ref.at[zi], q_in.at[head, core], s_q.at[zi], r_q.at[head, core]

    def kv_parts(zi):
        return sums.at[2 * zi + x], kv_in.at[head, core], s_kv.at[zi], r_kv.at[head, core]

    def home(zi, parts):
        src, dst, send, recv = parts(zi)
        here = (z == zi) & (core == batch)

        @pl.when(here)
        def _():
            pltpu.make_async_copy(src, dst, recv).start()

        @pl.when(jnp.logical_not(here))
        def _():
            remote(src, dst, send, recv, device(base, zi, x, batch)).start()

    stage(0)
    ends, starts, perm = read_meta(q_ref)
    set_bounds_t(ends, starts, low_ref, high_ref)
    load_rows(q_ref, perm, q_all)
    load_rows(da_ref, perm, da_all)
    acc[...] = jnp.zeros(acc.shape, f32)

    def products(block, picks, first):
        keys = key_ref[0, block * TILE : (block + 1) * TILE, :]
        values = key_ref[1, block * TILE : (block + 1) * TILE, :]
        q = stacked(q_all, picks)
        da = stacked(da_all, picks)
        t = lax.dot_general(keys, q, NT, preferred_element_type=f32) * (0.5 * SCALE)
        dp = lax.dot_general(values, da, NT, preferred_element_type=f32)
        low = jnp.concatenate([low_ref[i] for i in picks], axis=1)[0:1] - block * TILE
        high = jnp.concatenate([high_ref[i] for i in picks], axis=1)[0:1] - block * TILE
        pos = lax.broadcasted_iota(jnp.int32, t.shape, 0)
        gate = jnp.where((pos >= low) & (pos < high), 1.0 + jnp.tanh(t), 0.0)
        p = t * gate
        ds = (dp * (gate * ((1.0 + t + t) - p))).astype(bf16)
        dk = jnp.dot(ds, q, preferred_element_type=f32)
        dv = jnp.dot(p.astype(bf16), da, preferred_element_type=f32)
        if first:
            dk_acc[...] = dk
            dv_acc[...] = dv
        else:
            dk_acc[...] += dk
            dv_acc[...] += dv
        out = lax.dot_general(ds, keys, TN, preferred_element_type=f32)
        for n, pick in enumerate(picks):
            acc[pick] += out[n * HALF : (n + 1) * HALF]

    def key_block(block):
        for n, picks in enumerate(PLAN[block]):
            products(block, picks, n == 0)
        low = block * SHARDS
        dk = (dk_acc[...] * (0.5 * SCALE)).astype(bf16)
        dkv_ref[0, low : low + SHARDS] = dk.reshape(SHARDS, TOK, DIM)
        dkv_ref[1, low : low + SHARDS] = dv_acc[...].astype(bf16).reshape(SHARDS, TOK, DIM)
        for zi in levels(block):
            beside(zi, 1 - x).start()
            beside(zi, x).start()

    def levels(block):
        return range(block * SHARDS // 2, (block + 1) * SHARDS // 2)

    def add_beside(zi, side):
        s = 2 * zi + side
        landed(beside_in.at[s], r_s.at[s])
        return dkv_ref[core, s].astype(f32) + beside_in[s].astype(f32)

    def cross(block):
        for zi in levels(block):
            sums[2 * zi + 1 - x] = add_beside(zi, 1 - x).astype(bf16)
            across(zi).start()

    def finish(block):
        for zi in levels(block):
            total = add_beside(zi, x)
            landed(across_in.at[zi], r_x.at[zi])
            sums[2 * zi + x] = (total + across_in[zi].astype(f32)).astype(bf16)
            home(zi, kv_parts)

    key_block(0)
    stage(1)
    key_block(1)
    cross(0)
    stage(2)
    key_block(2)
    cross(1)
    finish(0)
    stage(3)
    key_block(3)
    cross(2)
    finish(1)
    store_rows(acc, perm, dq_ref, 0.5 * SCALE)
    for zi in range(ZN):
        home(zi, q_parts)
    stage(4)
    cross(3)
    finish(2)
    finish(3)
    stage(5)
    for kind in range(2):
        for h in range(HEADS):
            landed(q_in.at[h, kind], r_q.at[h, kind])
            landed(kv_in.at[h, kind], r_kv.at[h, kind])
    for axis in range(2):
        for place in range(SIDE):
            landed(g_all.at[1 - core, 1 - axis, place], r_b.at[axis, place])

    for step in range(1, ZN):
        scatter_z(step).wait_send()
        gather_z(step).wait_send()
    for axis in range(2):
        for step in range(1, SIDE):
            two(axis, step).wait_send()
            five(axis, step).wait_send()
            six(axis, step).wait_send()
        for place in range(SIDE):
            gather_b(axis, place).wait_send()
    for zi in range(ZN):
        beside(zi, x).wait_send()
        beside(zi, 1 - x).wait_send()
        across(zi).wait_send()

        @pl.when(jnp.logical_not((z == zi) & (core == batch)))
        def _():
            for parts in (q_parts, kv_parts):
                src, dst, send, recv = parts(zi)
                remote(src, dst, send, recv, device(base, zi, x, batch)).wait_send()


def finish_kernel(
    q_in, kv_in, g_all, y_ref, du_ref, q_out, c_out, k_out, v_out, g_out,
    y_out, cy_out, du_out, cdu_out, sems, y_sem, du_sem,
):
    z = coords()[0]
    copies = [(g_all, g_out)]
    for h in range(HEADS):
        cols = slice(h * DIM, (h + 1) * DIM)
        copies.append((kv_in.at[h, 0], k_out.at[:, cols]))
        copies.append((kv_in.at[h, 1], v_out.at[:, cols]))
        for kind in range(2):
            start = half_start(kind, z)
            copies.append((q_in.at[h, kind, 0:HALF], q_out.at[pl.ds(start, HALF), cols]))
            copies.append(
                (
                    q_in.at[h, kind, HALF:ROWS],
                    c_out.at[kind * CHALF : (kind + 1) * CHALF, cols],
                )
            )
    started = [
        pltpu.make_async_copy(src, dst, sems.at[i]) for i, (src, dst) in enumerate(copies)
    ]
    started += ordered(y_ref, y_out, cy_out, y_sem) + ordered(du_ref, du_out, cdu_out, du_sem)
    for copy in started:
        copy.start()
    for copy in started:
        copy.wait()


VM = pl.BlockSpec(memory_space=pltpu.VMEM)
HB = pl.BlockSpec(memory_space=pltpu.HBM)
DMA = pltpu.SemaphoreType.DMA


def shape(*dims, dtype=bf16):
    return jax.ShapeDtypeStruct(dims, dtype)


def params(collective=None, mib=40):
    if collective is None:
        return pltpu.CompilerParams(vmem_limit_bytes=mib << 20)
    return pltpu.CompilerParams(
        vmem_limit_bytes=mib << 20, collective_id=collective, has_side_effects=True
    )


def local(
    q_hist, k_hist, v_hist, u_hist, cand_q, cand_u, lengths, cand_user, w_out, grad_hist, grad_cand
):
    packs, kv = pl.pallas_call(
        spread_kernel,
        out_shape=(shape(ZN, PACK, DIM), shape(2, 2 * ZN, TOK, DIM)),
        in_specs=[HB] * 6,
        out_specs=(VM, VM),
        scratch_shapes=[
            pltpu.VMEM((TOK, WIDTH), bf16),
            pltpu.VMEM((2, HEADS, TOK, DIM), bf16),
            pltpu.VMEM((CAND, WIDTH), bf16),
            pltpu.VMEM((1, CAND), jnp.int32),
            pltpu.SMEM((1, 4), jnp.int32),
            DMA((2 * HEADS + 4,)),
            pltpu.VMEM((HEADS, 2, PACK, DIM), bf16),
            DMA((HEADS, 2)),
            DMA((ZN,)),
            DMA((HEADS, 2)),
            DMA((ZN,)),
            DMA((ZN,)),
            DMA((ZN,)),
            DMA((2 * ZN,)),
            DMA((2 * ZN,)),
        ],
        compiler_params=params(0),
        name="spread",
    )(*[
        pltpu.with_memory_space_constraint(a, pltpu.HBM)
        for a in (q_hist[0], k_hist[0], v_hist[0], cand_q[0], cand_user, lengths)
    ])
    kv = kv.reshape(2, KEYS, DIM)
    att = pl.pallas_call(
        forward_kernel,
        out_shape=shape(ZN, ROWS, DIM),
        in_specs=[VM] * 2,
        out_specs=VM,
        scratch_shapes=[
            pltpu.VMEM((NTILE + 1, HALF, DIM), bf16),
            pltpu.VMEM((NTILE + 1, HALF, DIM), f32),
            pltpu.VMEM((NTILE + 1, HALF, DIM), jnp.int32),
            pltpu.VMEM((NTILE + 1, HALF, DIM), jnp.int32),
            pltpu.SMEM((ROOM,), jnp.int32),
            pltpu.SMEM((BLOCKS,), jnp.int32),
        ],
        compiler_params=params(),
        name="forward",
    )(packs, kv)
    y, du, gw, datt = pl.pallas_call(
        middle_kernel,
        out_shape=(
            shape(2, 2 * PART, MODEL),
            shape(2, 2 * PART, WIDTH),
            shape(2, BAND, MODEL),
            shape(ZN, ROWS, DIM),
        ),
        in_specs=[VM] * 6,
        out_specs=(VM,) * 4,
        scratch_shapes=[
            pltpu.VMEM((2, HEADS, 2, PART, DIM), bf16),
            pltpu.VMEM((2, HEADS, 2, PART, DIM), bf16),
            pltpu.VMEM((2, 2 * PART, WIDTH), bf16),
            pltpu.VMEM((2, 2 * PART, MODEL), bf16),
            pltpu.VMEM((2, 2 * PART, WIDTH), bf16),
            pltpu.VMEM((2, 2 * PART, WIDTH), f32),
            pltpu.VMEM((2, SLAB, MODEL), f32),
            pltpu.VMEM((SLAB, MODEL), bf16),
            pltpu.VMEM((SLAB, MODEL), bf16),
            pltpu.VMEM((SLAB, MODEL), bf16),
            pltpu.VMEM((2, SIDE, BAND, MODEL), bf16),
            DMA((2, ZN)),
            DMA((2, HEADS, 2)),
            DMA((2, HEADS, 2)),
            DMA((2, ZN)),
            DMA((1,)),
            DMA((1,)),
            DMA((2, SIDE)),
            DMA((2, SIDE)),
        ],
        compiler_params=params(1),
        name="middle",
    )(att, u_hist[0], cand_u[0], grad_hist[0], grad_cand[0], w_out)
    q_in, kv_in, g_all = pl.pallas_call(
        gradient_kernel,
        out_shape=(
            shape(HEADS, 2, ROWS, DIM),
            shape(HEADS, 2, TOK, DIM),
            shape(2, 2, SIDE, BAND, MODEL),
        ),
        in_specs=[VM] * 4,
        out_specs=(VM,) * 3,
        scratch_shapes=[
            pltpu.VMEM((NTILE + 1, HALF, DIM), bf16),
            pltpu.VMEM((NTILE + 1, HALF, DIM), bf16),
            pltpu.VMEM((NTILE + 1, HALF, DIM), f32),
            pltpu.VMEM((NTILE + 1, 8, HALF), jnp.int32),
            pltpu.VMEM((NTILE + 1, 8, HALF), jnp.int32),
            pltpu.VMEM((TILE, DIM), f32),
            pltpu.VMEM((TILE, DIM), f32),
            pltpu.VMEM((ZN, ROWS, DIM), bf16),
            pltpu.VMEM((2, 2 * ZN, TOK, DIM), bf16),
            pltpu.VMEM((2 * ZN, TOK, DIM), bf16),
            pltpu.VMEM((ZN, TOK, DIM), bf16),
            pltpu.VMEM((2 * ZN, TOK, DIM), bf16),
            pltpu.VMEM((2, SIDE, BAND, SLAB), bf16),
            pltpu.VMEM((2, BAND, SLAB), bf16),
            pltpu.VMEM((ZN, 16, DIM), bf16),
            pltpu.VMEM((16, DIM), bf16),
            DMA((ZN,)),
            DMA((HEADS, 2)),
            DMA((2 * ZN,)),
            DMA((2 * ZN,)),
            DMA((ZN,)),
            DMA((ZN,)),
            DMA((ZN,)),
            DMA((HEADS, 2)),
            DMA((2, SIDE)),
            DMA((2, SIDE)),
            DMA((ZN,)),
            DMA((ZN,)),
            DMA((ZN,)),
            DMA((ZN,)),
            DMA((2, SIDE)),
            DMA((2, SIDE)),
            DMA((2, SIDE)),
            DMA((2, SIDE)),
            DMA((2, SIDE)),
            DMA((2, SIDE)),
        ],
        compiler_params=params(2),
        name="gradient",
    )(packs, kv, datt, gw)
    gq, gcq, gk, gv, g_out, y_hist, y_cand, du_hist, du_cand = pl.pallas_call(
        finish_kernel,
        out_shape=(
            shape(TOK, WIDTH),
            shape(CAND, WIDTH),
            shape(TOK, WIDTH),
            shape(TOK, WIDTH),
            shape(WIDTH, MODEL),
            shape(TOK, MODEL),
            shape(CAND, MODEL),
            shape(TOK, WIDTH),
            shape(CAND, WIDTH),
        ),
        in_specs=[VM] * 5,
        out_specs=(HB,) * 9,
        scratch_shapes=[DMA((1 + 6 * HEADS,)), DMA((2, 3)), DMA((2, 3))],
        compiler_params=params(),
        name="finish",
    )(q_in, kv_in, g_all.reshape(WIDTH, MODEL), y, du)
    return (
        y_hist[None], y_cand[None], gq[None], gk[None], gv[None], du_hist[None], gcq[None],
        du_cand[None], g_out,
    )


def solution(mesh):
    rows = P("dp", "ctx", None)
    return jax.shard_map(
        local,
        mesh=mesh,
        in_specs=(rows, rows, rows, rows, rows, rows, P("dp", None), P("dp", "ctx"), P(), rows, rows),
        out_specs=(rows, rows, rows, rows, rows, rows, rows, rows, P()),
        check_vma=False,
    )
```

```python
import functools
import math

import jax
import jax.numpy as jnp
from jax import lax
from jax.experimental import pallas as pl
from jax.experimental.pallas import tpu as pltpu
from jax.sharding import PartitionSpec as P

HEADS = 4
DIM = 128
EPS = 1e-05
ZN = 8
SIDE = 4
BAND = 32
SLAB = 256
PART = 64
TOK = 192
CAND = 64
HALF = TOK // 2
CHALF = CAND // 2
ROWS = HALF + CHALF
META = 16
PACK = ROWS + META
KEYS = 3072
WIDTH = HEADS * DIM
MODEL = 1024
CANDS = ZN * CHALF
SCALE = 1.0 / math.sqrt(DIM)
ORDER = (0, 1, 7, 2, 6, 3, 5, 4)
TILE = 768
GROUP = 4
NTILE = 11
BLOCKS = KEYS // TILE
ROOM = BLOCKS * (NTILE + GROUP)
SHARDS = TILE // TOK
PLAN = (
    ((0, 1, 2, 3), (4, 5, 8, 9, 10)),
    ((2, 3, 4, 5), (6, 7, 8, 9, 10)),
    ((4, 5, 6, 7), (8, 9, 10)),
    ((6, 7, 8, 9, 10),),
)
MESH = pl.DeviceIdType.MESH
bf16 = jnp.bfloat16
f32 = jnp.float32


def coords():
    ctx, dp = lax.axis_index("ctx"), lax.axis_index("dp")
    core = dp % 2
    return ctx // 2, ctx % 2, core, dp - core


def device(base, z, x, core):
    return {"ctx": z * 2 + x, "dp": base + core}


def column(z, x, core, base):
    return [
        device(base, (z + step) % ZN, x, (core + other) % 2)
        for step in range(ZN)
        for other in range(2)
        if step or other
    ]


def spots(x, base):
    return base // 8 * 2 + x, base % 8 // 2


def along(z, core, axis, spot, place):
    wide, high = (place, spot[1]) if axis == 0 else (spot[0], place)
    return {"ctx": z * 2 + wide % 2, "dp": wide // 2 * 8 + high * 2 + core}


def plane(z, x, core, base):
    spot = spots(x, base)
    return [
        along(z, core, axis, spot, (spot[axis] + step) % SIDE)
        for axis in range(2)
        for step in range(1, SIDE)
    ]


def greet(others):
    barrier = pltpu.get_barrier_semaphore()
    for other in others:
        pl.semaphore_signal(barrier, inc=1, device_id=other, device_id_type=MESH)
    pl.semaphore_wait(barrier, len(others))


def landed(ref, sem):
    pltpu.make_async_copy(ref, ref, sem).wait()


def remote(src, dst, send, recv, where):
    return pltpu.make_async_remote_copy(
        src_ref=src,
        dst_ref=dst,
        send_sem=send,
        recv_sem=recv,
        device_id=where,
        device_id_type=MESH,
    )


def half_start(core, z):
    return pl.multiple_of(((core + z) % 2) * HALF, HALF)


def spread_kernel(
    q_hbm, k_hbm, v_hbm, c_hbm, user_hbm, len_hbm, q_out, kv_out,
    q_ref, kv_ref, c_ref, user_ref, len_ref, l_sem, pack, s_q, r_q, s_kv, r_kv, s_x, r_x, s_s, r_s,
):
    z, x, core, base = coords()
    fetches = [
        pltpu.make_async_copy(src, dst, l_sem.at[i])
        for i, (src, dst) in enumerate(
            [
                (src.at[:, h * DIM : (h + 1) * DIM], kv_ref.at[kind, h])
                for h in range(HEADS)
                for kind, src in ((0, k_hbm), (1, v_hbm))
            ]
            + [
                (q_hbm, q_ref),
                (c_hbm, c_ref),
                (user_hbm, user_ref),
                (len_hbm, len_ref),
            ]
        )
    ]
    for fetch in fetches:
        fetch.start()
    greet(column(z, x, core, base) + [device(base, z, 1 - x, core)])
    own = 2 * z + x
    turn = jnp.where(z % 2 > core, 1, 3)
    turns = (0, turn, 4 - turn, 2)
    dests = []
    for j in range(HEADS):
        h = (z // 2 + turns[j]) % HEADS
        dests.append((h, 2 * h + core))
    at_home = dests[0][1] == z

    def kv_source(j, kind):
        return kv_ref.at[kind, dests[j][0]]

    def send_kv(j, kind):
        return remote(
            kv_source(j, kind), kv_out.at[kind, own], s_kv.at[j, kind], r_kv.at[z],
            device(base, dests[j][1], x, kind),
        )

    def send_q(j, kind):
        return remote(
            pack.at[dests[j][0], kind], q_out.at[z], s_q.at[j, kind], r_q.at[z],
            device(base, dests[j][1], x, kind),
        )

    for fetch in fetches[: 2 * HEADS]:
        fetch.wait()
    def start_all(j, send, local_pair):
        for kind in range(2):
            if j:
                send(j, kind).start()
            else:
                here = at_home & (core == kind)

                @pl.when(here)
                def _():
                    pltpu.make_async_copy(*local_pair(kind)).start()

                @pl.when(jnp.logical_not(here))
                def _():
                    send(j, kind).start()

    def sent(j, send):
        for kind in range(2):
            if j:
                send(j, kind).wait_send()
            else:

                @pl.when(jnp.logical_not(at_home & (core == kind)))
                def _():
                    send(j, kind).wait_send()

    def start_kv(j):
        start_all(j, send_kv, lambda kind: (kv_source(0, kind), kv_out.at[kind, own], r_kv.at[z]))

    def start_q(j):
        start_all(j, send_q, lambda kind: (pack.at[dests[0][0], kind], q_out.at[z], r_q.at[z]))

    for j in range(HEADS):
        start_kv(j)
    for fetch in fetches[2 * HEADS :]:
        fetch.wait()
    lane = lax.broadcasted_iota(jnp.int32, (META, DIM), 1)
    row = lax.broadcasted_iota(jnp.int32, (META, DIM), 0)
    lens = jnp.zeros((META, DIM), jnp.int32)
    for i in range(4):
        lens = jnp.where(lane == i, len_ref[0, i], lens)
    lens_f = lens.astype(f32)
    high = jnp.floor(lens_f * (1.0 / 64.0))
    low = lens_f - high * 64.0
    users = jnp.broadcast_to(user_ref[...].astype(f32), (META, CAND)).astype(bf16)
    sel_j = lax.broadcasted_iota(jnp.int32, (CAND, DIM), 0)
    sel_l = lax.broadcasted_iota(jnp.int32, (CAND, DIM), 1)
    spot = CHALF * (z % 4)
    for kind in range(2):
        start = half_start(kind, z)
        pick = (
            (sel_l - spot + CHALF * kind == sel_j) & (sel_l >= spot) & (sel_l < spot + CHALF)
        ).astype(f32)
        placed = jnp.dot(users, pick.astype(bf16), preferred_element_type=f32)
        meta = jnp.where(row == 0, placed, jnp.where(row == 1, high, low)).astype(bf16)
        for h in range(HEADS):
            cols = slice(h * DIM, (h + 1) * DIM)
            pack[h, kind, 0:HALF, :] = q_ref[pl.ds(start, HALF), cols]
            pack[h, kind, HALF:ROWS, :] = c_ref[kind * CHALF : (kind + 1) * CHALF, cols]
            pack[h, kind, ROWS:PACK, :] = meta
    def across(s, zi):
        slot = kv_out.at[core, s]
        return remote(slot, slot, s_x.at[zi], r_x.at[zi], device(base, z, 1 - x, core))

    def beside(s):
        slot = kv_out.at[core, s]
        return remote(slot, slot, s_s.at[s], r_s.at[s], device(base, z, x, 1 - core))

    def pass_on(step):
        zi = (z + ORDER[step]) % ZN
        s = 2 * zi + (1 - x)
        landed(kv_out.at[core, s], r_x.at[zi])
        beside(s).start()

    for step in range(ZN):
        zi = (z + ORDER[step]) % ZN
        s = 2 * zi + x
        landed(kv_out.at[core, s], r_kv.at[zi])
        across(s, zi).start()
        beside(s).start()
        if step == 0:
            sent(0, send_kv)
        if step == 2:
            sent(1, send_kv)
        if step == 4:
            sent(2, send_kv)
            start_q(0)
            start_q(1)
        if step == 6:
            sent(3, send_kv)
            start_q(2)
            start_q(3)
        if step >= 2:
            pass_on(step - 2)
    pass_on(ZN - 2)
    pass_on(ZN - 1)
    for zi in range(ZN):
        landed(q_out.at[zi], r_q.at[zi])
    for s in range(2 * ZN):
        landed(kv_out.at[1 - core, s], r_s.at[s])
    for s in range(2 * ZN):
        beside(s).wait_send()
    for zi in range(ZN):
        across(2 * zi + x, zi).wait_send()
    for j in range(HEADS):
        sent(j, send_q)


def read_meta(q_ref):
    first = sum(q_ref[zi, ROWS:PACK, :].astype(f32) for zi in range(4))[0:1]
    second = sum(q_ref[zi, ROWS:PACK, :].astype(f32) for zi in range(4, 8))[0:1]
    users = jnp.concatenate([first, second], axis=1)
    block = q_ref[0, ROWS:PACK, :].astype(f32)
    lens = block[1:2] * 64.0 + block[2:3]
    lane = lax.broadcasted_iota(jnp.int32, (1, DIM), 1)
    ends = []
    for i in range(3):
        ends.append(jnp.sum(jnp.where(lane <= i, lens, 0.0)).astype(jnp.int32))
    starts = [jnp.sum((users < float(i)).astype(f32)).astype(jnp.int32) for i in range(1, 4)]
    sub = lax.broadcasted_iota(jnp.int32, (8, CANDS), 0).astype(f32)
    hot = (users == sub).astype(f32)
    before = jnp.sum((users < sub).astype(f32), axis=1, keepdims=True)
    rows = lax.broadcasted_iota(jnp.int32, (CANDS, CANDS), 0)
    cols = lax.broadcasted_iota(jnp.int32, (CANDS, CANDS), 1)
    upper = (rows < cols).astype(f32).astype(bf16)
    prior = jnp.dot(hot.astype(bf16), upper, preferred_element_type=f32)
    rank = jnp.sum(hot * (prior + before), axis=0, keepdims=True).astype(jnp.int32)
    perm = (rows == rank).astype(f32).astype(bf16)
    return ends, starts, perm


def first_of(ends, pos):
    low = jnp.where(pos >= ends[0], ends[0], 0)
    low = jnp.where(pos >= ends[1], ends[1], low)
    return jnp.where(pos >= ends[2], ends[2], low)


def cand_range(ends, starts, row):
    low = jnp.where(row >= starts[0], ends[0], 0)
    low = jnp.where(row >= starts[1], ends[1], low)
    low = jnp.where(row >= starts[2], ends[2], low)
    high = jnp.where(row >= starts[0], ends[1], ends[0])
    high = jnp.where(row >= starts[1], ends[2], high)
    high = jnp.where(row >= starts[2], KEYS, high)
    return low, high


def hist_start(zi):
    z, x, core, base = coords()
    return (2 * zi + x) * TOK + ((core + zi) % 2) * HALF


NT = (((1,), (1,)), ((), ()))
TN = (((0,), (0,)), ((), ()))


def work_list(z, x, core, ends, starts, tiles, counts):
    ranges = []
    for zi in range(ZN):
        p0 = hist_start(zi)
        ranges.append((first_of(ends, p0), p0 + HALF))
    for c in range(NTILE - ZN):
        first, last = c * HALF, min((c + 1) * HALF, CANDS) - 1
        ranges.append((cand_range(ends, starts, first)[0], cand_range(ends, starts, last)[1]))
    for block in range(BLOCKS):
        at = block * (NTILE + GROUP)
        used = jnp.int32(0)
        for i, (low, high) in enumerate(ranges):
            hit = (low < (block + 1) * TILE) & (high > block * TILE)
            tiles[at + used] = jnp.int32(i)
            used = used + hit.astype(jnp.int32)
        for i in range(GROUP - 1):
            tiles[at + used + i] = jnp.int32(NTILE)
        counts[block] = used


def set_bounds(ends, starts, low_ref, high_ref):
    lane = lax.broadcasted_iota(jnp.int32, (HALF, DIM), 1)
    row = lax.broadcasted_iota(jnp.int32, (HALF, DIM), 0)
    for zi in range(ZN):
        pos = hist_start(zi) + row
        low_ref[zi] = first_of(ends, pos) - lane
        high_ref[zi] = pos + 1 - lane
    for c in range(NTILE - ZN):
        low, high = cand_range(ends, starts, c * HALF + row)
        low_ref[ZN + c] = low - lane
        high_ref[ZN + c] = jnp.where(c * HALF + row < CANDS, high, 0) - lane
    low_ref[NTILE] = jnp.zeros((HALF, DIM), jnp.int32)
    high_ref[NTILE] = jnp.full((HALF, DIM), -KEYS, jnp.int32)


def set_bounds_t(ends, starts, low_ref, high_ref):
    lane = lax.broadcasted_iota(jnp.int32, (8, HALF), 1)
    for zi in range(ZN):
        pos = hist_start(zi) + lane
        low_ref[zi] = first_of(ends, pos)
        high_ref[zi] = pos + 1
    for c in range(NTILE - ZN):
        low, high = cand_range(ends, starts, c * HALF + lane)
        low_ref[ZN + c] = low
        high_ref[ZN + c] = jnp.where(c * HALF + lane < CANDS, high, 0)
    low_ref[NTILE] = jnp.zeros((8, HALF), jnp.int32)
    high_ref[NTILE] = jnp.full((8, HALF), -KEYS, jnp.int32)


def inside(low, high, start):
    masks = []
    for i in range(TILE // DIM):
        at = start + i * DIM
        masks.append((low <= at) & (high > at))
    return jnp.concatenate(masks, axis=1)


def load_rows(src, perm, dst):
    for zi in range(ZN):
        dst[zi] = src[zi, 0:HALF, :]
    cand = jnp.concatenate([src[zi, HALF:ROWS, :] for zi in range(ZN)], axis=0)
    cand = jnp.dot(perm, cand, preferred_element_type=f32).astype(bf16)
    dst[ZN] = cand[0:HALF]
    dst[ZN + 1] = cand[HALF : 2 * HALF]
    dst[ZN + 2, 0 : CANDS - 2 * HALF, :] = cand[2 * HALF :]
    dst[ZN + 2, CANDS - 2 * HALF :, :] = jnp.zeros((3 * HALF - CANDS, DIM), bf16)
    dst[NTILE] = jnp.zeros((HALF, DIM), bf16)


def store_rows(acc, perm, dst, factor):
    for zi in range(ZN):
        dst[zi, 0:HALF, :] = (acc[zi] * factor).astype(bf16)
    cand = jnp.concatenate([acc[ZN], acc[ZN + 1], acc[ZN + 2, 0 : CANDS - 2 * HALF, :]], axis=0)
    back = lax.dot_general(
        perm, (cand * factor).astype(bf16), TN, preferred_element_type=f32
    ).astype(bf16)
    for zi in range(ZN):
        dst[zi, HALF:ROWS, :] = back[zi * CHALF : (zi + 1) * CHALF]


def for_groups(tiles, counts, block, body):
    at = block * (NTILE + GROUP)
    used = counts[block]
    whole = used // GROUP
    rest = used - whole * GROUP

    def step(i, carry):
        body([tiles[at + i * GROUP + n] for n in range(GROUP)])
        return carry

    lax.fori_loop(0, whole, step, jnp.int32(0))

    @pl.when((rest > 0) & (rest <= GROUP // 2))
    def _():
        body([tiles[at + whole * GROUP + n] for n in range(GROUP // 2)])

    @pl.when(rest > GROUP // 2)
    def _():
        body([tiles[at + whole * GROUP + n] for n in range(GROUP)])


def stacked(ref, picks):
    return jnp.concatenate([ref[i] for i in picks], axis=0)


def forward_kernel(q_ref, kv_ref, a_ref, q_all, acc, low_ref, high_ref, tiles, counts):
    z, x, core, base = coords()
    ends, starts, perm = read_meta(q_ref)
    work_list(z, x, core, ends, starts, tiles, counts)
    set_bounds(ends, starts, low_ref, high_ref)
    load_rows(q_ref, perm, q_all)
    acc[...] = jnp.zeros(acc.shape, f32)
    for block in range(BLOCKS):
        start = block * TILE

        def body(picks):
            keys = kv_ref[0, start : start + TILE, :]
            values = kv_ref[1, start : start + TILE, :]
            q = stacked(q_all, picks)
            t = lax.dot_general(q, keys, NT, preferred_element_type=f32) * (0.5 * SCALE)
            ok = inside(stacked(low_ref, picks), stacked(high_ref, picks), start)
            gate = jnp.where(ok, 1.0 + jnp.tanh(t), 0.0)
            out = jnp.dot((t * gate).astype(bf16), values, preferred_element_type=f32)
            for n, pick in enumerate(picks):
                acc[pick] += out[n * HALF : (n + 1) * HALF]

        for_groups(tiles, counts, block, body)
    store_rows(acc, perm, a_ref, 1.0)


def ordered(src, hist, cand, sems):
    z = coords()[0]
    copies = []
    for kind in range(2):
        start = half_start(kind, z)
        low = kind * PART
        pieces = (
            (src.at[0, pl.ds(low, PART)], hist.at[pl.ds(start, PART)]),
            (src.at[1, pl.ds(low, HALF - PART)], hist.at[pl.ds(start + PART, HALF - PART)]),
            (src.at[1, pl.ds(low + HALF - PART, CHALF)], cand.at[pl.ds(kind * CHALF, CHALF)]),
        )
        for i, (one, two) in enumerate(pieces):
            copies.append(pltpu.make_async_copy(one, two, sems.at[kind, i]))
    return copies


def middle_kernel(
    a_ref, u_ref, cu_ref, g_ref, cg_ref, w_ref, y_out, du_out, gw_out, da_out,
    a_in, da_pack, gated, up, gates, dgs, g_part, g_send, g_in, g_sum, g_side,
    s_a, r_a, s_d, r_d, s_g, r_g, s_p, r_p,
):
    z, x, core, base = coords()
    greet(column(z, x, core, base) + plane(z, x, core, base))
    batch = z % 2
    head = z // 2

    def send_a(part, step):
        zi = (z + step) % ZN
        return remote(
            a_ref.at[zi, pl.ds(part * PART, PART)], a_in.at[part, head, core],
            s_a.at[part, step], r_a.at[part, head, core], device(base, zi, x, batch),
        )

    def start_a(part):
        for step in (4, 3, 5, 2, 6, 1, 7):
            send_a(part, step).start()

        @pl.when(core == batch)
        def _():
            pltpu.make_async_copy(
                a_ref.at[z, pl.ds(part * PART, PART)],
                a_in.at[part, head, core],
                r_a.at[part, head, core],
            ).start()

        @pl.when(core != batch)
        def _():
            send_a(part, 0).start()

    start_a(0)
    for kind in range(2):
        start = half_start(kind, z)
        low, mid, high = kind * PART, kind * PART + HALF - PART, (kind + 1) * PART
        later = pl.multiple_of(start + PART, 32)
        cands = slice(kind * CHALF, (kind + 1) * CHALF)
        for dst, hist, cand in ((up, g_ref, cg_ref), (gates, u_ref, cu_ref)):
            dst[0, low:high, :] = hist[pl.ds(start, PART), :]
            dst[1, low:mid, :] = hist[pl.ds(later, HALF - PART), :]
            dst[1, mid:high, :] = cand[cands, :]
    for part in range(2):
        dgs[part] = lax.dot_general(up[part], w_ref[...], NT, preferred_element_type=f32)
        if part == 0:
            start_a(1)

    def dest(j):
        h = (z // 2 + j) % HEADS
        return h, 2 * h + core

    def send_d(part, j, kind):
        h, z2 = dest(j)
        return remote(
            da_pack.at[part, h, kind], da_out.at[z, pl.ds(part * PART, PART)],
            s_d.at[part, j, kind], r_d.at[part, z], device(base, z2, x, kind),
        )

    at_home = dest(0)[1] == z
    for part in range(2):
        for h in range(HEADS):
            for kind in range(2):
                landed(a_in.at[part, h, kind], r_a.at[part, h, kind])
        att = jnp.concatenate(
            [a_in[part, h].reshape(2 * PART, DIM) for h in range(HEADS)], axis=1
        ).astype(f32)
        mean = jnp.mean(att, axis=1, keepdims=True)
        centered = att - mean
        var = jnp.mean(centered * centered, axis=1, keepdims=True)
        rstd = lax.rsqrt(var + EPS)
        normed = centered * rstd
        gate = gates[part].astype(f32)
        dg = dgs[part]
        dn = dg * gate
        da = rstd * (
            dn
            - jnp.mean(dn, axis=1, keepdims=True)
            - normed * jnp.mean(dn * normed, axis=1, keepdims=True)
        )
        for h in range(HEADS):
            da_pack[part, h] = (
                da[:, h * DIM : (h + 1) * DIM].astype(bf16).reshape(2, PART, DIM)
            )
        for j in (2, 1, 3):
            for kind in range(2):
                send_d(part, j, kind).start()
        for kind in range(2):
            here = at_home & (core == kind)

            @pl.when(here)
            def _():
                pltpu.make_async_copy(
                    da_pack.at[part, dest(0)[0], kind],
                    da_out.at[z, pl.ds(part * PART, PART)],
                    r_d.at[part, z],
                ).start()

            @pl.when(jnp.logical_not(here))
            def _():
                send_d(part, 0, kind).start()

        gated[part] = (normed * gate).astype(bf16)
        if part == 0:
            for half in range(2):
                g_part[half] = lax.dot_general(
                    gated[0, :, half * SLAB : (half + 1) * SLAB], up[0], TN,
                    preferred_element_type=f32,
                )
        dgs[part] = dg * normed

    def weight_half(owner):
        cols = pl.ds(pl.multiple_of(owner * SLAB, SLAB), SLAB)
        total = lax.dot_general(gated[1, :, cols], up[1], TN, preferred_element_type=f32)
        return (g_part[owner] + total) * (1.0 / 256.0)

    g_send[...] = weight_half(1 - core).astype(bf16)
    beside = remote(g_send, g_in, s_g.at[0], r_g.at[0], device(base, z, x, 1 - core))
    beside.start()
    own = weight_half(core)
    landed(g_in, r_g.at[0])
    g_sum[...] = (own + g_in[...].astype(f32)).astype(bf16)
    spot = spots(x, base)

    def piece(axis, place):
        row = pl.multiple_of(((1 - axis) * SIDE + place) * BAND, BAND)
        return g_sum.at[pl.ds(row, BAND)]

    def send_p(axis, step):
        place = (spot[axis] + step) % SIDE
        return remote(
            piece(axis, place), g_side.at[axis, spot[axis]], s_p.at[axis, step],
            r_p.at[axis, spot[axis]], along(z, core, axis, spot, place),
        )

    for axis in range(2):
        for step in (2, 1, 3):
            send_p(axis, step).start()
        pltpu.make_async_copy(
            piece(axis, spot[axis]), g_side.at[axis, spot[axis]], r_p.at[axis, spot[axis]]
        ).start()
    for part in range(2):
        du_out[part] = dgs[part].astype(bf16)
    for part in range(2):
        y_out[part] = jnp.dot(gated[part], w_ref[...], preferred_element_type=f32).astype(bf16)
    for axis in range(2):
        for place in range(SIDE):
            landed(g_side.at[axis, place], r_p.at[axis, place])
        gw_out[axis] = jnp.sum(g_side[axis].astype(f32), axis=0).astype(bf16)

    for part in range(2):
        for zi in range(ZN):
            landed(da_out.at[zi, pl.ds(part * PART, PART)], r_d.at[part, zi])
        for step in range(1, ZN):
            send_a(part, step).wait_send()

        @pl.when(core != batch)
        def _():
            send_a(part, 0).wait_send()

        for j in range(HEADS):
            for kind in range(2):
                if j:
                    send_d(part, j, kind).wait_send()
                else:

                    @pl.when(jnp.logical_not(at_home & (core == kind)))
                    def _():
                        send_d(part, 0, kind).wait_send()

    beside.wait_send()
    for axis in range(2):
        for step in range(1, SIDE):
            send_p(axis, step).wait_send()


def gradient_kernel(
    q_ref, key_ref, da_ref, gw_ref, q_in, kv_in, g_all,
    q_all, da_all, acc, low_ref, high_ref, dk_acc, dv_acc, dq_ref, dkv_ref,
    beside_in, across_in, sums, g_two, g_slab, g_z, g_mine,
    s_q, r_q, s_s, r_s, s_x, r_x, s_kv, r_kv,
    s_two, r_two, s_z, r_z, s_zz, r_zz, s_five, r_five, s_six, r_six, s_b, r_b,
):
    z, x, core, base = coords()
    greet(column(z, x, core, base) + plane(z, x, core, base))
    batch = z % 2
    head = z // 2
    spot = spots(x, base)

    def block(axis, rows, slab):
        return g_all.at[core, 1 - axis, rows, :, slab]

    def slab_of(place):
        return pl.ds(pl.multiple_of(place * SLAB, SLAB), SLAB)

    def two(axis, step):
        other = 1 - axis
        place = (spot[other] + step) % SIDE
        return remote(
            gw_ref.at[axis, :, slab_of(place)], g_two.at[axis, spot[other]],
            s_two.at[axis, step], r_two.at[axis, spot[other]],
            along(z, core, other, spot, place),
        )

    def z_part(zi):
        return (
            zi // 4,
            pl.ds(pl.multiple_of(zi % 2 * 16, 16), 16),
            pl.ds(pl.multiple_of(zi // 2 % 2 * DIM, DIM), DIM),
        )

    def z_place(zi):
        half, rows, lanes = z_part(zi)
        start = jnp.where(half == 0, spot[1], spot[0]) * SLAB + zi // 2 % 2 * DIM
        band = jnp.where(half == 0, spot[0], spot[1])
        return g_all.at[core, 1 - half, band, rows, pl.ds(pl.multiple_of(start, DIM), DIM)]

    def scatter_z(step):
        zi = (z + step) % ZN
        half, rows, lanes = z_part(zi)
        return remote(
            g_slab.at[half, rows, lanes], g_z.at[z], s_z.at[step], r_z.at[z],
            device(base, zi, x, core),
        )

    def gather_z(step):
        zi = (z + step) % ZN
        return remote(
            g_mine, z_place(z), s_zz.at[step], r_zz.at[z], device(base, zi, x, core)
        )

    def five(axis, step):
        other = 1 - axis
        here = block(axis, spot[axis], slab_of(spot[other]))
        return remote(
            here, here, s_five.at[axis, step], r_five.at[axis, spot[other]],
            along(z, core, other, spot, (spot[other] + step) % SIDE),
        )

    def six(axis, step):
        here = g_all.at[core, 1 - axis, spot[axis]]
        return remote(
            here, here, s_six.at[axis, step], r_six.at[axis, spot[axis]],
            along(z, core, axis, spot, (spot[axis] + step) % SIDE),
        )

    def gather_b(axis, place):
        here = g_all.at[core, 1 - axis, place]
        return remote(
            here, here, s_b.at[axis, place], r_b.at[axis, place],
            device(base, z, x, 1 - core),
        )

    def stage(number):
        if number == 0:
            for axis in range(2):
                for step in (2, 1, 3):
                    two(axis, step).start()
                mine = spot[1 - axis]
                pltpu.make_async_copy(
                    gw_ref.at[axis, :, slab_of(mine)], g_two.at[axis, mine],
                    r_two.at[axis, mine],
                ).start()
        if number == 1:
            for axis in range(2):
                for place in range(SIDE):
                    landed(g_two.at[axis, place], r_two.at[axis, place])
                g_slab[axis] = jnp.sum(g_two[axis].astype(f32), axis=0).astype(bf16)
            for step in (4, 3, 5, 2, 6, 1, 7):
                scatter_z(step).start()
            half, rows, lanes = z_part(z)
            pltpu.make_async_copy(g_slab.at[half, rows, lanes], g_z.at[z], r_z.at[z]).start()
        if number == 2:
            for zi in range(ZN):
                landed(g_z.at[zi], r_z.at[zi])
            g_mine[...] = jnp.sum(g_z[...].astype(f32), axis=0).astype(bf16)
            for step in (4, 3, 5, 2, 6, 1, 7):
                gather_z(step).start()
            pltpu.make_async_copy(g_mine, z_place(z), r_zz.at[z]).start()
        if number == 3:
            for zi in range(ZN):
                landed(z_place(zi), r_zz.at[zi])
            for axis in range(2):
                for step in (2, 1, 3):
                    five(axis, step).start()
        if number == 4:
            for axis in range(2):
                other = 1 - axis
                for step in range(1, SIDE):
                    place = (spot[other] + step) % SIDE
                    landed(block(axis, spot[axis], slab_of(place)), r_five.at[axis, place])
                for step in (2, 1, 3):
                    six(axis, step).start()
                gather_b(axis, spot[axis]).start()
        if number == 5:
            for axis in range(2):
                for step in (1, 3, 2):
                    place = (spot[axis] + step) % SIDE
                    landed(g_all.at[core, 1 - axis, place], r_six.at[axis, place])
                    gather_b(axis, place).start()

    def beside(zi, side):
        s = 2 * zi + side
        return remote(
            dkv_ref.at[1 - core, s], beside_in.at[s], s_s.at[s], r_s.at[s],
            device(base, z, x, 1 - core),
        )

    def across(zi):
        return remote(
            sums.at[2 * zi + 1 - x], across_in.at[zi], s_x.at[zi], r_x.at[zi],
            device(base, z, 1 - x, core),
        )

    def q_parts(zi):
        return dq_ref.at[zi], q_in.at[head, core], s_q.at[zi], r_q.at[head, core]

    def kv_parts(zi):
        return sums.at[2 * zi + x], kv_in.at[head, core], s_kv.at[zi], r_kv.at[head, core]

    def home(zi, parts):
        src, dst, send, recv = parts(zi)
        here = (z == zi) & (core == batch)

        @pl.when(here)
        def _():
            pltpu.make_async_copy(src, dst, recv).start()

        @pl.when(jnp.logical_not(here))
        def _():
            remote(src, dst, send, recv, device(base, zi, x, batch)).start()

    stage(0)
    ends, starts, perm = read_meta(q_ref)
    set_bounds_t(ends, starts, low_ref, high_ref)
    load_rows(q_ref, perm, q_all)
    load_rows(da_ref, perm, da_all)
    acc[...] = jnp.zeros(acc.shape, f32)

    def products(block, picks, first):
        keys = key_ref[0, block * TILE : (block + 1) * TILE, :]
        values = key_ref[1, block * TILE : (block + 1) * TILE, :]
        q = stacked(q_all, picks)
        da = stacked(da_all, picks)
        t = lax.dot_general(keys, q, NT, preferred_element_type=f32) * (0.5 * SCALE)
        dp = lax.dot_general(values, da, NT, preferred_element_type=f32)
        low = jnp.concatenate([low_ref[i] for i in picks], axis=1)[0:1] - block * TILE
        high = jnp.concatenate([high_ref[i] for i in picks], axis=1)[0:1] - block * TILE
        pos = lax.broadcasted_iota(jnp.int32, t.shape, 0)
        gate = jnp.where((pos >= low) & (pos < high), 1.0 + jnp.tanh(t), 0.0)
        p = t * gate
        ds = (dp * (gate * ((1.0 + t + t) - p))).astype(bf16)
        dk = jnp.dot(ds, q, preferred_element_type=f32)
        dv = jnp.dot(p.astype(bf16), da, preferred_element_type=f32)
        if first:
            dk_acc[...] = dk
            dv_acc[...] = dv
        else:
            dk_acc[...] += dk
            dv_acc[...] += dv
        out = lax.dot_general(ds, keys, TN, preferred_element_type=f32)
        for n, pick in enumerate(picks):
            acc[pick] += out[n * HALF : (n + 1) * HALF]

    def key_block(block):
        for n, picks in enumerate(PLAN[block]):
            products(block, picks, n == 0)
        low = block * SHARDS
        dk = (dk_acc[...] * (0.5 * SCALE)).astype(bf16)
        dkv_ref[0, low : low + SHARDS] = dk.reshape(SHARDS, TOK, DIM)
        dkv_ref[1, low : low + SHARDS] = dv_acc[...].astype(bf16).reshape(SHARDS, TOK, DIM)
        for zi in levels(block):
            beside(zi, 1 - x).start()
            beside(zi, x).start()

    def levels(block):
        return range(block * SHARDS // 2, (block + 1) * SHARDS // 2)

    def add_beside(zi, side):
        s = 2 * zi + side
        landed(beside_in.at[s], r_s.at[s])
        return dkv_ref[core, s].astype(f32) + beside_in[s].astype(f32)

    def cross(block):
        for zi in levels(block):
            sums[2 * zi + 1 - x] = add_beside(zi, 1 - x).astype(bf16)
            across(zi).start()

    def finish(block):
        for zi in levels(block):
            total = add_beside(zi, x)
            landed(across_in.at[zi], r_x.at[zi])
            sums[2 * zi + x] = (total + across_in[zi].astype(f32)).astype(bf16)
            home(zi, kv_parts)

    key_block(0)
    stage(1)
    key_block(1)
    cross(0)
    stage(2)
    key_block(2)
    cross(1)
    finish(0)
    stage(3)
    key_block(3)
    cross(2)
    finish(1)
    cross(3)
    store_rows(acc, perm, dq_ref, 0.5 * SCALE)
    for zi in range(ZN):
        home(zi, q_parts)
    stage(4)
    finish(2)
    finish(3)
    stage(5)
    for kind in range(2):
        for h in range(HEADS):
            landed(q_in.at[h, kind], r_q.at[h, kind])
            landed(kv_in.at[h, kind], r_kv.at[h, kind])
    for axis in range(2):
        for place in range(SIDE):
            landed(g_all.at[1 - core, 1 - axis, place], r_b.at[axis, place])

    for step in range(1, ZN):
        scatter_z(step).wait_send()
        gather_z(step).wait_send()
    for axis in range(2):
        for step in range(1, SIDE):
            two(axis, step).wait_send()
            five(axis, step).wait_send()
            six(axis, step).wait_send()
        for place in range(SIDE):
            gather_b(axis, place).wait_send()
    for zi in range(ZN):
        beside(zi, x).wait_send()
        beside(zi, 1 - x).wait_send()
        across(zi).wait_send()

        @pl.when(jnp.logical_not((z == zi) & (core == batch)))
        def _():
            for parts in (q_parts, kv_parts):
                src, dst, send, recv = parts(zi)
                remote(src, dst, send, recv, device(base, zi, x, batch)).wait_send()


def finish_kernel(
    q_in, kv_in, g_all, y_ref, du_ref, q_out, c_out, k_out, v_out, g_out,
    y_out, cy_out, du_out, cdu_out, sems, y_sem, du_sem,
):
    z = coords()[0]
    copies = [(g_all, g_out)]
    for h in range(HEADS):
        cols = slice(h * DIM, (h + 1) * DIM)
        copies.append((kv_in.at[h, 0], k_out.at[:, cols]))
        copies.append((kv_in.at[h, 1], v_out.at[:, cols]))
        for kind in range(2):
            start = half_start(kind, z)
            copies.append((q_in.at[h, kind, 0:HALF], q_out.at[pl.ds(start, HALF), cols]))
            copies.append(
                (
                    q_in.at[h, kind, HALF:ROWS],
                    c_out.at[kind * CHALF : (kind + 1) * CHALF, cols],
                )
            )
    started = [
        pltpu.make_async_copy(src, dst, sems.at[i]) for i, (src, dst) in enumerate(copies)
    ]
    started += ordered(y_ref, y_out, cy_out, y_sem) + ordered(du_ref, du_out, cdu_out, du_sem)
    for copy in started:
        copy.start()
    for copy in started:
        copy.wait()


VM = pl.BlockSpec(memory_space=pltpu.VMEM)
HB = pl.BlockSpec(memory_space=pltpu.HBM)
DMA = pltpu.SemaphoreType.DMA


def shape(*dims, dtype=bf16):
    return jax.ShapeDtypeStruct(dims, dtype)


def params(collective=None, mib=40):
    if collective is None:
        return pltpu.CompilerParams(vmem_limit_bytes=mib << 20)
    return pltpu.CompilerParams(
        vmem_limit_bytes=mib << 20, collective_id=collective, has_side_effects=True
    )


def local(
    q_hist, k_hist, v_hist, u_hist, cand_q, cand_u, lengths, cand_user, w_out, grad_hist, grad_cand
):
    packs, kv = pl.pallas_call(
        spread_kernel,
        out_shape=(shape(ZN, PACK, DIM), shape(2, 2 * ZN, TOK, DIM)),
        in_specs=[HB] * 6,
        out_specs=(VM, VM),
        scratch_shapes=[
            pltpu.VMEM((TOK, WIDTH), bf16),
            pltpu.VMEM((2, HEADS, TOK, DIM), bf16),
            pltpu.VMEM((CAND, WIDTH), bf16),
            pltpu.VMEM((1, CAND), jnp.int32),
            pltpu.SMEM((1, 4), jnp.int32),
            DMA((2 * HEADS + 4,)),
            pltpu.VMEM((HEADS, 2, PACK, DIM), bf16),
            DMA((HEADS, 2)),
            DMA((ZN,)),
            DMA((HEADS, 2)),
            DMA((ZN,)),
            DMA((ZN,)),
            DMA((ZN,)),
            DMA((2 * ZN,)),
            DMA((2 * ZN,)),
        ],
        compiler_params=params(0),
        name="spread",
    )(*[
        pltpu.with_memory_space_constraint(a, pltpu.HBM)
        for a in (q_hist[0], k_hist[0], v_hist[0], cand_q[0], cand_user, lengths)
    ])
    kv = kv.reshape(2, KEYS, DIM)
    att = pl.pallas_call(
        forward_kernel,
        out_shape=shape(ZN, ROWS, DIM),
        in_specs=[VM] * 2,
        out_specs=VM,
        scratch_shapes=[
            pltpu.VMEM((NTILE + 1, HALF, DIM), bf16),
            pltpu.VMEM((NTILE + 1, HALF, DIM), f32),
            pltpu.VMEM((NTILE + 1, HALF, DIM), jnp.int32),
            pltpu.VMEM((NTILE + 1, HALF, DIM), jnp.int32),
            pltpu.SMEM((ROOM,), jnp.int32),
            pltpu.SMEM((BLOCKS,), jnp.int32),
        ],
        compiler_params=params(),
        name="forward",
    )(packs, kv)
    y, du, gw, datt = pl.pallas_call(
        middle_kernel,
        out_shape=(
            shape(2, 2 * PART, MODEL),
            shape(2, 2 * PART, WIDTH),
            shape(2, BAND, MODEL),
            shape(ZN, ROWS, DIM),
        ),
        in_specs=[VM] * 6,
        out_specs=(VM,) * 4,
        scratch_shapes=[
            pltpu.VMEM((2, HEADS, 2, PART, DIM), bf16),
            pltpu.VMEM((2, HEADS, 2, PART, DIM), bf16),
            pltpu.VMEM((2, 2 * PART, WIDTH), bf16),
            pltpu.VMEM((2, 2 * PART, MODEL), bf16),
            pltpu.VMEM((2, 2 * PART, WIDTH), bf16),
            pltpu.VMEM((2, 2 * PART, WIDTH), f32),
            pltpu.VMEM((2, SLAB, MODEL), f32),
            pltpu.VMEM((SLAB, MODEL), bf16),
            pltpu.VMEM((SLAB, MODEL), bf16),
            pltpu.VMEM((SLAB, MODEL), bf16),
            pltpu.VMEM((2, SIDE, BAND, MODEL), bf16),
            DMA((2, ZN)),
            DMA((2, HEADS, 2)),
            DMA((2, HEADS, 2)),
            DMA((2, ZN)),
            DMA((1,)),
            DMA((1,)),
            DMA((2, SIDE)),
            DMA((2, SIDE)),
        ],
        compiler_params=params(1),
        name="middle",
    )(att, u_hist[0], cand_u[0], grad_hist[0], grad_cand[0], w_out)
    q_in, kv_in, g_all = pl.pallas_call(
        gradient_kernel,
        out_shape=(
            shape(HEADS, 2, ROWS, DIM),
            shape(HEADS, 2, TOK, DIM),
            shape(2, 2, SIDE, BAND, MODEL),
        ),
        in_specs=[VM] * 4,
        out_specs=(VM,) * 3,
        scratch_shapes=[
            pltpu.VMEM((NTILE + 1, HALF, DIM), bf16),
            pltpu.VMEM((NTILE + 1, HALF, DIM), bf16),
            pltpu.VMEM((NTILE + 1, HALF, DIM), f32),
            pltpu.VMEM((NTILE + 1, 8, HALF), jnp.int32),
            pltpu.VMEM((NTILE + 1, 8, HALF), jnp.int32),
            pltpu.VMEM((TILE, DIM), f32),
            pltpu.VMEM((TILE, DIM), f32),
            pltpu.VMEM((ZN, ROWS, DIM), bf16),
            pltpu.VMEM((2, 2 * ZN, TOK, DIM), bf16),
            pltpu.VMEM((2 * ZN, TOK, DIM), bf16),
            pltpu.VMEM((ZN, TOK, DIM), bf16),
            pltpu.VMEM((2 * ZN, TOK, DIM), bf16),
            pltpu.VMEM((2, SIDE, BAND, SLAB), bf16),
            pltpu.VMEM((2, BAND, SLAB), bf16),
            pltpu.VMEM((ZN, 16, DIM), bf16),
            pltpu.VMEM((16, DIM), bf16),
            DMA((ZN,)),
            DMA((HEADS, 2)),
            DMA((2 * ZN,)),
            DMA((2 * ZN,)),
            DMA((ZN,)),
            DMA((ZN,)),
            DMA((ZN,)),
            DMA((HEADS, 2)),
            DMA((2, SIDE)),
            DMA((2, SIDE)),
            DMA((ZN,)),
            DMA((ZN,)),
            DMA((ZN,)),
            DMA((ZN,)),
            DMA((2, SIDE)),
            DMA((2, SIDE)),
            DMA((2, SIDE)),
            DMA((2, SIDE)),
            DMA((2, SIDE)),
            DMA((2, SIDE)),
        ],
        compiler_params=params(2),
        name="gradient",
    )(packs, kv, datt, gw)
    gq, gcq, gk, gv, g_out, y_hist, y_cand, du_hist, du_cand = pl.pallas_call(
        finish_kernel,
        out_shape=(
            shape(TOK, WIDTH),
            shape(CAND, WIDTH),
            shape(TOK, WIDTH),
            shape(TOK, WIDTH),
            shape(WIDTH, MODEL),
            shape(TOK, MODEL),
            shape(CAND, MODEL),
            shape(TOK, WIDTH),
            shape(CAND, WIDTH),
        ),
        in_specs=[VM] * 5,
        out_specs=(HB,) * 9,
        scratch_shapes=[DMA((1 + 6 * HEADS,)), DMA((2, 3)), DMA((2, 3))],
        compiler_params=params(),
        name="finish",
    )(q_in, kv_in, g_all.reshape(WIDTH, MODEL), y, du)
    return (
        y_hist[None], y_cand[None], gq[None], gk[None], gv[None], du_hist[None], gcq[None],
        du_cand[None], g_out,
    )


def solution(mesh):
    rows = P("dp", "ctx", None)
    return jax.shard_map(
        local,
        mesh=mesh,
        in_specs=(rows, rows, rows, rows, rows, rows, P("dp", None), P("dp", "ctx"), P(), rows, rows),
        out_specs=(rows, rows, rows, rows, rows, rows, rows, rows, P()),
        check_vma=False,
    )
```
